128 devices in a mesh: section: 2 (over x_lo), shard: 16 (over z, x_hi, core), replica: 4 (over y).
Axes of the slice: x: 4 (x_hi: 2, x_lo: 2; x = x_hi * 2 + x_lo), y: 4, z: 4, core: 2. Of those that a mesh axis runs over, the one named last changes fastest.
Arguments:
- inputs: bfloat16 [2, 4, 1024, 1024], P(None, 'replica', 'shard'), may hold values from -6 to 6
- segments: int32 [2, 4, 1024], P(None, 'replica', 'shard'), may hold values from 0 to 2, as said below
- cotangent: bfloat16 [2, 4, 1024, 1024], P(None, 'replica', 'shard'), may hold values from -6 to 6
- attend_weight: bfloat16 [2, 1024, 3072], P('section', 'shard'), may hold values from -0.1875 to 0.1875
- output_weight: bfloat16 [2, 1024, 1024], P('section', 'shard'), may hold values from -2 to 2
- expand_weight: bfloat16 [2, 1024, 4096], P('section', 'shard'), may hold values from -0.1875 to 0.1875
- contract_weight: bfloat16 [2, 4096, 1024], P('section', 'shard'), may hold values from -0.09375 to 0.09375
- biases: bfloat16 [2, 6, 1024], P('section', None, 'shard'), may hold values from -1.5 to 1.5
- hidden_bias: bfloat16 [2, 4096], P('section', 'shard'), may hold values from -1.5 to 1.5
- gains: bfloat16 [2, 2, 1024], P('section', None, 'shard'), may hold values from 0.5 to 1.5
Outputs:
- layer_output: bfloat16 [2, 2, 4, 1024, 1024], P('section', None, 'replica', 'shard')
- input_grad: float32 [2, 2, 4, 1024, 1024], P('section', None, 'replica', 'shard')
- attend_grad: float32 [2, 1024, 3072], P('section', 'shard')
- output_grad: float32 [2, 1024, 1024], P('section', 'shard')
- expand_grad: float32 [2, 1024, 4096], P('section', 'shard')
- contract_grad: float32 [2, 4096, 1024], P('section', 'shard')
- biases_grad: float32 [2, 6, 1024], P('section', None, 'shard')
- hidden_grad: float32 [2, 4096], P('section', 'shard')
- gains_grad: float32 [2, 2, 1024], P('section', None, 'shard')
The draws below stay inside these ranges and needn't reach their ends.
Inputs may be any that keep to these rules, and one draw needn't show every extreme that they name: `segments`: along each sequence the numbers start at 0 and rise by one where a document starts; a sequence holds one to three documents, one of them longer than half the sequence, every other one of 204 tokens or more. A token attends to the tokens of its own sequence that carry the same number.
All inputs are finite; a program needn't handle non-finite values.
Results may differ from the reference program's by a relative error of at most 0.019.
Values may be sent and summed in bfloat16 or wider, within the bound.
No kernel may reach another device: no remote copies, remote signals or barrier semaphores. Data moves between devices by JAX's collectives and lax.ppermute only.
A program may use at most 192 MiB of HBM per device.

```python
import math
import jax
import jax.numpy as jnp
from jax import lax

D = 1024
FF = 4096
HEADS = 16
HEAD_DIM = 64
SEQ = 1024
MICRO = 2
SEQS_ALL = 4
N_SECTION = 2


def draw_segments(key, part):
    key = jax.random.fold_in(key, 7)
    lead_key, trail_key, lead_on_key, trail_on_key = jax.random.split(key, 4)
    shortest = SEQ // 5
    room = (SEQ - SEQ // 2 - SEQ // 16) // 2
    shape = (MICRO, SEQS_ALL, 1)
    lead_length = jax.random.randint(lead_key, shape, shortest, room + 1)
    trail_length = jax.random.randint(trail_key, shape, shortest, room + 1)
    first_flag = (jnp.arange(MICRO * SEQS_ALL).reshape(shape) == 0).astype(jnp.int32)
    lead_on = jnp.maximum(jax.random.randint(lead_on_key, shape, 0, 2), first_flag)
    trail_on = jnp.maximum(jax.random.randint(trail_on_key, shape, 0, 2), first_flag)
    trail_cut = SEQ - trail_length * trail_on
    tokens = jnp.arange(SEQ).astype(jnp.int32)[None, None, :]
    lead_part = (tokens >= lead_length).astype(jnp.int32) * lead_on
    trail_part = (tokens >= trail_cut).astype(jnp.int32)
    return (lead_part + trail_part).astype(jnp.int32)


def block_levels(own_key, shape, cuts, low, top_value):
    level = 1.0
    for axis_at, blocks in cuts:
        heights = jax.random.uniform(jax.random.fold_in(jax.random.fold_in(own_key, 6), axis_at), (blocks,), jnp.float32, low / len(cuts), top_value / len(cuts))
        level = level * jnp.repeat(jnp.exp(heights), shape[axis_at] // blocks).reshape((-1,) + (1,) * (len(shape) - 1 - axis_at))
    return level


def gaussian(key, extent, deviation, reach, cuts=(), kind=jnp.bfloat16):
    level = block_levels(key, extent, cuts, -0.22, 0.18) if cuts else 1.0
    array = jax.random.normal(key, extent, jnp.float32) * deviation * level
    return jnp.minimum(jnp.maximum(array, -reach), reach).astype(kind)


def setup_inputs(seed: int = 0) -> dict:
    keys = jax.random.split(jax.random.key(seed), 11)
    inputs = gaussian(keys[0], (MICRO, SEQS_ALL, SEQ, D), 1.0, 6.0, ((1, 4), (2, 16)))
    segments = draw_segments(jax.random.fold_in(keys[10], 71), 0)
    cotangent = gaussian(keys[2], (MICRO, SEQS_ALL, SEQ, D), 1.0, 6.0, ((1, 4), (2, 16)))
    attend_weight = gaussian(keys[3], (N_SECTION, D, 3 * D), D ** -0.5, 0.1875, ((0, 2), (1, 16)))
    output_weight = gaussian(keys[4], (N_SECTION, D, D), (max(1, D // 128)) ** -0.5, 2.0, ((0, 2), (1, 16)))
    expand_weight = gaussian(keys[5], (N_SECTION, D, FF), D ** -0.5, 0.1875, ((0, 2), (1, 16)))
    contract_weight = gaussian(keys[6], (N_SECTION, FF, D), FF ** -0.5, 0.09375, ((0, 2), (1, 16)))
    biases = gaussian(keys[7], (N_SECTION, 6, D), 0.3, 1.5, ((0, 2), (2, 16)))
    hidden_bias = gaussian(keys[8], (N_SECTION, FF), 0.3, 1.5, ((0, 2), (1, 16)))
    gains = jnp.clip(1.0 + 0.1 * jax.random.normal(keys[9], (N_SECTION, 2, D), jnp.float32), 0.5, 1.5).astype(jnp.bfloat16)
    return {"inputs": inputs, "segments": segments, "cotangent": cotangent, "attend_weight": attend_weight, "output_weight": output_weight, "expand_weight": expand_weight, "contract_weight": contract_weight, "biases": biases, "hidden_bias": hidden_bias, "gains": gains}


NEGATIVE = -1e+30
EPSILON = 1e-05
HIGHEST = lax.Precision.HIGHEST

@jax.custom_vjp
def low(v):
    return lax.optimization_barrier(v.astype(jnp.bfloat16)).astype(jnp.float32)

@jax.custom_vjp
def low_back(v):
    return v

def low_keep(v):
    return (low(v), None)

def low_pass(kept, grad):
    return (grad,)

def back_keep(v):
    return (v, None)

def back_low(kept, grad):
    return (low(grad),)
low.defvjp(low_keep, low_pass)
low_back.defvjp(back_keep, back_low)

def layer_norm(value, gain, shift):
    mean_value = lax.optimization_barrier(jnp.mean(value, -1, keepdims=True))
    centred = value - mean_value
    spread = lax.optimization_barrier(jnp.mean(centred * centred, -1, keepdims=True))
    return centred * lax.rsqrt(spread + EPSILON) * gain + shift

def gelu_exact(value):
    return jax.nn.gelu(value, approximate=False)

def product(left, right):
    return jnp.dot(left, right, precision=HIGHEST, preferred_element_type=jnp.float32)

def sequence_layer(hidden, seg_row, attend_weight, output_weight, expand_weight, contract_weight, biases, hidden_bias, gains):
    length, features = hidden.shape
    packed_bias = jnp.concatenate([biases[0], jnp.zeros_like(biases[0]), biases[1]])
    packed = low(low_back(product(hidden, attend_weight) + packed_bias))
    queries = packed[:, :features].reshape(length, HEADS, HEAD_DIM)
    key_heads = packed[:, features:2 * features].reshape(length, HEADS, HEAD_DIM)
    value_heads = packed[:, 2 * features:].reshape(length, HEADS, HEAD_DIM)
    scaled = jnp.einsum('qhd,khd->hqk', queries, key_heads, precision=HIGHEST) * (1.0 / math.sqrt(HEAD_DIM))
    scaled = low_back(scaled)
    matching = seg_row[:, None] == seg_row[None, :]
    scores = jnp.where(matching[None], scaled, NEGATIVE)
    highest = lax.optimization_barrier(jnp.max(scores, -1, keepdims=True))
    exponent = jnp.exp(scores - highest)
    soft_weights = low(exponent / lax.optimization_barrier(jnp.sum(exponent, -1, keepdims=True)))
    context = jnp.einsum('hqk,khd->qhd', soft_weights, value_heads, precision=HIGHEST).reshape(length, features)
    context = low(low_back(context))
    attention = low_back(product(context, output_weight) + biases[2])
    first = layer_norm(hidden + attention, gains[0], biases[3])
    inner = low_back(product(low(first), expand_weight) + hidden_bias)
    activation = low(gelu_exact(inner))
    mlp_out = low_back(product(activation, contract_weight) + biases[4])
    return layer_norm(first + mlp_out, gains[1], biases[5])

def run_layer(hidden, seg_rows, weights):
    checked_layer = jax.checkpoint(sequence_layer)

    def scan_step(unused, element):
        return (unused, checked_layer(element[0], element[1], *weights))
    unused, outputs = lax.scan(scan_step, None, (hidden, seg_rows))
    return outputs

def reference(inputs, segments, cotangent, attend_weight, output_weight, expand_weight, contract_weight, biases, hidden_bias, gains):
    total_seqs = MICRO * SEQS_ALL
    flat_inputs = inputs.astype(jnp.float32).reshape(total_seqs, SEQ, D)
    seg_rows = segments.reshape(total_seqs, SEQ)
    weights = (attend_weight.astype(jnp.float32), output_weight.astype(jnp.float32), expand_weight.astype(jnp.float32), contract_weight.astype(jnp.float32), biases.astype(jnp.float32), hidden_bias.astype(jnp.float32), gains.astype(jnp.float32))

    def forward(probe, weight_set):
        outputs = []
        hidden = flat_inputs + probe[0]
        for layer_index in range(N_SECTION):
            if layer_index > 0:
                hidden = low(low_back(hidden)) + probe[layer_index]
            hidden = run_layer(hidden, seg_rows, tuple((weight[layer_index] for weight in weight_set)))
            outputs.append(hidden)
        return jnp.stack(outputs)
    probe = jnp.zeros((N_SECTION, total_seqs, SEQ, D), jnp.float32)
    outputs, pullback = jax.vjp(forward, probe, weights)
    seed_grad = jnp.zeros_like(outputs).at[N_SECTION - 1].set(cotangent.astype(jnp.float32).reshape(total_seqs, SEQ, D))
    grad_probe, grad_weights = pullback(seed_grad)
    section_shape = (N_SECTION, MICRO, SEQS_ALL, SEQ, D)
    return (outputs.astype(jnp.bfloat16).reshape(section_shape), grad_probe.reshape(section_shape), grad_weights[0], grad_weights[1], grad_weights[2], grad_weights[3], grad_weights[4], grad_weights[5], grad_weights[6])
```

```python
import math

import jax
import jax.numpy as jnp
from jax import lax
from jax.sharding import PartitionSpec as P

HEADS = 16
HEAD_DIM = 64
NEGATIVE = -1e30
EPSILON = 1e-05
SCALE = 1.0 / math.sqrt(HEAD_DIM)
LOW = jnp.bfloat16
ALL = ("section", "shard")
REST = ("shard", "replica")


def layer_norm(value, gain, shift):
    mean_value = jnp.mean(value, -1, keepdims=True)
    centred = value - mean_value
    spread = jnp.mean(centred * centred, -1, keepdims=True)
    return centred * lax.rsqrt(spread + EPSILON) * gain + shift


def gelu_exact(value):
    return jax.nn.gelu(value, approximate=False)


def matmul(left, right):
    return jnp.dot(left, right, preferred_element_type=jnp.float32)


def times_transposed(left, right):
    return lax.dot_general(
        left, right, (((1,), (1,)), ((), ())), preferred_element_type=jnp.float32
    )


def transposed_times(left, right):
    return lax.dot_general(
        left, right, (((0,), (0,)), ((), ())), preferred_element_type=jnp.float32
    )


def exchange(value, axes):
    return lax.all_to_all(value, axes, 0, 0, tiled=True)


def swap_cores(value):
    return lax.ppermute(value, "shard", [(i, i ^ 1) for i in range(16)])


def whole_sequence(tokens):
    core = lax.axis_index("shard") % 2
    micros, rows, features = tokens.shape
    half = rows // 2
    sends = jnp.broadcast_to(
        tokens.reshape(micros, 1, 2, half, features), (micros, 4, 2, half, features)
    ).reshape(16, half, features)
    mine = exchange(sends, "shard")
    other = swap_cores(mine)
    lower = jnp.where(core == 0, mine, other)
    upper = jnp.where(core == 0, other, mine)
    return jnp.stack([lower, upper], 1).reshape(16 * rows, features)


def to_tokens(value, parts):
    width = parts * HEAD_DIM
    sends = jnp.broadcast_to(value.reshape(1, 16, 64, width), (2, 16, 64, width))
    got = exchange(sends.reshape(32, 64, width), ALL)
    got = got.reshape(2, 2, 8, 64, parts, HEAD_DIM).transpose(1, 3, 4, 0, 2, 5)
    return got.reshape(128, parts * 1024)


def to_head(value, layer):
    sends = value.reshape(2, 64, 2, 8, HEAD_DIM).transpose(2, 0, 3, 1, 4).reshape(32, 64, HEAD_DIM)
    got = exchange(sends, ALL)
    return got[16 * layer : 16 * layer + 16].reshape(1024, HEAD_DIM)


def masked_scores(queries, keys, seg):
    scores = times_transposed(queries, keys) * SCALE
    return jnp.where(seg[:, None] == seg[None, :], scores, NEGATIVE)


def attend(packed, seg):
    queries, keys, values = jnp.split(packed, 3, 1)
    scores = masked_scores(queries, keys, seg)
    highest = jnp.max(scores, -1, keepdims=True)
    exponent = jnp.exp(scores - highest)
    totals = jnp.sum(exponent, -1, keepdims=True)
    context = matmul((exponent / totals).astype(LOW), values).astype(LOW)
    return context, highest + jnp.log(totals)


def attend_back(packed, log_totals, seg, grad_context):
    queries, keys, values = jnp.split(packed, 3, 1)
    soft = jnp.exp(masked_scores(queries, keys, seg) - log_totals)
    grad_soft = times_transposed(grad_context, values)
    row_total = jnp.sum(soft * grad_soft, -1, keepdims=True)
    grad_scores = (soft * (grad_soft - row_total)).astype(LOW)
    return jnp.concatenate(
        [
            matmul(grad_scores, keys) * SCALE,
            transposed_times(grad_scores, queries) * SCALE,
            transposed_times(soft.astype(LOW), grad_context),
        ],
        1,
    ).astype(LOW)


def block_forward(tokens, context, weights, biases, hidden_bias, gains):
    output_weight, expand_weight, contract_weight = weights
    residual = tokens.astype(jnp.float32) + (matmul(context, output_weight) + biases[2])
    first = layer_norm(residual, gains[0], biases[3])
    first_low = first.astype(LOW)
    inner = jnp.concatenate([matmul(first_low, part) for part in expand_weight], 1) + hidden_bias
    activation = gelu_exact(inner).astype(LOW)
    second = first + (matmul(activation, contract_weight) + biases[4])
    output = layer_norm(second, gains[1], biases[5]).astype(LOW)
    return output, (residual, first_low, inner, second)


def block_back(grad, saved, weights, biases, gains):
    output_weight, expand_weight, contract_weight = weights
    residual, first_low, inner, second = saved
    unused, norm_back_two = jax.vjp(layer_norm, second, gains[1], biases[5])
    grad_second, grad_gain_two, grad_shift_two = norm_back_two(grad)
    grad_mlp = grad_second.astype(LOW)
    unused, gelu_back = jax.vjp(gelu_exact, inner)
    grad_inner = gelu_back(times_transposed(grad_mlp, contract_weight))[0].astype(LOW)
    grad_first = grad_second
    for part, piece in zip(expand_weight, jnp.split(grad_inner, 4, 1)):
        grad_first = grad_first + times_transposed(piece, part)
    unused, norm_back_one = jax.vjp(layer_norm, residual, gains[0], biases[3])
    grad_residual, grad_gain_one, grad_shift_one = norm_back_one(grad_first)
    grad_attn = grad_residual.astype(LOW)
    grad_context = times_transposed(grad_attn, output_weight).astype(LOW)
    attn_sum = jnp.sum(grad_attn.astype(jnp.float32), 0)
    sums = jnp.stack([grad_gain_one, grad_gain_two, attn_sum, grad_shift_one, grad_shift_two])
    return grad_mlp, grad_residual, grad_attn, grad_context, sums


def on_device(
    inputs,
    segments,
    cotangent,
    attend_weight,
    output_weight,
    expand_weight,
    contract_weight,
    biases,
    hidden_bias,
    gains,
):
    section = lax.axis_index("section")
    shard = lax.axis_index("shard")
    on_first = section == 0
    micro = shard // 8
    head = section * 8 + shard % 8
    inputs = inputs[:, 0]

    with jax.named_scope("gather_block_weights"):
        rows = jnp.concatenate(
            [output_weight[0]] + jnp.split(expand_weight[0], 4, 1) + [contract_weight[0]], 0
        )
        gathered = lax.all_gather(rows, "shard", axis=0, tiled=False)
        weights = (
            gathered[:, :64].reshape(1024, 1024),
            [gathered[:, 64 + 64 * q : 128 + 64 * q].reshape(1024, 1024) for q in range(4)],
            gathered[:, 320:576].reshape(4096, 1024),
        )

    with jax.named_scope("head_weights"):
        by_head = attend_weight[0].reshape(64, 3, HEADS, HEAD_DIM).transpose(2, 0, 1, 3)
        small = jnp.concatenate(
            [
                biases.reshape(384),
                gains.reshape(128),
                hidden_bias.reshape(256),
                segments.reshape(128).astype(LOW),
                jnp.zeros((16 * 192 - 896,), LOW),
            ]
        ).reshape(1, 16, 192)
        block = jnp.concatenate(
            [by_head.reshape(HEADS, 64, 192), jnp.broadcast_to(small, (HEADS, 16, 192))], 1
        )
        block = jnp.broadcast_to(block.reshape(2, 1, 8, 80, 192), (2, 2, 8, 80, 192))
        got = exchange(block.reshape(32, 80, 192), ALL).reshape(2, 16, 80, 192)
        head_weight = got[:, :, :64].reshape(2, 1024, 192)
        small = got[:, :, 64:69].reshape(2, 16, 960)
        all_biases = small[:, :, :384].reshape(2, 16, 6, 64).transpose(0, 2, 1, 3)
        all_biases = all_biases.reshape(2, 6, 1024).astype(jnp.float32)
        all_gains = small[:, :, 384:512].reshape(2, 16, 2, 64).transpose(0, 2, 1, 3)
        all_gains = all_gains.reshape(2, 2, 1024).astype(jnp.float32)
        all_hidden = small[:, :, 512:768].reshape(2, 4096).astype(jnp.float32)
        seg = small[0, :, 768:896].reshape(16, 2, 64)
        seg = jnp.where(micro == 0, seg[:, 0], seg[:, 1]).reshape(1024)
        own_biases = jnp.where(on_first, all_biases[0], all_biases[1])
        own_gains = jnp.where(on_first, all_gains[0], all_gains[1])
        own_hidden = jnp.where(on_first, all_hidden[0], all_hidden[1])
        head_bias = lax.dynamic_slice_in_dim(
            all_biases.reshape(2, 6, HEADS, HEAD_DIM), head, 1, 2
        )[:, :, 0]
        head_bias = jnp.concatenate(
            [head_bias[:, 0], jnp.zeros_like(head_bias[:, 0]), head_bias[:, 1]], 1
        )

    def attention(layer, tokens):
        with jax.named_scope("sequence_tokens"):
            whole = whole_sequence(tokens)
        with jax.named_scope("attention"):
            packed = (matmul(whole, head_weight[layer]) + head_bias[layer]).astype(LOW)
            context, log_totals = attend(packed, seg)
        with jax.named_scope("context_out"):
            context = to_tokens(context, 1)
        return context, (whole, packed, log_totals)

    def attention_back(layer, grad_context, kept):
        whole, packed, log_totals = kept
        with jax.named_scope("grad_context_in"):
            grad_context = to_head(grad_context, layer)
        with jax.named_scope("attention_back"):
            grad_packed = attend_back(packed, log_totals, seg, grad_context)
            grad_weight = transposed_times(whole, grad_packed)
            grad_sums = jnp.sum(grad_packed.astype(jnp.float32), 0)
        return grad_packed, grad_weight, grad_sums

    context_0, kept_0 = attention(0, inputs)
    tokens_0 = inputs.reshape(128, 1024)
    with jax.named_scope("block_0"):
        output, unused = block_forward(
            tokens_0, context_0, weights, own_biases, own_hidden, own_gains
        )
    with jax.named_scope("to_next_section"):
        tokens_1 = jnp.where(
            on_first, output, lax.ppermute(output, "section", [(0, 1)])
        )
    with jax.named_scope("gather_attend_weight"):
        late_weight, unused = lax.optimization_barrier((attend_weight[0], output))
        whole_attend = lax.all_gather(late_weight, "shard", axis=0, tiled=True)
    context_1, kept_1 = attention(1, tokens_1.reshape(2, 64, 1024))
    own_tokens = jnp.where(on_first, tokens_0, tokens_1)
    own_context = jnp.where(on_first, context_0, context_1)
    with jax.named_scope("block_1"):
        output, saved = block_forward(
            own_tokens, own_context, weights, own_biases, own_hidden, own_gains
        )
    layer_output = output.reshape(1, 2, 1, 64, 1024)
    with jax.named_scope("gather_first"):
        first_all = lax.all_gather(saved[1], "shard", axis=0, tiled=True)

    last_grad = cotangent.reshape(128, 1024)
    with jax.named_scope("block_back_1"):
        unused, grad_residual, unused, grad_context, unused = block_back(
            last_grad.astype(jnp.float32), saved, weights, own_biases, own_gains
        )
    grad_packed, grad_attend_1, grad_sums_1 = attention_back(1, grad_context, kept_1)
    with jax.named_scope("grad_tokens_1"):
        grad_tokens_1 = grad_residual + times_transposed(to_tokens(grad_packed, 3), whole_attend)
    with jax.named_scope("to_previous_section"):
        arrived = lax.ppermute(grad_tokens_1.astype(LOW), "section", [(1, 0)])
        own_grad = jnp.where(on_first, arrived, last_grad)
    with jax.named_scope("block_back_0"):
        grad_mlp, grad_residual, grad_attn, grad_context, norm_sums = block_back(
            own_grad.astype(jnp.float32), saved, weights, own_biases, own_gains
        )
    with jax.named_scope("gather_grad_mlp"):
        grad_mlp_all = lax.all_gather(grad_mlp, "shard", axis=0, tiled=True)
    grad_packed, grad_attend_0, grad_sums_0 = attention_back(0, grad_context, kept_0)

    with jax.named_scope("swap_attend_grad"):
        grad_attend_0 = grad_attend_0.astype(LOW)
        grad_attend_1 = grad_attend_1.astype(LOW)
        sums = jnp.stack([grad_sums_0, grad_sums_1]).astype(LOW)
        pad = jnp.zeros((15, 192), LOW)
        part_0 = jnp.concatenate([grad_attend_0, sums[0:1], pad], 0)
        part_1 = jnp.concatenate([grad_attend_1, sums[1:2], pad], 0)
        keep = jnp.where(on_first, part_0, part_1)
        give = jnp.where(on_first, part_1, part_0)
        take = lax.ppermute(give, "section", [(0, 1), (1, 0)])
        lower = jnp.where(on_first, keep, take)
        upper = jnp.where(on_first, take, keep)
        attend_part = jnp.concatenate([lower[:1024], upper[:1024]], 1)
        sums = jnp.stack([lower[1024], upper[1024]]).reshape(2, 3, HEAD_DIM)
    with jax.named_scope("block_weight_grads"):
        quarter = lax.dynamic_index_in_dim(
            jnp.stack([part for part in weights[1]]), shard // 4, 0, keepdims=False
        )
        expand_part = lax.dynamic_slice_in_dim(quarter, (shard % 4) * 256, 256, 1)
        hidden_part = lax.dynamic_slice_in_dim(own_hidden, shard * 256, 256, 0)
        inner = matmul(first_all, expand_part) + hidden_part
        activation, gelu_back = jax.vjp(gelu_exact, inner)
        grad_inner = gelu_back(times_transposed(grad_mlp_all, contract_weight[0]))[0].astype(LOW)
        expand_grad = transposed_times(first_all, grad_inner)
        contract_grad = transposed_times(activation.astype(LOW), grad_mlp_all)
        output_grad = transposed_times(own_context, grad_attn)
        hidden_sum = jnp.sum(grad_inner.astype(jnp.float32), 0)
        mlp_sum = jnp.sum(grad_mlp_all.astype(jnp.float32), 0)
    with jax.named_scope("sum_contract"):
        rows = jnp.concatenate(
            [
                contract_grad,
                jnp.concatenate([hidden_sum, jnp.zeros((768,), jnp.float32)])[None],
                mlp_sum[None],
                jnp.zeros((14, 1024), jnp.float32),
            ],
            0,
        ).astype(LOW)
        contract_total = lax.psum(rows, "replica").astype(jnp.float32)
    with jax.named_scope("sum_weight_grads"):
        norm_rows = norm_sums.reshape(5, 16, 64).transpose(1, 0, 2)
        mine = jnp.arange(8) == shard % 8
        head_rows = jnp.where(
            mine[None, :, None, None], sums[:, None, ::2].astype(jnp.float32), 0.0
        ).reshape(16, 2, 64)
        vectors = jnp.pad(
            jnp.concatenate([norm_rows, head_rows], 1), ((0, 0), (0, 9), (0, 64))
        )
        vectors = jnp.broadcast_to(vectors[:, None], (16, 4, 16, 128)).reshape(1024, 128)
        parts = jnp.concatenate(
            [
                attend_part,
                output_grad.astype(LOW),
                expand_grad.astype(LOW),
                vectors.astype(LOW),
            ],
            1,
        )
        got = exchange(parts.reshape(64, 16, 1792), REST).astype(jnp.float32)
        got_attend = got[:, :, :384].reshape(2, 8, 4, 16, 2, 3, 64).sum((0, 2))
        got_attend = got_attend.transpose(1, 3, 2, 0, 4).reshape(16, 3072)
        got_output = got[:, :, 384:1408].sum(0)
        got_expand = got[:, :, 1408:1664].reshape(16, 4, 16, 256).sum(1)
        got_expand = got_expand.transpose(1, 0, 2).reshape(16, 4096)
        got_vectors = got[:, :7, 1664:1728].sum(0)
        owned = jnp.concatenate([got_attend, got_output, got_expand], 1).astype(LOW)
    with jax.named_scope("gather_weight_grads"):
        totals = lax.all_gather(owned, "replica", axis=0, tiled=True)
        totals = totals.astype(jnp.float32)
    with jax.named_scope("grad_tokens_0"):
        late_packed, unused = lax.optimization_barrier((grad_packed, owned))
        grad_tokens_0 = grad_residual + times_transposed(to_tokens(late_packed, 3), whole_attend)
    input_grad = jnp.where(on_first, grad_tokens_0, grad_tokens_1).reshape(1, 2, 1, 64, 1024)
    mlp_own = lax.dynamic_slice_in_dim(contract_total[257], shard * 64, 64, 0)
    biases_grad = jnp.stack(
        [
            got_vectors[5],
            got_vectors[6],
            got_vectors[2],
            got_vectors[3],
            mlp_own,
            got_vectors[4],
        ]
    )
    return (
        layer_output,
        input_grad,
        totals[None, :, :3072],
        totals[None, :, 3072:4096],
        totals[None, :, 4096:],
        contract_total[None, :256],
        biases_grad[None],
        contract_total[None, 256, :256],
        got_vectors[None, :2],
    )


def solution(mesh):
    placed = (
        P(None, "replica", "shard", None),
        P(None, "replica", "shard"),
        P(None, "replica", "shard", None),
        P("section", "shard", None),
        P("section", "shard", None),
        P("section", "shard", None),
        P("section", "shard", None),
        P("section", None, "shard"),
        P("section", "shard"),
        P("section", None, "shard"),
    )
    return jax.shard_map(
        on_device,
        mesh=mesh,
        in_specs=placed,
        out_specs=(
            P("section", None, "replica", "shard", None),
            P("section", None, "replica", "shard", None),
            P("section", "shard", None),
            P("section", "shard", None),
            P("section", "shard", None),
            P("section", "shard", None),
            P("section", None, "shard"),
            P("section", "shard"),
            P("section", None, "shard"),
        ),
        check_vma=False,
    )
```

```python
import math

import jax
import jax.numpy as jnp
from jax import lax
from jax.sharding import PartitionSpec as P

HEADS = 16
HEAD_DIM = 64
NEGATIVE = -1e30
EPSILON = 1e-05
SCALE = 1.0 / math.sqrt(HEAD_DIM)
LOW = jnp.bfloat16
ALL = ("section", "shard")
REST = ("shard", "replica")


def layer_norm(value, gain, shift):
    mean_value = jnp.mean(value, -1, keepdims=True)
    centred = value - mean_value
    spread = jnp.mean(centred * centred, -1, keepdims=True)
    return centred * lax.rsqrt(spread + EPSILON) * gain + shift


def gelu_exact(value):
    return jax.nn.gelu(value, approximate=False)


def matmul(left, right):
    return jnp.dot(left, right, preferred_element_type=jnp.float32)


def times_transposed(left, right):
    return lax.dot_general(
        left, right, (((1,), (1,)), ((), ())), preferred_element_type=jnp.float32
    )


def transposed_times(left, right):
    return lax.dot_general(
        left, right, (((0,), (0,)), ((), ())), preferred_element_type=jnp.float32
    )


def exchange(value, axes):
    return lax.all_to_all(value, axes, 0, 0, tiled=True)


def swap_cores(value):
    return lax.ppermute(value, "shard", [(i, i ^ 1) for i in range(16)])


def whole_sequence(tokens):
    core = lax.axis_index("shard") % 2
    micros, rows, features = tokens.shape
    half = rows // 2
    sends = jnp.broadcast_to(
        tokens.reshape(micros, 1, 2, half, features), (micros, 4, 2, half, features)
    ).reshape(16, half, features)
    mine = exchange(sends, "shard")
    other = swap_cores(mine)
    lower = jnp.where(core == 0, mine, other)
    upper = jnp.where(core == 0, other, mine)
    return jnp.stack([lower, upper], 1).reshape(16 * rows, features)


def send_tokens(value, parts):
    core = lax.axis_index("shard") % 2
    width = parts * HEAD_DIM
    halves = value.reshape(16, 2, 32, width)
    keep = jnp.where(core == 0, halves[:, 0], halves[:, 1])
    take = swap_cores(jnp.where(core == 0, halves[:, 1], halves[:, 0]))
    lower = jnp.split(jnp.where(core == 0, keep, take), parts, 2)
    upper = jnp.split(jnp.where(core == 0, take, keep), parts, 2)
    pair = jnp.concatenate([piece for both in zip(lower, upper) for piece in both], 2)
    sends = jnp.broadcast_to(pair[None], (2, 16, 32, 2 * width)).reshape(32, 32, 2 * width)
    return exchange(sends, ALL).reshape(2, 2, 4, 2, 32, 2 * width)


def as_rows(got):
    return got.transpose(1, 3, 4, 0, 2, 5).reshape(128, 8 * got.shape[-1])


def to_head(value, layer):
    core = lax.axis_index("shard") % 2
    sends = value.reshape(2, 64, 2, 4, 128).transpose(2, 0, 3, 1, 4)[:, :, :, None]
    sends = jnp.broadcast_to(sends, (2, 2, 4, 2, 64, 128)).reshape(32, 64, 128)
    got = exchange(sends, ALL)
    got = got[16 * layer : 16 * layer + 16].reshape(1024, 128)
    return jnp.where(core == 0, got[:, :HEAD_DIM], got[:, HEAD_DIM:])


def masked_scores(queries, keys, seg):
    scores = times_transposed(queries, keys) * SCALE
    return jnp.where(seg[:, None] == seg[None, :], scores, NEGATIVE)


def attend(packed, seg):
    queries, keys, values = jnp.split(packed, 3, 1)
    scores = masked_scores(queries, keys, seg)
    highest = jnp.max(scores, -1, keepdims=True)
    exponent = jnp.exp(scores - highest)
    totals = jnp.sum(exponent, -1, keepdims=True)
    context = matmul((exponent / totals).astype(LOW), values).astype(LOW)
    return context, highest + jnp.log(totals)


def attend_back(packed, log_totals, seg, grad_context):
    queries, keys, values = jnp.split(packed, 3, 1)
    soft = jnp.exp(masked_scores(queries, keys, seg) - log_totals)
    grad_soft = times_transposed(grad_context, values)
    row_total = jnp.sum(soft * grad_soft, -1, keepdims=True)
    grad_scores = (soft * (grad_soft - row_total)).astype(LOW)
    return jnp.concatenate(
        [
            matmul(grad_scores, keys) * SCALE,
            transposed_times(grad_scores, queries) * SCALE,
            transposed_times(soft.astype(LOW), grad_context),
        ],
        1,
    ).astype(LOW)


def block_forward(tokens, context, weights, biases, hidden_bias, gains):
    output_weight, expand_weight, contract_weight = weights
    residual = tokens.astype(jnp.float32) + (matmul(context, output_weight) + biases[2])
    first = layer_norm(residual, gains[0], biases[3])
    first_low = first.astype(LOW)
    inner = jnp.concatenate([matmul(first_low, part) for part in expand_weight], 1) + hidden_bias
    activation = gelu_exact(inner).astype(LOW)
    second = first + (matmul(activation, contract_weight) + biases[4])
    output = layer_norm(second, gains[1], biases[5]).astype(LOW)
    return output, (residual, first_low, inner, second)


def block_back(grad, saved, weights, biases, gains):
    output_weight, expand_weight, contract_weight = weights
    residual, first_low, inner, second = saved
    unused, norm_back_two = jax.vjp(layer_norm, second, gains[1], biases[5])
    grad_second, grad_gain_two, grad_shift_two = norm_back_two(grad)
    grad_mlp = grad_second.astype(LOW)
    unused, gelu_back = jax.vjp(gelu_exact, inner)
    grad_inner = gelu_back(times_transposed(grad_mlp, contract_weight))[0].astype(LOW)
    grad_first = grad_second
    for part, piece in zip(expand_weight, jnp.split(grad_inner, 4, 1)):
        grad_first = grad_first + times_transposed(piece, part)
    unused, norm_back_one = jax.vjp(layer_norm, residual, gains[0], biases[3])
    grad_residual, grad_gain_one, grad_shift_one = norm_back_one(grad_first)
    grad_attn = grad_residual.astype(LOW)
    grad_context = times_transposed(grad_attn, output_weight).astype(LOW)
    attn_sum = jnp.sum(grad_attn.astype(jnp.float32), 0)
    sums = jnp.stack([grad_gain_one, grad_gain_two, attn_sum, grad_shift_one, grad_shift_two])
    return grad_mlp, grad_residual, grad_attn, grad_context, sums


def unpack_weights(gathered):
    return (
        gathered[:, :64].reshape(1024, 1024),
        [gathered[:, 64 + 64 * q : 128 + 64 * q].reshape(1024, 1024) for q in range(4)],
        gathered[:, 320:576].reshape(4096, 1024),
    )


def with_sums(grad, sums):
    rows = jnp.concatenate([sums[None], jnp.zeros((15, sums.shape[0]), jnp.float32)], 0)
    return jnp.concatenate([grad.astype(LOW), rows.astype(LOW)], 0)


def on_device(
    inputs,
    segments,
    cotangent,
    attend_weight,
    output_weight,
    expand_weight,
    contract_weight,
    biases,
    hidden_bias,
    gains,
):
    section = lax.axis_index("section")
    shard = lax.axis_index("shard")
    on_first = section == 0
    micro = shard // 8
    head = section * 8 + shard % 8
    inputs = inputs[:, 0]

    with jax.named_scope("gather_block_weights"):
        rows = jnp.concatenate(
            [output_weight[0]] + jnp.split(expand_weight[0], 4, 1) + [contract_weight[0]], 0
        )
        quarter = lax.dynamic_slice_in_dim(rows, lax.axis_index("replica") * 144, 144, 0)
        gathered = lax.all_gather(quarter, REST, axis=0, tiled=False).reshape(16, 576, 1024)
        weights = unpack_weights(gathered)

    with jax.named_scope("head_weights"):
        by_head = attend_weight[0].reshape(64, 3, HEADS, HEAD_DIM).transpose(2, 0, 1, 3)
        small = jnp.concatenate(
            [
                biases.reshape(384),
                gains.reshape(128),
                hidden_bias.reshape(256),
                segments.reshape(128).astype(LOW),
                jnp.zeros((16 * 192 - 896,), LOW),
            ]
        ).reshape(1, 16, 192)
        block = jnp.concatenate(
            [by_head.reshape(HEADS, 64, 192), jnp.broadcast_to(small, (HEADS, 16, 192))], 1
        )
        block = jnp.broadcast_to(block.reshape(2, 1, 8, 80, 192), (2, 2, 8, 80, 192))
        got = exchange(block.reshape(32, 80, 192), ALL).reshape(2, 16, 80, 192)
        head_weight = got[:, :, :64].reshape(2, 1024, 192)
        small = got[:, :, 64:69].reshape(2, 16, 960)
        all_biases = small[:, :, :384].reshape(2, 16, 6, 64).transpose(0, 2, 1, 3)
        all_biases = all_biases.reshape(2, 6, 1024).astype(jnp.float32)
        all_gains = small[:, :, 384:512].reshape(2, 16, 2, 64).transpose(0, 2, 1, 3)
        all_gains = all_gains.reshape(2, 2, 1024).astype(jnp.float32)
        all_hidden = small[:, :, 512:768].reshape(2, 4096).astype(jnp.float32)
        seg = small[0, :, 768:896].reshape(16, 2, 64)
        seg = jnp.where(micro == 0, seg[:, 0], seg[:, 1]).reshape(1024)
        own_biases = jnp.where(on_first, all_biases[0], all_biases[1])
        own_gains = jnp.where(on_first, all_gains[0], all_gains[1])
        own_hidden = jnp.where(on_first, all_hidden[0], all_hidden[1])
        head_bias = lax.dynamic_slice_in_dim(
            all_biases.reshape(2, 6, HEADS, HEAD_DIM), head, 1, 2
        )[:, :, 0]
        head_bias = jnp.concatenate(
            [head_bias[:, 0], jnp.zeros_like(head_bias[:, 0]), head_bias[:, 1]], 1
        )

    def attention(layer, tokens):
        with jax.named_scope("sequence_tokens"):
            whole = whole_sequence(tokens)
        with jax.named_scope("attention"):
            packed = (matmul(whole, head_weight[layer]) + head_bias[layer]).astype(LOW)
            context, log_totals = attend(packed, seg)
        with jax.named_scope("context_out"):
            context = as_rows(send_tokens(context, 1))
        return context, (whole, packed, log_totals)

    def attention_back(layer, grad_context, kept):
        whole, packed, log_totals = kept
        with jax.named_scope("grad_context_in"):
            grad_context = to_head(grad_context, layer)
        with jax.named_scope("attention_back"):
            grad_packed = attend_back(packed, log_totals, seg, grad_context)
            grad_weight = transposed_times(whole, grad_packed)
            grad_sums = jnp.sum(grad_packed.astype(jnp.float32), 0)
        return grad_packed, grad_weight, grad_sums

    context_0, kept_0 = attention(0, inputs)
    tokens_0 = inputs.reshape(128, 1024)
    with jax.named_scope("block_0"):
        output, unused = block_forward(
            tokens_0, context_0, weights, own_biases, own_hidden, own_gains
        )
    with jax.named_scope("to_next_section"):
        tokens_1 = jnp.where(
            on_first, output, lax.ppermute(output, "section", [(0, 1)])
        )
    with jax.named_scope("gather_attend_weight"):
        by_pair = attend_weight[0].reshape(64, 3, 8, 128).transpose(0, 2, 1, 3).reshape(64, 3072)
        late_weight, unused = lax.optimization_barrier((by_pair, output))
        whole_attend = lax.all_gather(late_weight, "shard", axis=0, tiled=True)
    context_1, kept_1 = attention(1, tokens_1.reshape(2, 64, 1024))
    own_tokens = jnp.where(on_first, tokens_0, tokens_1)
    own_context = jnp.where(on_first, context_0, context_1)
    with jax.named_scope("block_1"):
        output, saved = block_forward(
            own_tokens, own_context, weights, own_biases, own_hidden, own_gains
        )
    layer_output = output.reshape(1, 2, 1, 64, 1024)
    with jax.named_scope("gather_first"):
        first_all = lax.all_gather(saved[1], "shard", axis=0, tiled=True)

    last_grad = cotangent.reshape(128, 1024)
    with jax.named_scope("block_back_1"):
        unused, grad_residual, unused, grad_context, unused = block_back(
            last_grad.astype(jnp.float32), saved, weights, own_biases, own_gains
        )
    grad_packed, grad_attend_1, grad_sums_1 = attention_back(1, grad_context, kept_1)
    with jax.named_scope("swap_attend_grad"):
        part_1 = with_sums(grad_attend_1, grad_sums_1)
        take_1 = lax.ppermute(part_1, "section", [(0, 1)])
    with jax.named_scope("grad_tokens_1"):
        grad_tokens_1 = grad_residual + times_transposed(as_rows(send_tokens(grad_packed, 3)), whole_attend)
    with jax.named_scope("to_previous_section"):
        arrived = lax.ppermute(grad_tokens_1.astype(LOW), "section", [(1, 0)])
        own_grad = jnp.where(on_first, arrived, last_grad)
    with jax.named_scope("block_back_0"):
        grad_mlp, grad_residual, grad_attn, grad_context, norm_sums = block_back(
            own_grad.astype(jnp.float32), saved, weights, own_biases, own_gains
        )
    with jax.named_scope("gather_grad_mlp"):
        grad_mlp_all = lax.all_gather(grad_mlp, "shard", axis=0, tiled=True)
    grad_packed, grad_attend_0, grad_sums_0 = attention_back(0, grad_context, kept_0)

    with jax.named_scope("sum_attend_grads"):
        part_0 = with_sums(grad_attend_0, grad_sums_0)
        take_0 = lax.ppermute(part_0, "section", [(1, 0)])
        lower = jnp.where(on_first, part_0, take_1)
        upper = jnp.where(on_first, take_0, part_1)
        attend_part = jnp.concatenate([lower[:1024], upper[:1024]], 1)
        sums = jnp.stack([lower[1024], upper[1024]]).reshape(2, 3, HEAD_DIM)
        output_grad = transposed_times(own_context, grad_attn).astype(LOW)
        norm_rows = norm_sums.reshape(5, 16, 64).transpose(1, 0, 2)
        mine = jnp.arange(8) == shard % 8
        head_rows = jnp.where(
            mine[None, :, None, None], sums[:, None, ::2].astype(jnp.float32), 0.0
        ).reshape(16, 2, 64)
        vectors = jnp.pad(
            jnp.concatenate([norm_rows, head_rows], 1), ((0, 0), (0, 9), (0, 64))
        )
        vectors = jnp.broadcast_to(vectors[:, None], (16, 4, 16, 128)).reshape(1024, 128)
        parts = jnp.concatenate([attend_part, output_grad, vectors.astype(LOW)], 1)
        got = exchange(parts.reshape(64, 16, 1536), REST)
    with jax.named_scope("block_weight_grads"):
        quarter = lax.dynamic_index_in_dim(
            jnp.stack([part for part in weights[1]]), shard // 4, 0, keepdims=False
        )
        expand_part = lax.dynamic_slice_in_dim(quarter, (shard % 4) * 256, 256, 1)
        hidden_part = lax.dynamic_slice_in_dim(own_hidden, shard * 256, 256, 0)
        inner = matmul(first_all, expand_part) + hidden_part
        activation, gelu_back = jax.vjp(gelu_exact, inner)
        grad_inner = gelu_back(times_transposed(grad_mlp_all, contract_weight[0]))[0].astype(LOW)
        expand_grad = transposed_times(first_all, grad_inner).astype(LOW)
        contract_grad = transposed_times(activation.astype(LOW), grad_mlp_all).astype(LOW)
        hidden_sum = jnp.sum(grad_inner.astype(jnp.float32), 0)
        mlp_sum = jnp.sum(grad_mlp_all.astype(jnp.float32), 0)
        extra = jnp.concatenate(
            [
                jnp.concatenate([hidden_sum, jnp.zeros((768,), jnp.float32)])[None],
                mlp_sum[None],
                jnp.zeros((14, 1024), jnp.float32),
            ],
            0,
        ).astype(LOW)
        rows = jnp.concatenate(
            [contract_grad.reshape(4, 64, 1024), jnp.broadcast_to(extra, (4, 16, 1024))], 1
        )
    got, expand_grad, rows = lax.optimization_barrier((got, expand_grad, rows))
    with jax.named_scope("sum_expand"):
        got_expand = exchange(expand_grad.reshape(64, 16, 256), REST).reshape(16, 4, 16, 256)
        got_expand = got_expand.astype(jnp.float32).sum(1).astype(LOW)
        got_expand = got_expand.transpose(1, 0, 2).reshape(16, 4096)
    with jax.named_scope("sum_contract"):
        got_contract = exchange(rows, "replica").astype(jnp.float32).sum(0)
    with jax.named_scope("sum_attend_grads"):
        got_attend = got[:, :, :384].astype(jnp.float32).reshape(2, 8, 4, 16, 384).sum((0, 2))
        got_output = got[:, :, 384:1408].astype(jnp.float32).sum(0).astype(LOW)
        got_vectors = got[:, :7, 1408:1472].astype(jnp.float32).sum(0)
        got_attend, got_output = lax.optimization_barrier((got_attend.astype(LOW), got_output))
        got_attend = got_attend.reshape(8, 16, 2, 3, 64).transpose(1, 3, 2, 0, 4)
        got_attend = got_attend.reshape(16, 3072)
    with jax.named_scope("gather_weight_grads"):
        contract_rows = got_contract[:64].astype(LOW).reshape(4, 16, 1024)
        owned = jnp.concatenate([got_attend, got_output, got_expand, *contract_rows], 1)
    with jax.named_scope("grad_tokens_0"):
        late_packed, owned = lax.optimization_barrier((grad_packed, owned))
        packed_rows = as_rows(send_tokens(late_packed, 3))
        grad_tokens_0 = grad_residual + times_transposed(packed_rows, whole_attend)
    with jax.named_scope("gather_weight_grads"):
        totals = lax.all_gather(owned, "replica", axis=0, tiled=True)
        contract_total = totals[:, 8192:].reshape(4, 16, 4, 1024).transpose(0, 2, 1, 3)
        contract_total = contract_total.reshape(1, 256, 1024).astype(jnp.float32)
        totals = totals[None, :, :8192].astype(jnp.float32)
    input_grad = jnp.where(on_first, grad_tokens_0, grad_tokens_1).reshape(1, 2, 1, 64, 1024)
    mlp_own = lax.dynamic_slice_in_dim(got_contract[65], shard * 64, 64, 0)
    biases_grad = jnp.stack(
        [
            got_vectors[5],
            got_vectors[6],
            got_vectors[2],
            got_vectors[3],
            mlp_own,
            got_vectors[4],
        ]
    )
    return (
        layer_output,
        input_grad,
        totals[:, :, :3072],
        totals[:, :, 3072:4096],
        totals[:, :, 4096:],
        contract_total,
        biases_grad[None],
        got_contract[None, 64, :256],
        got_vectors[None, :2],
    )


def solution(mesh):
    placed = (
        P(None, "replica", "shard", None),
        P(None, "replica", "shard"),
        P(None, "replica", "shard", None),
        P("section", "shard", None),
        P("section", "shard", None),
        P("section", "shard", None),
        P("section", "shard", None),
        P("section", None, "shard"),
        P("section", "shard"),
        P("section", None, "shard"),
    )
    return jax.shard_map(
        on_device,
        mesh=mesh,
        in_specs=placed,
        out_specs=(
            P("section", None, "replica", "shard", None),
            P("section", None, "replica", "shard", None),
            P("section", "shard", None),
            P("section", "shard", None),
            P("section", "shard", None),
            P("section", "shard", None),
            P("section", None, "shard"),
            P("section", "shard"),
            P("section", None, "shard"),
        ),
        check_vma=False,
    )
```

```python
import math

import jax
import jax.numpy as jnp
from jax import lax
from jax.experimental import pallas as pl
from jax.experimental.pallas import tpu as pltpu
from jax.sharding import PartitionSpec as P

HEADS = 16
HEAD_DIM = 64
NEGATIVE = -1e30
EPSILON = 1e-05
SCALE = 1.0 / math.sqrt(HEAD_DIM)
LOW = jnp.bfloat16
ALL = ("section", "shard")
REST = ("shard", "replica")


def matmul(left, right):
    return jnp.dot(left, right, preferred_element_type=jnp.float32)


def times_transposed(left, right):
    return lax.dot_general(
        left, right, (((1,), (1,)), ((), ())), preferred_element_type=jnp.float32
    )


def transposed_times(left, right):
    return lax.dot_general(
        left, right, (((0,), (0,)), ((), ())), preferred_element_type=jnp.float32
    )


def exchange(value, axes):
    return lax.all_to_all(value, axes, 0, 0, tiled=True)


def swap_cores(value):
    return lax.ppermute(value, "shard", [(i, i ^ 1) for i in range(16)])


def whole_sequence(tokens):
    core = lax.axis_index("shard") % 2
    micros, rows, features = tokens.shape
    half = rows // 2
    sends = jnp.broadcast_to(
        tokens.reshape(micros, 1, 2, half, features), (micros, 4, 2, half, features)
    ).reshape(16, half, features)
    mine = exchange(sends, "shard")
    other = swap_cores(mine)
    lower = jnp.where(core == 0, mine, other)
    upper = jnp.where(core == 0, other, mine)
    return jnp.stack([lower, upper], 1).reshape(16 * rows, features)


def send_tokens(value, parts):
    core = lax.axis_index("shard") % 2
    width = parts * HEAD_DIM
    halves = value.reshape(16, 2, 32, width)
    keep = jnp.where(core == 0, halves[:, 0], halves[:, 1])
    take = swap_cores(jnp.where(core == 0, halves[:, 1], halves[:, 0]))
    lower = jnp.split(jnp.where(core == 0, keep, take), parts, 2)
    upper = jnp.split(jnp.where(core == 0, take, keep), parts, 2)
    pair = jnp.concatenate([piece for both in zip(lower, upper) for piece in both], 2)
    sends = jnp.broadcast_to(pair[None], (2, 16, 32, 2 * width)).reshape(32, 32, 2 * width)
    return exchange(sends, ALL).reshape(2, 2, 4, 2, 32, 2 * width)


def as_rows(got):
    return got.transpose(1, 3, 4, 0, 2, 5).reshape(128, 8 * got.shape[-1])


def to_head(value, layer):
    core = lax.axis_index("shard") % 2
    sends = value.reshape(2, 64, 2, 4, 128).transpose(2, 0, 3, 1, 4)[:, :, :, None]
    sends = jnp.broadcast_to(sends, (2, 2, 4, 2, 64, 128)).reshape(32, 64, 128)
    got = exchange(sends, ALL)
    got = got[16 * layer : 16 * layer + 16].reshape(1024, 128)
    return jnp.where(core == 0, got[:, :HEAD_DIM], got[:, HEAD_DIM:])


def masked_scores(queries, keys, seg):
    scores = times_transposed(queries, keys) * SCALE
    return jnp.where(seg[:, None] == seg[None, :], scores, NEGATIVE)


def attend(packed, seg):
    queries, keys, values = jnp.split(packed, 3, 1)
    scores = masked_scores(queries, keys, seg)
    highest = jnp.max(scores, -1, keepdims=True)
    exponent = jnp.exp(scores - highest)
    totals = jnp.sum(exponent, -1, keepdims=True)
    context = matmul((exponent / totals).astype(LOW), values).astype(LOW)
    return context, highest + jnp.log(totals)


def attend_back(packed, log_totals, seg, grad_context):
    queries, keys, values = jnp.split(packed, 3, 1)
    soft = jnp.exp(masked_scores(queries, keys, seg) - log_totals)
    grad_soft = times_transposed(grad_context, values)
    row_total = jnp.sum(soft * grad_soft, -1, keepdims=True)
    grad_scores = (soft * (grad_soft - row_total)).astype(LOW)
    return jnp.concatenate(
        [
            matmul(grad_scores, keys) * SCALE,
            transposed_times(grad_scores, queries) * SCALE,
            transposed_times(soft.astype(LOW), grad_context),
        ],
        1,
    ).astype(LOW)


def normed(value):
    mean_value = jnp.mean(value, -1, keepdims=True)
    centred = value - mean_value
    spread = jnp.mean(centred * centred, -1, keepdims=True)
    scale = lax.rsqrt(spread + EPSILON)
    return centred * scale, scale


def normed_back(grad, value, gain):
    unit, scale = normed(value)
    weighted = grad * gain
    inner_mean = jnp.mean(weighted * unit, -1, keepdims=True)
    grad_value = scale * (weighted - jnp.mean(weighted, -1, keepdims=True) - unit * inner_mean)
    return (
        grad_value,
        jnp.sum(grad * unit, 0, keepdims=True),
        jnp.sum(grad, 0, keepdims=True),
    )


def gelu_share(value):
    return 0.5 * (1.0 + lax.erf(value * math.sqrt(0.5)))


def gelu_slope(value):
    return gelu_share(value) + value * jnp.exp(-0.5 * value * value) * (0.5 / math.pi) ** 0.5


PARTS = 4
WIDTH = 1024


def this_part(j):
    return jnp.minimum(j, PARTS - 1)


def part_before(j):
    return jnp.maximum(j - 1, 0)


def weight_specs(expand_at, contract_at):
    return [
        pl.BlockSpec((16, 64, 1024), lambda j: (0, 4, 0)),
        pl.BlockSpec((16, 64, WIDTH), lambda j: (0, 5 + expand_at(j), 0)),
        pl.BlockSpec((4, 256, 1024), lambda j: (contract_at(j), 0, 0)),
    ]


def full(*shape):
    return pl.BlockSpec(shape, lambda j: (0,) * len(shape))


ROWS_F32 = jax.ShapeDtypeStruct((128, 1024), jnp.float32)
ROWS_LOW = jax.ShapeDtypeStruct((128, 1024), LOW)
BLOCK_PARAMS = pltpu.CompilerParams(
    dimension_semantics=("arbitrary",), vmem_limit_bytes=48 * 1024 * 1024
)
BLOCK_COST = pl.CostEstimate(
    flops=2 * 128 * 1024 * 9216, bytes_accessed=24 * 1024 * 1024, transcendentals=128 * 4096
)


def forward_kernel(
    tokens,
    context,
    output_weight,
    expand_weight,
    contract_weight,
    params,
    hidden,
    output,
    residual,
    first_low,
    inner,
    second,
    first,
    total,
    before,
):
    step = pl.program_id(0)

    @pl.when(step == 0)
    def start():
        attention = matmul(context[...], output_weight[...].reshape(1024, 1024))
        summed = tokens[...].astype(jnp.float32) + (attention + params[0:1])
        residual[...] = summed
        after = normed(summed)[0] * params[4:5] + params[1:2]
        first[...] = after
        first_low[...] = after.astype(LOW)
        total[...] = jnp.zeros_like(total)
        before[...] = jnp.zeros_like(before)

    last_part = before[...]
    inner_part = matmul(first_low[...], expand_weight[...].reshape(1024, WIDTH)) + hidden[0]
    inner[...] = inner_part
    activation = (last_part * gelu_share(last_part)).astype(LOW)
    total[...] += matmul(activation, contract_weight[...].reshape(WIDTH, 1024))
    before[...] = inner_part

    @pl.when(step == PARTS)
    def finish():
        summed = first[...] + (total[...] + params[2:3])
        second[...] = summed
        output[...] = (normed(summed)[0] * params[5:6] + params[3:4]).astype(LOW)


def block_forward(tokens, context, gathered, params, hidden):
    output, *saved = pl.pallas_call(
        forward_kernel,
        grid=(PARTS + 1,),
        in_specs=[
            full(128, 1024),
            full(128, 1024),
            *weight_specs(this_part, part_before),
            full(8, 1024),
            pl.BlockSpec((1, 1, WIDTH), lambda j: (this_part(j), 0, 0)),
        ],
        out_specs=[
            full(128, 1024),
            full(128, 1024),
            full(128, 1024),
            pl.BlockSpec((128, WIDTH), lambda j: (0, this_part(j))),
            full(128, 1024),
        ],
        out_shape=[
            ROWS_LOW,
            ROWS_F32,
            ROWS_LOW,
            jax.ShapeDtypeStruct((128, 4096), jnp.float32),
            ROWS_F32,
        ],
        scratch_shapes=[
            pltpu.VMEM((128, 1024), jnp.float32),
            pltpu.VMEM((128, 1024), jnp.float32),
            pltpu.VMEM((128, WIDTH), jnp.float32),
        ],
        compiler_params=BLOCK_PARAMS,
        cost_estimate=BLOCK_COST,
    )(tokens, context, gathered, gathered, gathered, params, hidden)
    return output, saved


def backward_kernel(
    grad,
    output_weight,
    expand_weight,
    contract_weight,
    params,
    residual,
    inner,
    second,
    grad_mlp,
    grad_residual,
    grad_attn,
    grad_context,
    sums,
    grad_second,
    total,
    before,
):
    step = pl.program_id(0)

    @pl.when(step == 0)
    def start():
        by_value, by_gain, by_shift = normed_back(
            grad[...].astype(jnp.float32), second[...], params[5:6]
        )
        grad_second[...] = by_value
        grad_mlp[...] = by_value.astype(LOW)
        sums[1:2] = by_gain
        sums[4:5] = by_shift
        total[...] = jnp.zeros_like(total)
        before[...] = jnp.zeros_like(before)

    last_part = before[...]
    before[...] = times_transposed(grad_mlp[...], contract_weight[...].reshape(WIDTH, 1024))
    grad_inner = (last_part * gelu_slope(inner[...])).astype(LOW)
    total[...] += times_transposed(grad_inner, expand_weight[...].reshape(1024, WIDTH))

    @pl.when(step == PARTS)
    def finish():
        by_value, by_gain, by_shift = normed_back(
            grad_second[...] + total[...], residual[...], params[4:5]
        )
        grad_residual[...] = by_value
        rounded = by_value.astype(LOW)
        grad_attn[...] = rounded
        grad_context[...] = times_transposed(
            rounded, output_weight[...].reshape(1024, 1024)
        ).astype(LOW)
        sums[0:1] = by_gain
        sums[2:3] = jnp.sum(rounded.astype(jnp.float32), 0, keepdims=True)
        sums[3:4] = by_shift
        sums[5:8] = jnp.zeros((3, 1024), jnp.float32)


def block_back(grad, saved, gathered, params):
    residual, unused, inner, second = saved
    return pl.pallas_call(
        backward_kernel,
        grid=(PARTS + 1,),
        in_specs=[
            full(128, 1024),
            *weight_specs(part_before, this_part),
            full(8, 1024),
            full(128, 1024),
            pl.BlockSpec((128, WIDTH), lambda j: (0, part_before(j))),
            full(128, 1024),
        ],
        out_specs=[full(128, 1024)] * 4 + [full(8, 1024)],
        out_shape=[
            ROWS_LOW,
            ROWS_F32,
            ROWS_LOW,
            ROWS_LOW,
            jax.ShapeDtypeStruct((8, 1024), jnp.float32),
        ],
        scratch_shapes=[
            pltpu.VMEM((128, 1024), jnp.float32),
            pltpu.VMEM((128, 1024), jnp.float32),
            pltpu.VMEM((128, WIDTH), jnp.float32),
        ],
        compiler_params=BLOCK_PARAMS,
        cost_estimate=BLOCK_COST,
    )(grad, gathered, gathered, gathered, params, residual, inner, second)


def with_sums(grad, sums):
    rows = jnp.concatenate([sums[None], jnp.zeros((15, sums.shape[0]), jnp.float32)], 0)
    return jnp.concatenate([grad.astype(LOW), rows.astype(LOW)], 0)


def on_device(
    inputs,
    segments,
    cotangent,
    attend_weight,
    output_weight,
    expand_weight,
    contract_weight,
    biases,
    hidden_bias,
    gains,
):
    section = lax.axis_index("section")
    shard = lax.axis_index("shard")
    on_first = section == 0
    micro = shard // 8
    head = section * 8 + shard % 8
    inputs = inputs[:, 0]

    with jax.named_scope("gather_block_weights"):
        rows = jnp.concatenate(
            [contract_weight[0], output_weight[0]] + jnp.split(expand_weight[0], 4, 1), 0
        )
        quarter = lax.dynamic_slice_in_dim(rows, lax.axis_index("replica") * 144, 144, 0)
        gathered = lax.all_gather(quarter, REST, axis=0, tiled=False).reshape(16, 576, 1024)

    with jax.named_scope("head_weights"):
        by_head = attend_weight[0].reshape(64, 3, HEADS, HEAD_DIM).transpose(2, 0, 1, 3)
        small = jnp.concatenate(
            [
                biases.reshape(384),
                gains.reshape(128),
                hidden_bias.reshape(256),
                segments.reshape(128).astype(LOW),
                jnp.zeros((16 * 192 - 896,), LOW),
            ]
        ).reshape(1, 16, 192)
        block = jnp.concatenate(
            [by_head.reshape(HEADS, 64, 192), jnp.broadcast_to(small, (HEADS, 16, 192))], 1
        )
        block = jnp.broadcast_to(block.reshape(2, 1, 8, 80, 192), (2, 2, 8, 80, 192))
        got = exchange(block.reshape(32, 80, 192), ALL).reshape(2, 16, 80, 192)
        head_weight = got[:, :, :64].reshape(2, 1024, 192)
        small = got[:, :, 64:69].reshape(2, 16, 960)
        all_biases = small[:, :, :384].reshape(2, 16, 6, 64).transpose(0, 2, 1, 3)
        all_biases = all_biases.reshape(2, 6, 1024).astype(jnp.float32)
        all_gains = small[:, :, 384:512].reshape(2, 16, 2, 64).transpose(0, 2, 1, 3)
        all_gains = all_gains.reshape(2, 2, 1024).astype(jnp.float32)
        all_hidden = small[:, :, 512:768].reshape(2, 4096).astype(jnp.float32)
        seg = small[0, :, 768:896].reshape(16, 2, 64)
        seg = jnp.where(micro == 0, seg[:, 0], seg[:, 1]).reshape(1024)
        own_biases = jnp.where(on_first, all_biases[0], all_biases[1])
        own_gains = jnp.where(on_first, all_gains[0], all_gains[1])
        own_hidden = jnp.where(on_first, all_hidden[0], all_hidden[1]).reshape(PARTS, 1, WIDTH)
        params = jnp.concatenate([own_biases[2:], own_gains, jnp.zeros((2, 1024))], 0)
        head_bias = lax.dynamic_slice_in_dim(
            all_biases.reshape(2, 6, HEADS, HEAD_DIM), head, 1, 2
        )[:, :, 0]
        head_bias = jnp.concatenate(
            [head_bias[:, 0], jnp.zeros_like(head_bias[:, 0]), head_bias[:, 1]], 1
        )

    def attention(layer, tokens):
        with jax.named_scope("sequence_tokens"):
            whole = whole_sequence(tokens)
        with jax.named_scope("attention"):
            packed = (matmul(whole, head_weight[layer]) + head_bias[layer]).astype(LOW)
            context, log_totals = attend(packed, seg)
        with jax.named_scope("context_out"):
            context = as_rows(send_tokens(context, 1))
        return context, (whole, packed, log_totals)

    def attention_back(layer, grad_context, kept):
        whole, packed, log_totals = kept
        with jax.named_scope("grad_context_in"):
            grad_context = to_head(grad_context, layer)
        with jax.named_scope("attention_back"):
            grad_packed = attend_back(packed, log_totals, seg, grad_context)
            grad_weight = transposed_times(whole, grad_packed)
            grad_sums = jnp.sum(grad_packed.astype(jnp.float32), 0)
        return grad_packed, grad_weight, grad_sums

    context_0, kept_0 = attention(0, inputs)
    tokens_0 = inputs.reshape(128, 1024)
    with jax.named_scope("block_0"):
        output, unused = block_forward(tokens_0, context_0, gathered, params, own_hidden)
    with jax.named_scope("to_next_section"):
        tokens_1 = jnp.where(
            on_first, output, lax.ppermute(output, "section", [(0, 1)])
        )
    with jax.named_scope("gather_attend_weight"):
        by_pair = attend_weight[0].reshape(64, 3, 8, 128).transpose(0, 2, 1, 3).reshape(64, 3072)
        late_weight, unused = lax.optimization_barrier((by_pair, output))
        whole_attend = lax.all_gather(late_weight, "shard", axis=0, tiled=True)
    context_1, kept_1 = attention(1, tokens_1.reshape(2, 64, 1024))
    own_tokens = jnp.where(on_first, tokens_0, tokens_1)
    own_context = jnp.where(on_first, context_0, context_1)
    with jax.named_scope("block_1"):
        output, saved = block_forward(own_tokens, own_context, gathered, params, own_hidden)
    layer_output = output.reshape(1, 2, 1, 64, 1024)
    with jax.named_scope("gather_first"):
        first_all = lax.all_gather(saved[1], "shard", axis=0, tiled=True)

    last_grad = cotangent.reshape(128, 1024)
    with jax.named_scope("block_back_1"):
        unused, grad_residual, unused, grad_context, unused = block_back(
            last_grad, saved, gathered, params
        )
    grad_packed, grad_attend_1, grad_sums_1 = attention_back(1, grad_context, kept_1)
    with jax.named_scope("swap_attend_grad"):
        part_1 = with_sums(grad_attend_1, grad_sums_1)
        take_1 = lax.ppermute(part_1, "section", [(0, 1)])
    with jax.named_scope("grad_tokens_1"):
        grad_tokens_1 = grad_residual + times_transposed(as_rows(send_tokens(grad_packed, 3)), whole_attend)
    with jax.named_scope("to_previous_section"):
        arrived = lax.ppermute(grad_tokens_1.astype(LOW), "section", [(1, 0)])
        own_grad = jnp.where(on_first, arrived, last_grad)
    with jax.named_scope("block_back_0"):
        grad_mlp, grad_residual, grad_attn, grad_context, norm_sums = block_back(
            own_grad, saved, gathered, params
        )
    with jax.named_scope("gather_grad_mlp"):
        grad_mlp_all = lax.all_gather(grad_mlp, "shard", axis=0, tiled=True)
    grad_packed, grad_attend_0, grad_sums_0 = attention_back(0, grad_context, kept_0)

    with jax.named_scope("sum_output_grad"):
        output_grad = transposed_times(own_context, grad_attn).astype(LOW)
        output_got = exchange(output_grad.reshape(64, 16, 1024), REST)
    with jax.named_scope("swap_attend_grad"):
        part_0 = with_sums(grad_attend_0, grad_sums_0)
        take_0 = lax.ppermute(part_0, "section", [(1, 0)])
        lower = jnp.where(on_first, part_0, take_1)
        upper = jnp.where(on_first, take_0, part_1)
        attend_part = jnp.concatenate([lower[:1024], upper[:1024]], 1)
        sums = jnp.stack([lower[1024], upper[1024]]).reshape(2, 3, HEAD_DIM)
        norm_rows = norm_sums[:5].reshape(5, 16, 64).transpose(1, 0, 2)
        mine = jnp.arange(8) == shard % 8
        head_rows = jnp.where(
            mine[None, :, None, None], sums[:, None, ::2].astype(jnp.float32), 0.0
        ).reshape(16, 2, 64)
        vectors = jnp.pad(
            jnp.concatenate([norm_rows, head_rows], 1), ((0, 0), (0, 9), (0, 64))
        )
        vectors = jnp.broadcast_to(vectors[:, None], (16, 4, 16, 128)).reshape(1024, 128)
        vectors = vectors.astype(LOW)
    with jax.named_scope("block_weight_grads"):
        expand_part = lax.dynamic_slice(
            gathered, (0, 320 + shard // 4 * 64, shard % 4 * 256), (16, 64, 256)
        ).reshape(1024, 256)
        hidden_part = lax.dynamic_slice_in_dim(own_hidden.reshape(4096), shard * 256, 256, 0)
        inner = matmul(first_all, expand_part) + hidden_part
        activation = inner * gelu_share(inner)
        grad_inner = times_transposed(grad_mlp_all, contract_weight[0]) * gelu_slope(inner)
        grad_inner = grad_inner.astype(LOW)
        expand_grad = transposed_times(first_all, grad_inner).astype(LOW)
        contract_grad = transposed_times(activation.astype(LOW), grad_mlp_all).astype(LOW)
        hidden_sum = jnp.sum(grad_inner.astype(jnp.float32), 0)
        mlp_sum = jnp.sum(grad_mlp_all.astype(jnp.float32), 0)
        extra = jnp.concatenate(
            [
                jnp.concatenate([hidden_sum, jnp.zeros((768,), jnp.float32)])[None],
                mlp_sum[None],
                jnp.zeros((14, 1024), jnp.float32),
            ],
            0,
        ).astype(LOW)
        rows = jnp.concatenate(
            [contract_grad.reshape(4, 64, 1024), jnp.broadcast_to(extra, (4, 16, 1024))], 1
        )
    output_got, attend_part, expand_grad, vectors, rows = lax.optimization_barrier(
        (output_got, attend_part, expand_grad, vectors, rows)
    )
    with jax.named_scope("sum_attend_expand_grads"):
        parts = jnp.concatenate([attend_part, expand_grad, vectors], 1)
        got = exchange(parts.reshape(64, 16, 768), REST)
        got, rows = lax.optimization_barrier((got, rows))
    with jax.named_scope("sum_contract"):
        got_contract = exchange(rows, "replica").astype(jnp.float32).sum(0)
    with jax.named_scope("sum_attend_expand_grads"):
        got_output = output_got.astype(jnp.float32).sum(0).astype(LOW)
        got_attend = got[:, :, :384].astype(jnp.float32).reshape(2, 8, 4, 16, 384).sum((0, 2))
        got_expand = got[:, :, 384:640].astype(jnp.float32).reshape(16, 4, 16, 256).sum(1)
        got_expand = got_expand.astype(LOW).transpose(1, 0, 2).reshape(16, 4096)
        got_vectors = got[:, :7, 640:704].astype(jnp.float32).sum(0)
        got_attend, got_output = lax.optimization_barrier((got_attend.astype(LOW), got_output))
        got_attend = got_attend.reshape(8, 16, 2, 3, 64).transpose(1, 3, 2, 0, 4)
        got_attend = got_attend.reshape(16, 3072)
    with jax.named_scope("gather_weight_grads"):
        contract_rows = got_contract[:64].astype(LOW).reshape(4, 16, 1024)
        owned = jnp.concatenate([got_attend, got_output, got_expand, *contract_rows], 1)
    with jax.named_scope("grad_tokens_0"):
        late_packed, owned = lax.optimization_barrier((grad_packed, owned))
        packed_rows = as_rows(send_tokens(late_packed, 3))
        grad_tokens_0 = grad_residual + times_transposed(packed_rows, whole_attend)
    with jax.named_scope("gather_weight_grads"):
        totals = lax.all_gather(owned, "replica", axis=0, tiled=True)
        contract_total = totals[:, 8192:].reshape(4, 16, 4, 1024).transpose(0, 2, 1, 3)
        contract_total = contract_total.reshape(1, 256, 1024).astype(jnp.float32)
        totals = totals[None, :, :8192].astype(jnp.float32)
    input_grad = jnp.where(on_first, grad_tokens_0, grad_tokens_1).reshape(1, 2, 1, 64, 1024)
    mlp_own = lax.dynamic_slice_in_dim(got_contract[65], shard * 64, 64, 0)
    biases_grad = jnp.stack(
        [
            got_vectors[5],
            got_vectors[6],
            got_vectors[2],
            got_vectors[3],
            mlp_own,
            got_vectors[4],
        ]
    )
    return (
        layer_output,
        input_grad,
        totals[:, :, :3072],
        totals[:, :, 3072:4096],
        totals[:, :, 4096:],
        contract_total,
        biases_grad[None],
        got_contract[None, 64, :256],
        got_vectors[None, :2],
    )


def solution(mesh):
    placed = (
        P(None, "replica", "shard", None),
        P(None, "replica", "shard"),
        P(None, "replica", "shard", None),
        P("section", "shard", None),
        P("section", "shard", None),
        P("section", "shard", None),
        P("section", "shard", None),
        P("section", None, "shard"),
        P("section", "shard"),
        P("section", None, "shard"),
    )
    return jax.shard_map(
        on_device,
        mesh=mesh,
        in_specs=placed,
        out_specs=(
            P("section", None, "replica", "shard", None),
            P("section", None, "replica", "shard", None),
            P("section", "shard", None),
            P("section", "shard", None),
            P("section", "shard", None),
            P("section", "shard", None),
            P("section", None, "shard"),
            P("section", "shard"),
            P("section", None, "shard"),
        ),
        check_vma=False,
    )
```

```python
import math

import jax
import jax.numpy as jnp
from jax import lax
from jax.experimental import pallas as pl
from jax.experimental.pallas import tpu as pltpu
from jax.sharding import PartitionSpec as P

HEADS = 16
HEAD_DIM = 64
NEGATIVE = -1e30
EPSILON = 1e-05
SCALE = 1.0 / math.sqrt(HEAD_DIM)
LOW = jnp.bfloat16
ALL = ("section", "shard")
REST = ("shard", "replica")


def matmul(left, right):
    return jnp.dot(left, right, preferred_element_type=jnp.float32)


def times_transposed(left, right):
    return lax.dot_general(
        left, right, (((1,), (1,)), ((), ())), preferred_element_type=jnp.float32
    )


def transposed_times(left, right):
    return lax.dot_general(
        left, right, (((0,), (0,)), ((), ())), preferred_element_type=jnp.float32
    )


def exchange(value, axes):
    return lax.all_to_all(value, axes, 0, 0, tiled=True)


def swap_cores(value):
    return lax.ppermute(value, "shard", [(i, i ^ 1) for i in range(16)])


def whole_sequence(tokens):
    core = lax.axis_index("shard") % 2
    micros, rows, features = tokens.shape
    half = rows // 2
    sends = jnp.broadcast_to(
        tokens.reshape(micros, 1, 2, half, features), (micros, 4, 2, half, features)
    ).reshape(16, half, features)
    mine = exchange(sends, "shard")
    other = swap_cores(mine)
    lower = jnp.where(core == 0, mine, other)
    upper = jnp.where(core == 0, other, mine)
    return jnp.stack([lower, upper], 1).reshape(16 * rows, features)


def send_tokens(value, parts):
    core = lax.axis_index("shard") % 2
    width = parts * HEAD_DIM
    halves = value.reshape(16, 2, 32, width)
    keep = jnp.where(core == 0, halves[:, 0], halves[:, 1])
    take = swap_cores(jnp.where(core == 0, halves[:, 1], halves[:, 0]))
    lower = jnp.split(jnp.where(core == 0, keep, take), parts, 2)
    upper = jnp.split(jnp.where(core == 0, take, keep), parts, 2)
    pair = jnp.concatenate([piece for both in zip(lower, upper) for piece in both], 2)
    sends = jnp.broadcast_to(pair[None], (2, 16, 32, 2 * width)).reshape(32, 32, 2 * width)
    return exchange(sends, ALL).reshape(2, 2, 4, 2, 32, 2 * width)


def masked_scores(queries, keys, seg):
    scores = times_transposed(queries, keys) * SCALE
    return jnp.where(seg[:, None] == seg[None, :], scores, NEGATIVE)


def attend(packed, seg):
    queries, keys, values = jnp.split(packed, 3, 1)
    scores = masked_scores(queries, keys, seg)
    highest = jnp.max(scores, -1, keepdims=True)
    exponent = jnp.exp(scores - highest)
    totals = jnp.sum(exponent, -1, keepdims=True)
    context = matmul((exponent / totals).astype(LOW), values).astype(LOW)
    return context, highest + jnp.log(totals)


def normed(value):
    mean_value = jnp.mean(value, -1, keepdims=True)
    centred = value - mean_value
    spread = jnp.mean(centred * centred, -1, keepdims=True)
    scale = lax.rsqrt(spread + EPSILON)
    return centred * scale, scale


def normed_back(grad, value, gain):
    unit, scale = normed(value)
    weighted = grad * gain
    inner_mean = jnp.mean(weighted * unit, -1, keepdims=True)
    grad_value = scale * (weighted - jnp.mean(weighted, -1, keepdims=True) - unit * inner_mean)
    return (
        grad_value,
        jnp.sum(grad * unit, 0, keepdims=True),
        jnp.sum(grad, 0, keepdims=True),
    )


def gelu_share(value):
    return 0.5 * (1.0 + lax.erf(value * math.sqrt(0.5)))


def gelu_slope(value):
    return gelu_share(value) + value * jnp.exp(-0.5 * value * value) * (0.5 / math.pi) ** 0.5


PARTS = 4
WIDTH = 1024


def this_part(j):
    return jnp.minimum(j, PARTS - 1)


def part_before(j):
    return jnp.maximum(j - 1, 0)


def weight_specs(expand_at, contract_at):
    return [
        pl.BlockSpec((16, 64, 1024), lambda j: (0, 4, 0)),
        pl.BlockSpec((16, 64, WIDTH), lambda j: (0, 5 + expand_at(j), 0)),
        pl.BlockSpec((4, 256, 1024), lambda j: (contract_at(j), 0, 0)),
    ]


def full(*shape):
    return pl.BlockSpec(shape, lambda j: (0,) * len(shape))


ROWS_F32 = jax.ShapeDtypeStruct((128, 1024), jnp.float32)
ROWS_LOW = jax.ShapeDtypeStruct((128, 1024), LOW)
BLOCK_PARAMS = pltpu.CompilerParams(
    dimension_semantics=("arbitrary",), vmem_limit_bytes=48 * 1024 * 1024
)
BLOCK_COST = pl.CostEstimate(
    flops=2 * 128 * 1024 * 9216, bytes_accessed=24 * 1024 * 1024, transcendentals=128 * 4096
)


def forward_kernel(
    tokens,
    context,
    output_weight,
    expand_weight,
    contract_weight,
    params,
    hidden,
    output,
    residual,
    first_low,
    inner,
    second,
    context_rows,
    first,
    total,
    before,
):
    step = pl.program_id(0)

    @pl.when(step == 0)
    def start():
        pairs = [context[s, :, p].reshape(128, 128) for s in range(2) for p in range(4)]
        rows = jnp.concatenate(pairs, 1)
        context_rows[...] = rows
        attention = matmul(rows, output_weight[...].reshape(1024, 1024))
        summed = tokens[...].astype(jnp.float32) + (attention + params[0:1])
        residual[...] = summed
        after = normed(summed)[0] * params[4:5] + params[1:2]
        first[...] = after
        first_low[...] = after.astype(LOW)
        total[...] = jnp.zeros_like(total)
        before[...] = jnp.zeros_like(before)

    last_part = before[...]
    inner_part = matmul(first_low[...], expand_weight[...].reshape(1024, WIDTH)) + hidden[0]
    inner[...] = inner_part
    activation = (last_part * gelu_share(last_part)).astype(LOW)
    total[...] += matmul(activation, contract_weight[...].reshape(WIDTH, 1024))
    before[...] = inner_part

    @pl.when(step == PARTS)
    def finish():
        summed = first[...] + (total[...] + params[2:3])
        second[...] = summed
        output[...] = (normed(summed)[0] * params[5:6] + params[3:4]).astype(LOW)


def block_forward(tokens, context, gathered, params, hidden):
    output, *saved = pl.pallas_call(
        forward_kernel,
        grid=(PARTS + 1,),
        in_specs=[
            full(128, 1024),
            full(2, 2, 4, 2, 32, 128),
            *weight_specs(this_part, part_before),
            full(8, 1024),
            pl.BlockSpec((1, 1, WIDTH), lambda j: (this_part(j), 0, 0)),
        ],
        out_specs=[
            full(128, 1024),
            full(128, 1024),
            full(128, 1024),
            pl.BlockSpec((128, WIDTH), lambda j: (0, this_part(j))),
            full(128, 1024),
            full(128, 1024),
        ],
        out_shape=[
            ROWS_LOW,
            ROWS_F32,
            ROWS_LOW,
            jax.ShapeDtypeStruct((128, 4096), jnp.float32),
            ROWS_F32,
            ROWS_LOW,
        ],
        scratch_shapes=[
            pltpu.VMEM((128, 1024), jnp.float32),
            pltpu.VMEM((128, 1024), jnp.float32),
            pltpu.VMEM((128, WIDTH), jnp.float32),
        ],
        compiler_params=BLOCK_PARAMS,
        cost_estimate=BLOCK_COST,
    )(tokens, context, gathered, gathered, gathered, params, hidden)
    return output, saved


def backward_kernel(
    grad,
    output_weight,
    expand_weight,
    contract_weight,
    params,
    residual,
    inner,
    second,
    grad_residual,
    grad_attn,
    grad_context,
    sums,
    grad_mlp,
    grad_second,
    total,
    before,
):
    step = pl.program_id(0)

    @pl.when(step == 0)
    def start():
        by_value, by_gain, by_shift = normed_back(
            grad[...].astype(jnp.float32), second[...], params[5:6]
        )
        grad_second[...] = by_value
        grad_mlp[...] = by_value.astype(LOW)
        sums[1:2] = by_gain
        sums[4:5] = by_shift
        total[...] = jnp.zeros_like(total)
        before[...] = jnp.zeros_like(before)

    last_part = before[...]
    before[...] = times_transposed(grad_mlp[...], contract_weight[...].reshape(WIDTH, 1024))
    grad_inner = (last_part * gelu_slope(inner[...])).astype(LOW)
    total[...] += times_transposed(grad_inner, expand_weight[...].reshape(1024, WIDTH))

    @pl.when(step == PARTS)
    def finish():
        by_value, by_gain, by_shift = normed_back(
            grad_second[...] + total[...], residual[...], params[4:5]
        )
        grad_residual[...] = by_value
        rounded = by_value.astype(LOW)
        grad_attn[...] = rounded
        rows = times_transposed(rounded, output_weight[...].reshape(1024, 1024)).astype(LOW)
        for s, m, p in ((s, m, p) for s in range(2) for m in range(2) for p in range(4)):
            piece = rows[64 * m : 64 * m + 64, 128 * (4 * s + p) : 128 * (4 * s + p) + 128]
            grad_context[s, m, p, 0] = piece
            grad_context[s, m, p, 1] = piece
        sums[0:1] = by_gain
        sums[2:3] = jnp.sum(rounded.astype(jnp.float32), 0, keepdims=True)
        sums[3:4] = by_shift
        sums[5:8] = jnp.zeros((3, 1024), jnp.float32)


def block_back(grad, saved, gathered, params):
    residual, first_low, inner, second, context_rows = saved
    return pl.pallas_call(
        backward_kernel,
        grid=(PARTS + 1,),
        in_specs=[
            full(128, 1024),
            *weight_specs(part_before, this_part),
            full(8, 1024),
            full(128, 1024),
            pl.BlockSpec((128, WIDTH), lambda j: (0, part_before(j))),
            full(128, 1024),
        ],
        out_specs=[
            full(128, 1024),
            full(128, 1024),
            full(2, 2, 4, 2, 64, 128),
            full(8, 1024),
        ],
        out_shape=[
            ROWS_F32,
            ROWS_LOW,
            jax.ShapeDtypeStruct((2, 2, 4, 2, 64, 128), LOW),
            jax.ShapeDtypeStruct((8, 1024), jnp.float32),
        ],
        scratch_shapes=[
            pltpu.VMEM((128, 1024), LOW),
            pltpu.VMEM((128, 1024), jnp.float32),
            pltpu.VMEM((128, 1024), jnp.float32),
            pltpu.VMEM((128, WIDTH), jnp.float32),
        ],
        compiler_params=BLOCK_PARAMS,
        cost_estimate=BLOCK_COST,
    )(grad, gathered, gathered, gathered, params, residual, inner, second)


def grad_tokens_kernel(got, weight, grad_residual, result, rounded, total):
    step = pl.program_id(0)
    left = jnp.concatenate([got[0, :, p].reshape(128, 384) for p in range(2)], 1)
    product = times_transposed(left, weight[...])

    @pl.when(step == 0)
    def start():
        total[...] = grad_residual[...] + product

    @pl.when(step > 0)
    def proceed():
        total[...] += product

    @pl.when(step == 3)
    def finish():
        result[...] = total[...]
        rounded[...] = total[...].astype(LOW)


def grad_tokens(got, weight, grad_residual):
    return pl.pallas_call(
        grad_tokens_kernel,
        grid=(4,),
        in_specs=[
            pl.BlockSpec((1, 2, 2, 2, 32, 384), lambda i: (i // 2, 0, i % 2, 0, 0, 0)),
            pl.BlockSpec((1024, 768), lambda i: (0, i)),
            full(128, 1024),
        ],
        out_specs=[full(128, 1024), full(128, 1024)],
        out_shape=[ROWS_F32, ROWS_LOW],
        scratch_shapes=[pltpu.VMEM((128, 1024), jnp.float32)],
        compiler_params=BLOCK_PARAMS,
        cost_estimate=pl.CostEstimate(
            flops=2 * 128 * 3072 * 1024, bytes_accessed=8 * 1024 * 1024, transcendentals=0
        ),
    )(got, weight, grad_residual)


def attend_back_kernel(
    core,
    packed,
    log_totals,
    seg_rows,
    seg_columns,
    got,
    result,
    queries,
    keys,
    values,
    grads,
    grad_keys,
    grad_values,
):
    step = pl.program_id(0)

    @pl.when(step == 0)
    def start():
        queries[...] = packed[:, :HEAD_DIM]
        keys[...] = packed[:, HEAD_DIM : 2 * HEAD_DIM]
        values[...] = packed[:, 2 * HEAD_DIM :]
        pair = got[...].reshape(1024, 128)
        grads[...] = jnp.where(core[0] == 0, pair[:, :HEAD_DIM], pair[:, HEAD_DIM:])
        grad_keys[...] = jnp.zeros_like(grad_keys)
        grad_values[...] = jnp.zeros_like(grad_values)

    rows = pl.ds(pl.multiple_of(step * 256, 256), 256)
    block_queries = queries[rows]
    block_grads = grads[rows]
    scores = times_transposed(block_queries, keys[...]) * SCALE
    scores = jnp.where(seg_rows[rows] == seg_columns[...], scores, NEGATIVE)
    soft = jnp.exp(scores - log_totals[rows])
    grad_soft = times_transposed(block_grads, values[...])
    row_total = jnp.sum(soft * grad_soft, -1, keepdims=True)
    grad_scores = (soft * (grad_soft - row_total)).astype(LOW)
    result[rows, :HEAD_DIM] = (matmul(grad_scores, keys[...]) * SCALE).astype(LOW)
    grad_keys[...] += transposed_times(grad_scores, block_queries)
    grad_values[...] += transposed_times(soft.astype(LOW), block_grads)

    @pl.when(step == 3)
    def finish():
        result[:, HEAD_DIM : 2 * HEAD_DIM] = (grad_keys[...] * SCALE).astype(LOW)
        result[:, 2 * HEAD_DIM :] = grad_values[...].astype(LOW)


def attend_back(core, packed, log_totals, seg, got, layer):
    return pl.pallas_call(
        attend_back_kernel,
        grid=(4,),
        in_specs=[
            pl.BlockSpec(memory_space=pltpu.SMEM),
            full(1024, 192),
            full(1024, 1),
            full(1024, 1),
            full(1, 1024),
            pl.BlockSpec((16, 64, 128), lambda i: (layer, 0, 0)),
        ],
        out_specs=full(1024, 192),
        out_shape=jax.ShapeDtypeStruct((1024, 192), LOW),
        scratch_shapes=[pltpu.VMEM((1024, HEAD_DIM), LOW)] * 4
        + [pltpu.VMEM((1024, HEAD_DIM), jnp.float32)] * 2,
        compiler_params=BLOCK_PARAMS,
        cost_estimate=pl.CostEstimate(
            flops=10 * 1024 * 1024 * 64, bytes_accessed=2 * 1024 * 1024, transcendentals=1 << 20
        ),
    )(core, packed, log_totals, seg[:, None], seg[None, :], got)


def with_sums(grad, sums):
    rows = jnp.concatenate([sums[None], jnp.zeros((15, sums.shape[0]), jnp.float32)], 0)
    return jnp.concatenate([grad.astype(LOW), rows.astype(LOW)], 0)


def on_device(
    inputs,
    segments,
    cotangent,
    attend_weight,
    output_weight,
    expand_weight,
    contract_weight,
    biases,
    hidden_bias,
    gains,
):
    section = lax.axis_index("section")
    shard = lax.axis_index("shard")
    on_first = section == 0
    micro = shard // 8
    head = section * 8 + shard % 8
    inputs = inputs[:, 0]

    with jax.named_scope("gather_block_weights"):
        rows = jnp.concatenate(
            [contract_weight[0], output_weight[0]] + jnp.split(expand_weight[0], 4, 1), 0
        )
        quarter = lax.dynamic_slice_in_dim(rows, lax.axis_index("replica") * 144, 144, 0)
        gathered = lax.all_gather(quarter, REST, axis=0, tiled=False).reshape(16, 576, 1024)

    with jax.named_scope("head_weights"):
        by_head = attend_weight[0].reshape(64, 3, HEADS, HEAD_DIM).transpose(2, 0, 1, 3)
        small = jnp.concatenate(
            [
                biases.reshape(384),
                gains.reshape(128),
                hidden_bias.reshape(256),
                segments.reshape(128).astype(LOW),
                jnp.zeros((16 * 192 - 896,), LOW),
            ]
        ).reshape(1, 16, 192)
        block = jnp.concatenate(
            [by_head.reshape(HEADS, 64, 192), jnp.broadcast_to(small, (HEADS, 16, 192))], 1
        )
        block = jnp.broadcast_to(block.reshape(2, 1, 8, 80, 192), (2, 2, 8, 80, 192))
        got = exchange(block.reshape(32, 80, 192), ALL).reshape(2, 16, 80, 192)
        head_weight = got[:, :, :64].reshape(2, 1024, 192)
        small = got[:, :, 64:69].reshape(2, 16, 960)
        all_biases = small[:, :, :384].reshape(2, 16, 6, 64).transpose(0, 2, 1, 3)
        all_biases = all_biases.reshape(2, 6, 1024).astype(jnp.float32)
        all_gains = small[:, :, 384:512].reshape(2, 16, 2, 64).transpose(0, 2, 1, 3)
        all_gains = all_gains.reshape(2, 2, 1024).astype(jnp.float32)
        all_hidden = small[:, :, 512:768].reshape(2, 4096).astype(jnp.float32)
        seg = small[0, :, 768:896].reshape(16, 2, 64)
        seg = jnp.where(micro == 0, seg[:, 0], seg[:, 1]).reshape(1024)
        own_biases = jnp.where(on_first, all_biases[0], all_biases[1])
        own_gains = jnp.where(on_first, all_gains[0], all_gains[1])
        own_hidden = jnp.where(on_first, all_hidden[0], all_hidden[1]).reshape(PARTS, 1, WIDTH)
        params = jnp.concatenate([own_biases[2:], own_gains, jnp.zeros((2, 1024))], 0)
        head_bias = lax.dynamic_slice_in_dim(
            all_biases.reshape(2, 6, HEADS, HEAD_DIM), head, 1, 2
        )[:, :, 0]
        head_bias = jnp.concatenate(
            [head_bias[:, 0], jnp.zeros_like(head_bias[:, 0]), head_bias[:, 1]], 1
        )

    def attention(layer, tokens):
        with jax.named_scope("sequence_tokens"):
            whole = whole_sequence(tokens)
        with jax.named_scope("attention"):
            packed = (matmul(whole, head_weight[layer]) + head_bias[layer]).astype(LOW)
            context, log_totals = attend(packed, seg)
        with jax.named_scope("context_out"):
            context = send_tokens(context, 1)
        return context, (whole, packed, log_totals)

    def attention_back(layer, grad_context, kept):
        whole, packed, log_totals = kept
        with jax.named_scope("grad_context_in"):
            got = exchange(grad_context.reshape(32, 64, 128), ALL)
        with jax.named_scope("attention_back"):
            core = (shard % 2).astype(jnp.int32).reshape(1)
            grad_packed = attend_back(core, packed, log_totals, seg, got, layer)
            grad_weight = transposed_times(whole, grad_packed)
            grad_sums = jnp.sum(grad_packed.astype(jnp.float32), 0)
        return grad_packed, grad_weight, grad_sums

    context_0, kept_0 = attention(0, inputs)
    tokens_0 = inputs.reshape(128, 1024)
    with jax.named_scope("block_0"):
        output, unused = block_forward(tokens_0, context_0, gathered, params, own_hidden)
    with jax.named_scope("to_next_section"):
        tokens_1 = jnp.where(
            on_first, output, lax.ppermute(output, "section", [(0, 1)])
        )
    with jax.named_scope("gather_attend_weight"):
        by_pair = attend_weight[0].reshape(64, 3, 8, 128).transpose(0, 2, 1, 3).reshape(64, 3072)
        late_weight, unused = lax.optimization_barrier((by_pair, output))
        whole_attend = lax.all_gather(late_weight, "shard", axis=0, tiled=True)
    context_1, kept_1 = attention(1, tokens_1.reshape(2, 64, 1024))
    own_tokens = jnp.where(on_first, tokens_0, tokens_1)
    own_context = jnp.where(on_first, context_0, context_1)
    with jax.named_scope("block_1"):
        output, saved = block_forward(own_tokens, own_context, gathered, params, own_hidden)
    layer_output = output.reshape(1, 2, 1, 64, 1024)
    with jax.named_scope("gather_first"):
        first_all = lax.all_gather(saved[1], "shard", axis=0, tiled=True)

    last_grad = cotangent.reshape(128, 1024)
    with jax.named_scope("block_back_1"):
        grad_residual, unused, grad_context, unused = block_back(
            last_grad, saved, gathered, params
        )
    grad_packed, grad_attend_1, grad_sums_1 = attention_back(1, grad_context, kept_1)
    with jax.named_scope("swap_attend_grad"):
        part_1 = with_sums(grad_attend_1, grad_sums_1)
        take_1 = lax.ppermute(part_1, "section", [(0, 1)])
    with jax.named_scope("grad_tokens_1"):
        grad_tokens_1, rounded = grad_tokens(
            send_tokens(grad_packed, 3), whole_attend, grad_residual
        )
    with jax.named_scope("to_previous_section"):
        arrived = lax.ppermute(rounded, "section", [(1, 0)])
        own_grad = jnp.where(on_first, arrived, last_grad)
    with jax.named_scope("gather_grad_mlp"):
        grad_mlp = normed_back(own_grad.astype(jnp.float32), saved[3], params[5:6])[0].astype(LOW)
        grad_mlp, own_grad = lax.optimization_barrier((grad_mlp, own_grad))
        grad_mlp_all = lax.all_gather(grad_mlp, "shard", axis=0, tiled=True)
    with jax.named_scope("block_back_0"):
        grad_residual, grad_attn, grad_context, norm_sums = block_back(
            own_grad, saved, gathered, params
        )
    grad_packed, grad_attend_0, grad_sums_0 = attention_back(0, grad_context, kept_0)

    with jax.named_scope("sum_output_grad"):
        output_grad = transposed_times(saved[4], grad_attn).astype(LOW)
        output_got = exchange(output_grad.reshape(64, 16, 1024), REST)
    with jax.named_scope("swap_attend_grad"):
        part_0 = with_sums(grad_attend_0, grad_sums_0)
        take_0 = lax.ppermute(part_0, "section", [(1, 0)])
        lower = jnp.where(on_first, part_0, take_1)
        upper = jnp.where(on_first, take_0, part_1)
        attend_part = jnp.concatenate([lower[:1024], upper[:1024]], 1)
        sums = jnp.stack([lower[1024], upper[1024]]).reshape(2, 3, HEAD_DIM)
        norm_rows = norm_sums[:5].reshape(5, 16, 64).transpose(1, 0, 2)
        mine = jnp.arange(8) == shard % 8
        head_rows = jnp.where(
            mine[None, :, None, None], sums[:, None, ::2].astype(jnp.float32), 0.0
        ).reshape(16, 2, 64)
        vectors = jnp.pad(
            jnp.concatenate([norm_rows, head_rows], 1), ((0, 0), (0, 9), (0, 64))
        )
        vectors = jnp.broadcast_to(vectors[:, None], (16, 4, 16, 128)).reshape(1024, 128)
        vectors = vectors.astype(LOW)
    with jax.named_scope("sum_attend_grad"):
        parts = jnp.concatenate([attend_part, vectors], 1)
        output_got, parts = lax.optimization_barrier((output_got, parts))
        got = exchange(parts.reshape(64, 16, 512), REST)
    with jax.named_scope("block_weight_grads"):
        expand_part = lax.dynamic_slice(
            gathered, (0, 320 + shard // 4 * 64, shard % 4 * 256), (16, 64, 256)
        ).reshape(1024, 256)
        hidden_part = lax.dynamic_slice_in_dim(own_hidden.reshape(4096), shard * 256, 256, 0)
        inner = matmul(first_all, expand_part) + hidden_part
        activation = inner * gelu_share(inner)
        grad_inner = times_transposed(grad_mlp_all, contract_weight[0]) * gelu_slope(inner)
        grad_inner = grad_inner.astype(LOW)
        expand_grad = transposed_times(first_all, grad_inner).astype(LOW)
        contract_grad = transposed_times(activation.astype(LOW), grad_mlp_all).astype(LOW)
        hidden_sum = jnp.sum(grad_inner.astype(jnp.float32), 0)
        mlp_sum = jnp.sum(grad_mlp_all.astype(jnp.float32), 0)
        extra = jnp.concatenate(
            [
                jnp.concatenate([hidden_sum, jnp.zeros((768,), jnp.float32)])[None],
                mlp_sum[None],
                jnp.zeros((14, 1024), jnp.float32),
            ],
            0,
        ).astype(LOW)
        rows = jnp.concatenate(
            [contract_grad.reshape(4, 64, 1024), jnp.broadcast_to(extra, (4, 16, 1024))], 1
        )
    with jax.named_scope("sum_expand_grad"):
        got, expand_grad, rows = lax.optimization_barrier((got, expand_grad, rows))
        expand_got = exchange(expand_grad.reshape(64, 16, 256), REST)
        expand_got, rows = lax.optimization_barrier((expand_got, rows))
    with jax.named_scope("sum_contract"):
        got_contract = exchange(rows, "replica").astype(jnp.float32).sum(0)
    with jax.named_scope("sum_attend_grad"):
        got_output = output_got.astype(jnp.float32).sum(0).astype(LOW)
        got_attend = got[:, :, :384].astype(jnp.float32).reshape(2, 8, 4, 16, 384).sum((0, 2))
        got_expand = expand_got.astype(jnp.float32).reshape(16, 4, 16, 256).sum(1)
        got_expand = got_expand.astype(LOW).transpose(1, 0, 2).reshape(16, 4096)
        got_vectors = got[:, :7, 384:448].astype(jnp.float32).sum(0)
        got_attend, got_output = lax.optimization_barrier((got_attend.astype(LOW), got_output))
        got_attend = got_attend.reshape(8, 16, 2, 3, 64).transpose(1, 3, 2, 0, 4)
        got_attend = got_attend.reshape(16, 3072)
    with jax.named_scope("gather_weight_grads"):
        contract_rows = got_contract[:64].astype(LOW).reshape(4, 16, 1024)
        owned = jnp.concatenate([got_attend, got_output, got_expand, *contract_rows], 1)
    with jax.named_scope("grad_tokens_0"):
        late_packed, owned = lax.optimization_barrier((grad_packed, owned))
        grad_tokens_0, unused = grad_tokens(
            send_tokens(late_packed, 3), whole_attend, grad_residual
        )
    with jax.named_scope("gather_weight_grads"):
        totals = lax.all_gather(owned, "replica", axis=0, tiled=True)
        contract_total = totals[:, 8192:].reshape(4, 16, 4, 1024).transpose(0, 2, 1, 3)
        contract_total = contract_total.reshape(1, 256, 1024).astype(jnp.float32)
        totals = totals[None, :, :8192].astype(jnp.float32)
    input_grad = jnp.where(on_first, grad_tokens_0, grad_tokens_1).reshape(1, 2, 1, 64, 1024)
    mlp_own = lax.dynamic_slice_in_dim(got_contract[65], shard * 64, 64, 0)
    biases_grad = jnp.stack(
        [
            got_vectors[5],
            got_vectors[6],
            got_vectors[2],
            got_vectors[3],
            mlp_own,
            got_vectors[4],
        ]
    )
    return (
        layer_output,
        input_grad,
        totals[:, :, :3072],
        totals[:, :, 3072:4096],
        totals[:, :, 4096:],
        contract_total,
        biases_grad[None],
        got_contract[None, 64, :256],
        got_vectors[None, :2],
    )


def solution(mesh):
    placed = (
        P(None, "replica", "shard", None),
        P(None, "replica", "shard"),
        P(None, "replica", "shard", None),
        P("section", "shard", None),
        P("section", "shard", None),
        P("section", "shard", None),
        P("section", "shard", None),
        P("section", None, "shard"),
        P("section", "shard"),
        P("section", None, "shard"),
    )
    return jax.shard_map(
        on_device,
        mesh=mesh,
        in_specs=placed,
        out_specs=(
            P("section", None, "replica", "shard", None),
            P("section", None, "replica", "shard", None),
            P("section", "shard", None),
            P("section", "shard", None),
            P("section", "shard", None),
            P("section", "shard", None),
            P("section", None, "shard"),
            P("section", "shard"),
            P("section", None, "shard"),
        ),
        check_vma=False,
    )
```

```python
import math

import jax
import jax.numpy as jnp
from jax import lax
from jax.experimental import pallas as pl
from jax.experimental.pallas import tpu as pltpu
from jax.sharding import PartitionSpec as P

HEADS = 16
HEAD_DIM = 64
NEGATIVE = -1e30
EPSILON = 1e-05
SCALE = 1.0 / math.sqrt(HEAD_DIM)
LOW = jnp.bfloat16
ALL = ("section", "shard")
REST = ("shard", "replica")


def matmul(left, right):
    return jnp.dot(left, right, preferred_element_type=jnp.float32)


def times_transposed(left, right):
    return lax.dot_general(
        left, right, (((1,), (1,)), ((), ())), preferred_element_type=jnp.float32
    )


def transposed_times(left, right):
    return lax.dot_general(
        left, right, (((0,), (0,)), ((), ())), preferred_element_type=jnp.float32
    )


def exchange(value, axes):
    return lax.all_to_all(value, axes, 0, 0, tiled=True)


def swap_cores(value):
    return lax.ppermute(value, "shard", [(i, i ^ 1) for i in range(16)])


def whole_sequence(tokens):
    core = lax.axis_index("shard") % 2
    micros, rows, features = tokens.shape
    half = rows // 2
    sends = jnp.broadcast_to(
        tokens.reshape(micros, 1, 2, half, features), (micros, 4, 2, half, features)
    ).reshape(16, half, features)
    mine = exchange(sends, "shard")
    other = swap_cores(mine)
    lower = jnp.where(core == 0, mine, other)
    upper = jnp.where(core == 0, other, mine)
    return jnp.stack([lower, upper], 1).reshape(16 * rows, features)


def send_tokens(value, parts):
    core = lax.axis_index("shard") % 2
    width = parts * HEAD_DIM
    halves = value.reshape(16, 2, 32, width)
    keep = jnp.where(core == 0, halves[:, 0], halves[:, 1])
    take = swap_cores(jnp.where(core == 0, halves[:, 1], halves[:, 0]))
    lower = jnp.split(jnp.where(core == 0, keep, take), parts, 2)
    upper = jnp.split(jnp.where(core == 0, take, keep), parts, 2)
    pair = jnp.concatenate([piece for both in zip(lower, upper) for piece in both], 2)
    sends = jnp.broadcast_to(pair[None], (2, 16, 32, 2 * width)).reshape(32, 32, 2 * width)
    return exchange(sends, ALL).reshape(2, 2, 4, 2, 32, 2 * width)


def masked_scores(queries, keys, seg):
    scores = times_transposed(queries, keys) * SCALE
    return jnp.where(seg[:, None] == seg[None, :], scores, NEGATIVE)


def attend(packed, seg):
    queries, keys, values = jnp.split(packed, 3, 1)
    scores = masked_scores(queries, keys, seg)
    highest = jnp.max(scores, -1, keepdims=True)
    exponent = jnp.exp(scores - highest)
    totals = jnp.sum(exponent, -1, keepdims=True)
    context = matmul((exponent / totals).astype(LOW), values).astype(LOW)
    return context, highest + jnp.log(totals)


def normed(value):
    mean_value = jnp.mean(value, -1, keepdims=True)
    centred = value - mean_value
    spread = jnp.mean(centred * centred, -1, keepdims=True)
    scale = lax.rsqrt(spread + EPSILON)
    return centred * scale, scale


def normed_back(grad, value, gain):
    unit, scale = normed(value)
    weighted = grad * gain
    inner_mean = jnp.mean(weighted * unit, -1, keepdims=True)
    grad_value = scale * (weighted - jnp.mean(weighted, -1, keepdims=True) - unit * inner_mean)
    return (
        grad_value,
        jnp.sum(grad * unit, 0, keepdims=True),
        jnp.sum(grad, 0, keepdims=True),
    )


def gelu_share(value):
    return 0.5 * (1.0 + lax.erf(value * math.sqrt(0.5)))


def gelu_slope(value):
    return gelu_share(value) + value * jnp.exp(-0.5 * value * value) * (0.5 / math.pi) ** 0.5


PARTS = 4
WIDTH = 1024


def this_part(j):
    return jnp.minimum(j, PARTS - 1)


def part_before(j):
    return jnp.maximum(j - 1, 0)


def weight_specs(expand_at, contract_at):
    return [
        pl.BlockSpec((16, 64, 1024), lambda j: (0, 4, 0)),
        pl.BlockSpec((16, 64, WIDTH), lambda j: (0, 5 + expand_at(j), 0)),
        pl.BlockSpec((4, 256, 1024), lambda j: (contract_at(j), 0, 0)),
    ]


def full(*shape):
    return pl.BlockSpec(shape, lambda j: (0,) * len(shape))


ROWS_F32 = jax.ShapeDtypeStruct((128, 1024), jnp.float32)
ROWS_LOW = jax.ShapeDtypeStruct((128, 1024), LOW)
BLOCK_PARAMS = pltpu.CompilerParams(
    dimension_semantics=("arbitrary",), vmem_limit_bytes=48 * 1024 * 1024
)
BLOCK_COST = pl.CostEstimate(
    flops=2 * 128 * 1024 * 9216, bytes_accessed=24 * 1024 * 1024, transcendentals=128 * 4096
)


def forward_kernel(
    tokens,
    context,
    output_weight,
    expand_weight,
    contract_weight,
    params,
    hidden,
    output,
    residual,
    first_low,
    inner,
    second,
    context_rows,
    first,
    total,
    before,
):
    step = pl.program_id(0)

    @pl.when(step == 0)
    def start():
        pairs = [context[s, :, p].reshape(128, 128) for s in range(2) for p in range(4)]
        rows = jnp.concatenate(pairs, 1)
        context_rows[...] = rows
        attention = matmul(rows, output_weight[...].reshape(1024, 1024))
        summed = tokens[...].astype(jnp.float32) + (attention + params[0:1])
        residual[...] = summed
        after = normed(summed)[0] * params[4:5] + params[1:2]
        first[...] = after
        first_low[...] = after.astype(LOW)
        total[...] = jnp.zeros_like(total)
        before[...] = jnp.zeros_like(before)

    last_part = before[...]
    inner_part = matmul(first_low[...], expand_weight[...].reshape(1024, WIDTH)) + hidden[0]
    inner[...] = inner_part
    activation = (last_part * gelu_share(last_part)).astype(LOW)
    total[...] += matmul(activation, contract_weight[...].reshape(WIDTH, 1024))
    before[...] = inner_part

    @pl.when(step == PARTS)
    def finish():
        summed = first[...] + (total[...] + params[2:3])
        second[...] = summed
        output[...] = (normed(summed)[0] * params[5:6] + params[3:4]).astype(LOW)


def block_forward(tokens, context, gathered, params, hidden):
    output, *saved = pl.pallas_call(
        forward_kernel,
        grid=(PARTS + 1,),
        in_specs=[
            full(128, 1024),
            full(2, 2, 4, 2, 32, 128),
            *weight_specs(this_part, part_before),
            full(8, 1024),
            pl.BlockSpec((1, 1, WIDTH), lambda j: (this_part(j), 0, 0)),
        ],
        out_specs=[
            full(128, 1024),
            full(128, 1024),
            full(128, 1024),
            pl.BlockSpec((128, WIDTH), lambda j: (0, this_part(j))),
            full(128, 1024),
            full(128, 1024),
        ],
        out_shape=[
            ROWS_LOW,
            ROWS_F32,
            ROWS_LOW,
            jax.ShapeDtypeStruct((128, 4096), jnp.float32),
            ROWS_F32,
            ROWS_LOW,
        ],
        scratch_shapes=[
            pltpu.VMEM((128, 1024), jnp.float32),
            pltpu.VMEM((128, 1024), jnp.float32),
            pltpu.VMEM((128, WIDTH), jnp.float32),
        ],
        compiler_params=BLOCK_PARAMS,
        cost_estimate=BLOCK_COST,
    )(tokens, context, gathered, gathered, gathered, params, hidden)
    return output, saved


def backward_kernel(
    grad,
    output_weight,
    expand_weight,
    contract_weight,
    params,
    residual,
    inner,
    second,
    grad_residual,
    grad_attn,
    grad_context,
    sums,
    grad_mlp,
    grad_second,
    total,
    before,
):
    step = pl.program_id(0)

    @pl.when(step == 0)
    def start():
        by_value, by_gain, by_shift = normed_back(
            grad[...].astype(jnp.float32), second[...], params[5:6]
        )
        grad_second[...] = by_value
        grad_mlp[...] = by_value.astype(LOW)
        sums[1:2] = by_gain
        sums[4:5] = by_shift
        total[...] = jnp.zeros_like(total)
        before[...] = jnp.zeros_like(before)

    last_part = before[...]
    before[...] = times_transposed(grad_mlp[...], contract_weight[...].reshape(WIDTH, 1024))
    grad_inner = (last_part * gelu_slope(inner[...])).astype(LOW)
    total[...] += times_transposed(grad_inner, expand_weight[...].reshape(1024, WIDTH))

    @pl.when(step == PARTS)
    def finish():
        by_value, by_gain, by_shift = normed_back(
            grad_second[...] + total[...], residual[...], params[4:5]
        )
        grad_residual[...] = by_value
        rounded = by_value.astype(LOW)
        grad_attn[...] = rounded
        rows = times_transposed(rounded, output_weight[...].reshape(1024, 1024)).astype(LOW)
        for s, m, p in ((s, m, p) for s in range(2) for m in range(2) for p in range(4)):
            piece = rows[64 * m : 64 * m + 64, 128 * (4 * s + p) : 128 * (4 * s + p) + 128]
            grad_context[s, m, p, 0] = piece
            grad_context[s, m, p, 1] = piece
        sums[0:1] = by_gain
        sums[2:3] = jnp.sum(rounded.astype(jnp.float32), 0, keepdims=True)
        sums[3:4] = by_shift
        sums[5:8] = jnp.zeros((3, 1024), jnp.float32)


def block_back(grad, saved, gathered, params):
    residual, first_low, inner, second, context_rows = saved
    return pl.pallas_call(
        backward_kernel,
        grid=(PARTS + 1,),
        in_specs=[
            full(128, 1024),
            *weight_specs(part_before, this_part),
            full(8, 1024),
            full(128, 1024),
            pl.BlockSpec((128, WIDTH), lambda j: (0, part_before(j))),
            full(128, 1024),
        ],
        out_specs=[
            full(128, 1024),
            full(128, 1024),
            full(2, 2, 4, 2, 64, 128),
            full(8, 1024),
        ],
        out_shape=[
            ROWS_F32,
            ROWS_LOW,
            jax.ShapeDtypeStruct((2, 2, 4, 2, 64, 128), LOW),
            jax.ShapeDtypeStruct((8, 1024), jnp.float32),
        ],
        scratch_shapes=[
            pltpu.VMEM((128, 1024), LOW),
            pltpu.VMEM((128, 1024), jnp.float32),
            pltpu.VMEM((128, 1024), jnp.float32),
            pltpu.VMEM((128, WIDTH), jnp.float32),
        ],
        compiler_params=BLOCK_PARAMS,
        cost_estimate=BLOCK_COST,
    )(grad, gathered, gathered, gathered, params, residual, inner, second)


def grad_tokens_kernel(got, weight, grad_residual, result, rounded, total):
    step = pl.program_id(0)
    left = jnp.concatenate([got[0, :, p].reshape(128, 384) for p in range(2)], 1)
    product = times_transposed(left, weight[...].reshape(1024, 768))

    @pl.when(step == 0)
    def start():
        total[...] = grad_residual[...] + product

    @pl.when(step > 0)
    def proceed():
        total[...] += product

    @pl.when(step == 3)
    def finish():
        result[...] = total[...]
        rounded[...] = total[...].astype(LOW)


def grad_tokens(layer, got, weight, grad_residual):
    return pl.pallas_call(
        grad_tokens_kernel,
        grid=(4,),
        in_specs=[
            pl.BlockSpec((1, 2, 2, 2, 32, 384), lambda i: (i // 2, 0, i % 2, 0, 0, 0)),
            pl.BlockSpec((16, 64, 768), lambda i: (0, layer, i)),
            full(128, 1024),
        ],
        out_specs=[full(128, 1024), full(128, 1024)],
        out_shape=[ROWS_F32, ROWS_LOW],
        scratch_shapes=[pltpu.VMEM((128, 1024), jnp.float32)],
        compiler_params=BLOCK_PARAMS,
        cost_estimate=pl.CostEstimate(
            flops=2 * 128 * 3072 * 1024, bytes_accessed=8 * 1024 * 1024, transcendentals=0
        ),
    )(got, weight, grad_residual)


def attend_back_kernel(
    core,
    packed,
    log_totals,
    seg_rows,
    seg_columns,
    got,
    result,
    queries,
    keys,
    values,
    grads,
    grad_keys,
    grad_values,
):
    step = pl.program_id(0)

    @pl.when(step == 0)
    def start():
        queries[...] = packed[:, :HEAD_DIM]
        keys[...] = packed[:, HEAD_DIM : 2 * HEAD_DIM]
        values[...] = packed[:, 2 * HEAD_DIM :]
        pair = got[...].reshape(1024, 128)
        grads[...] = jnp.where(core[0] == 0, pair[:, :HEAD_DIM], pair[:, HEAD_DIM:])
        grad_keys[...] = jnp.zeros_like(grad_keys)
        grad_values[...] = jnp.zeros_like(grad_values)

    rows = pl.ds(pl.multiple_of(step * 256, 256), 256)
    block_queries = queries[rows]
    block_grads = grads[rows]
    scores = times_transposed(block_queries, keys[...]) * SCALE
    scores = jnp.where(seg_rows[rows] == seg_columns[...], scores, NEGATIVE)
    soft = jnp.exp(scores - log_totals[rows])
    grad_soft = times_transposed(block_grads, values[...])
    row_total = jnp.sum(soft * grad_soft, -1, keepdims=True)
    grad_scores = (soft * (grad_soft - row_total)).astype(LOW)
    result[rows, :HEAD_DIM] = (matmul(grad_scores, keys[...]) * SCALE).astype(LOW)
    grad_keys[...] += transposed_times(grad_scores, block_queries)
    grad_values[...] += transposed_times(soft.astype(LOW), block_grads)

    @pl.when(step == 3)
    def finish():
        result[:, HEAD_DIM : 2 * HEAD_DIM] = (grad_keys[...] * SCALE).astype(LOW)
        result[:, 2 * HEAD_DIM :] = grad_values[...].astype(LOW)


def attend_back(core, packed, log_totals, seg, got, layer):
    return pl.pallas_call(
        attend_back_kernel,
        grid=(4,),
        in_specs=[
            pl.BlockSpec(memory_space=pltpu.SMEM),
            full(1024, 192),
            full(1024, 1),
            full(1024, 1),
            full(1, 1024),
            pl.BlockSpec((16, 64, 128), lambda i: (layer, 0, 0)),
        ],
        out_specs=full(1024, 192),
        out_shape=jax.ShapeDtypeStruct((1024, 192), LOW),
        scratch_shapes=[pltpu.VMEM((1024, HEAD_DIM), LOW)] * 4
        + [pltpu.VMEM((1024, HEAD_DIM), jnp.float32)] * 2,
        compiler_params=BLOCK_PARAMS,
        cost_estimate=pl.CostEstimate(
            flops=10 * 1024 * 1024 * 64, bytes_accessed=2 * 1024 * 1024, transcendentals=1 << 20
        ),
    )(core, packed, log_totals, seg[:, None], seg[None, :], got)


def with_sums(grad, sums):
    rows = jnp.concatenate([sums[None], jnp.zeros((15, sums.shape[0]), jnp.float32)], 0)
    return jnp.concatenate([grad.astype(LOW), rows.astype(LOW)], 0)


def on_device(
    inputs,
    segments,
    cotangent,
    attend_weight,
    output_weight,
    expand_weight,
    contract_weight,
    biases,
    hidden_bias,
    gains,
):
    section = lax.axis_index("section")
    shard = lax.axis_index("shard")
    on_first = section == 0
    micro = shard // 8
    head = section * 8 + shard % 8
    inputs = inputs[:, 0]

    with jax.named_scope("gather_block_weights"):
        rows = jnp.concatenate(
            [contract_weight[0], output_weight[0]] + jnp.split(expand_weight[0], 4, 1), 0
        )
        quarter = lax.dynamic_slice_in_dim(rows, lax.axis_index("replica") * 144, 144, 0)
        gathered = lax.all_gather(quarter, REST, axis=0, tiled=False).reshape(16, 576, 1024)

    with jax.named_scope("head_weights"):
        by_head = attend_weight[0].reshape(64, 3, HEADS, HEAD_DIM).transpose(2, 0, 1, 3)
        small = jnp.concatenate(
            [
                biases.reshape(384),
                gains.reshape(128),
                hidden_bias.reshape(256),
                segments.reshape(128).astype(LOW),
                jnp.zeros((16 * 192 - 896,), LOW),
            ]
        ).reshape(1, 16, 192)
        block = jnp.concatenate(
            [by_head.reshape(HEADS, 64, 192), jnp.broadcast_to(small, (HEADS, 16, 192))], 1
        )
        block = jnp.broadcast_to(block.reshape(2, 1, 8, 80, 192), (2, 2, 8, 80, 192))
        got = exchange(block.reshape(32, 80, 192), ALL).reshape(2, 16, 80, 192)
        head_weight = got[:, :, :64].reshape(2, 1024, 192)
        small = got[:, :, 64:69].reshape(2, 16, 960)
        all_biases = small[:, :, :384].reshape(2, 16, 6, 64).transpose(0, 2, 1, 3)
        all_biases = all_biases.reshape(2, 6, 1024).astype(jnp.float32)
        all_gains = small[:, :, 384:512].reshape(2, 16, 2, 64).transpose(0, 2, 1, 3)
        all_gains = all_gains.reshape(2, 2, 1024).astype(jnp.float32)
        all_hidden = small[:, :, 512:768].reshape(2, 4096).astype(jnp.float32)
        seg = small[0, :, 768:896].reshape(16, 2, 64)
        seg = jnp.where(micro == 0, seg[:, 0], seg[:, 1]).reshape(1024)
        own_biases = jnp.where(on_first, all_biases[0], all_biases[1])
        own_gains = jnp.where(on_first, all_gains[0], all_gains[1])
        own_hidden = jnp.where(on_first, all_hidden[0], all_hidden[1]).reshape(PARTS, 1, WIDTH)
        params = jnp.concatenate([own_biases[2:], own_gains, jnp.zeros((2, 1024))], 0)
        head_bias = lax.dynamic_slice_in_dim(
            all_biases.reshape(2, 6, HEADS, HEAD_DIM), head, 1, 2
        )[:, :, 0]
        head_bias = jnp.concatenate(
            [head_bias[:, 0], jnp.zeros_like(head_bias[:, 0]), head_bias[:, 1]], 1
        )

    def attention(layer, tokens):
        with jax.named_scope("sequence_tokens"):
            whole = whole_sequence(tokens)
        with jax.named_scope("attention"):
            packed = (matmul(whole, head_weight[layer]) + head_bias[layer]).astype(LOW)
            context, log_totals = attend(packed, seg)
        with jax.named_scope("context_out"):
            context = send_tokens(context, 1)
        return context, (whole, packed, log_totals)

    def attention_back(layer, grad_context, kept):
        unused, packed, log_totals = kept
        with jax.named_scope("grad_context_in"):
            got = exchange(grad_context.reshape(32, 64, 128), ALL)
        with jax.named_scope("attention_back"):
            core = (shard % 2).astype(jnp.int32).reshape(1)
            grad_packed = attend_back(core, packed, log_totals, seg, got, layer)
        return grad_packed

    def attend_part(tokens, grad_packed):
        grad_weight = transposed_times(tokens, grad_packed)
        return with_sums(grad_weight, jnp.sum(grad_packed.astype(jnp.float32), 0))

    context_0, kept_0 = attention(0, inputs)
    tokens_0 = inputs.reshape(128, 1024)
    with jax.named_scope("block_0"):
        output, unused = block_forward(tokens_0, context_0, gathered, params, own_hidden)
    with jax.named_scope("to_next_section"):
        tokens_1 = jnp.where(
            on_first, output, lax.ppermute(output, "section", [(0, 1)])
        )
    with jax.named_scope("gather_attend_weight"):
        own_pairs = attend_weight[0].reshape(64, 3, 8, 128).transpose(0, 2, 1, 3).reshape(64, 3072)
        other_pairs = lax.ppermute(own_pairs, "section", [(0, 1), (1, 0)])
        both_pairs = jnp.concatenate(
            [
                jnp.where(on_first, own_pairs, other_pairs),
                jnp.where(on_first, other_pairs, own_pairs),
            ],
            0,
        )
        both_pairs, output = lax.optimization_barrier((both_pairs, output))
        whole_attend = lax.all_gather(both_pairs, "shard", axis=0, tiled=False)
    context_1, kept_1 = attention(1, tokens_1.reshape(2, 64, 1024))
    own_tokens = jnp.where(on_first, tokens_0, tokens_1)
    own_context = jnp.where(on_first, context_0, context_1)
    with jax.named_scope("block_1"):
        output, saved = block_forward(own_tokens, own_context, gathered, params, own_hidden)
    layer_output = output.reshape(1, 2, 1, 64, 1024)
    with jax.named_scope("gather_first"):
        first_all = lax.all_gather(saved[1], "shard", axis=0, tiled=True)

    last_grad = cotangent.reshape(128, 1024)
    with jax.named_scope("block_back_1"):
        grad_residual, unused, grad_context, unused = block_back(
            last_grad, saved, gathered, params
        )
    with jax.named_scope("residual_to_previous_section"):
        arrived = lax.ppermute(grad_residual, "section", [(1, 0)])
        grad_residual = jnp.where(on_first, arrived, grad_residual)
    grad_packed_1 = attention_back(1, grad_context, kept_1)
    with jax.named_scope("grad_tokens_1"):
        grad_tokens_1, rounded = grad_tokens(
            1, send_tokens(grad_packed_1, 3), whole_attend, grad_residual
        )
    own_grad = jnp.where(on_first, rounded, last_grad)
    with jax.named_scope("gather_grad_mlp"):
        grad_mlp = normed_back(own_grad.astype(jnp.float32), saved[3], params[5:6])[0].astype(LOW)
        grad_mlp, own_grad = lax.optimization_barrier((grad_mlp, own_grad))
        grad_mlp_all = lax.all_gather(grad_mlp, "shard", axis=0, tiled=True)
    with jax.named_scope("block_back_0"):
        grad_residual, grad_attn, grad_context, norm_sums = block_back(
            own_grad, saved, gathered, params
        )
    late_tokens, late_packed, late_gathered, grad_context = lax.optimization_barrier(
        (kept_1[0], grad_packed_1, gathered, grad_context)
    )
    with jax.named_scope("swap_attend_grad"):
        part_1 = attend_part(late_tokens, late_packed)
        take_1 = lax.ppermute(part_1, "section", [(0, 1)])
    grad_packed = attention_back(0, grad_context, kept_0)

    with jax.named_scope("sum_output_grad"):
        output_grad = transposed_times(saved[4], grad_attn)
        halves = [output_grad[:, :512], output_grad[:, 512:]]
        core = shard % 2
        keep = jnp.where(core == 0, halves[0], halves[1])
        give = jnp.where(core == 0, halves[1], halves[0]).astype(LOW)
        output_grad = (keep + swap_cores(give).astype(jnp.float32)).astype(LOW)
        output_got = exchange(output_grad.reshape(64, 16, 512), REST)
    with jax.named_scope("swap_attend_grad"):
        part_0 = attend_part(kept_0[0], grad_packed)
        take_0 = lax.ppermute(part_0, "section", [(1, 0)])
        lower = jnp.where(on_first, part_0, take_1)
        upper = jnp.where(on_first, take_0, part_1)
        attend_grad = jnp.concatenate([lower[:1024], upper[:1024]], 1)
        sums = jnp.stack([lower[1024], upper[1024]]).reshape(2, 3, HEAD_DIM)
        norm_rows = norm_sums[:5].reshape(5, 16, 64).transpose(1, 0, 2)
        mine = jnp.arange(8) == shard % 8
        head_rows = jnp.where(
            mine[None, :, None, None], sums[:, None, ::2].astype(jnp.float32), 0.0
        ).reshape(16, 2, 64)
        vectors = jnp.pad(
            jnp.concatenate([norm_rows, head_rows], 1), ((0, 0), (0, 9), (0, 64))
        )
        vectors = jnp.broadcast_to(vectors[:, None], (16, 4, 16, 128)).reshape(1024, 128)
        vectors = vectors.astype(LOW)
    with jax.named_scope("block_weight_grads"):
        expand_part = lax.dynamic_slice(
            late_gathered, (0, 320 + shard // 4 * 64, shard % 4 * 256), (16, 64, 256)
        ).reshape(1024, 256)
        hidden_part = lax.dynamic_slice_in_dim(own_hidden.reshape(4096), shard * 256, 256, 0)
        inner = matmul(first_all, expand_part) + hidden_part
        activation = inner * gelu_share(inner)
        grad_inner = times_transposed(grad_mlp_all, contract_weight[0]) * gelu_slope(inner)
        grad_inner = grad_inner.astype(LOW)
        expand_grad = transposed_times(first_all, grad_inner).astype(LOW)
        contract_grad = transposed_times(activation.astype(LOW), grad_mlp_all).astype(LOW)
        hidden_sum = jnp.sum(grad_inner.astype(jnp.float32), 0)
        mlp_sum = jnp.sum(grad_mlp_all.astype(jnp.float32), 0)
        extra = jnp.concatenate(
            [
                jnp.concatenate([hidden_sum, jnp.zeros((768,), jnp.float32)])[None],
                mlp_sum[None],
                jnp.zeros((14, 1024), jnp.float32),
            ],
            0,
        ).astype(LOW)
        rows = jnp.concatenate(
            [contract_grad.reshape(4, 64, 1024), jnp.broadcast_to(extra, (4, 16, 1024))], 1
        )
    with jax.named_scope("sum_attend_expand_grads"):
        parts = jnp.concatenate([attend_grad, expand_grad, vectors], 1)
        parts, rows, output_got = lax.optimization_barrier((parts, rows, output_got))
        got = exchange(parts.reshape(64, 16, 768), REST)
        got, rows = lax.optimization_barrier((got, rows))
    with jax.named_scope("sum_contract"):
        got_contract = exchange(rows, "replica").astype(jnp.float32).sum(0)
    with jax.named_scope("sum_attend_grad"):
        got_output = output_got.astype(jnp.float32).reshape(8, 2, 4, 16, 512).sum((0, 2))
        got_output = jnp.concatenate([got_output[0], got_output[1]], 1).astype(LOW)
        got_attend = got[:, :, :384].astype(jnp.float32).reshape(2, 8, 4, 16, 384).sum((0, 2))
        got_expand = got[:, :, 384:640].astype(jnp.float32).reshape(16, 4, 16, 256).sum(1)
        got_expand = got_expand.astype(LOW).transpose(1, 0, 2).reshape(16, 4096)
        got_vectors = got[:, :7, 640:704].astype(jnp.float32).sum(0)
        got_attend, got_output = lax.optimization_barrier((got_attend.astype(LOW), got_output))
        got_attend = got_attend.reshape(8, 16, 2, 3, 64).transpose(1, 3, 2, 0, 4)
        got_attend = got_attend.reshape(16, 3072)
    with jax.named_scope("gather_weight_grads"):
        contract_rows = got_contract[:64].astype(LOW).reshape(4, 16, 1024)
        owned = jnp.concatenate([got_attend, got_output, got_expand, *contract_rows], 1)
    with jax.named_scope("grad_tokens_0"):
        late_packed, owned = lax.optimization_barrier((grad_packed, owned))
        grad_tokens_0, unused = grad_tokens(
            0, send_tokens(late_packed, 3), whole_attend, grad_residual
        )
    with jax.named_scope("gather_weight_grads"):
        totals = lax.all_gather(owned, "replica", axis=0, tiled=True)
        contract_total = totals[:, 8192:].reshape(4, 16, 4, 1024).transpose(0, 2, 1, 3)
        contract_total = contract_total.reshape(1, 256, 1024).astype(jnp.float32)
        totals = totals[None, :, :8192].astype(jnp.float32)
    input_grad = jnp.where(on_first, grad_tokens_0, grad_tokens_1).reshape(1, 2, 1, 64, 1024)
    mlp_own = lax.dynamic_slice_in_dim(got_contract[65], shard * 64, 64, 0)
    biases_grad = jnp.stack(
        [
            got_vectors[5],
            got_vectors[6],
            got_vectors[2],
            got_vectors[3],
            mlp_own,
            got_vectors[4],
        ]
    )
    return (
        layer_output,
        input_grad,
        totals[:, :, :3072],
        totals[:, :, 3072:4096],
        totals[:, :, 4096:],
        contract_total,
        biases_grad[None],
        got_contract[None, 64, :256],
        got_vectors[None, :2],
    )


def solution(mesh):
    placed = (
        P(None, "replica", "shard", None),
        P(None, "replica", "shard"),
        P(None, "replica", "shard", None),
        P("section", "shard", None),
        P("section", "shard", None),
        P("section", "shard", None),
        P("section", "shard", None),
        P("section", None, "shard"),
        P("section", "shard"),
        P("section", None, "shard"),
    )
    return jax.shard_map(
        on_device,
        mesh=mesh,
        in_specs=placed,
        out_specs=(
            P("section", None, "replica", "shard", None),
            P("section", None, "replica", "shard", None),
            P("section", "shard", None),
            P("section", "shard", None),
            P("section", "shard", None),
            P("section", "shard", None),
            P("section", None, "shard"),
            P("section", "shard"),
            P("section", None, "shard"),
        ),
        check_vma=False,
    )
```

```python
import math

import jax
import jax.numpy as jnp
from jax import lax
from jax.experimental import pallas as pl
from jax.experimental.pallas import tpu as pltpu
from jax.sharding import PartitionSpec as P

HEADS = 16
HEAD_DIM = 64
NEGATIVE = -1e30
EPSILON = 1e-05
SCALE = 1.0 / math.sqrt(HEAD_DIM)
LOW = jnp.bfloat16
ALL = ("section", "shard")
REST = ("shard", "replica")


def matmul(left, right):
    return jnp.dot(left, right, preferred_element_type=jnp.float32)


def times_transposed(left, right):
    return lax.dot_general(
        left, right, (((1,), (1,)), ((), ())), preferred_element_type=jnp.float32
    )


def transposed_times(left, right):
    return lax.dot_general(
        left, right, (((0,), (0,)), ((), ())), preferred_element_type=jnp.float32
    )


def exchange(value, axes):
    return lax.all_to_all(value, axes, 0, 0, tiled=True)


def swap_cores(value):
    return lax.ppermute(value, "shard", [(i, i ^ 1) for i in range(16)])


def whole_sequence(tokens):
    core = lax.axis_index("shard") % 2
    micros, rows, features = tokens.shape
    half = rows // 2
    sends = jnp.broadcast_to(
        tokens.reshape(micros, 1, 2, half, features), (micros, 4, 2, half, features)
    ).reshape(16, half, features)
    mine = exchange(sends, "shard")
    other = swap_cores(mine)
    lower = jnp.where(core == 0, mine, other)
    upper = jnp.where(core == 0, other, mine)
    return jnp.stack([lower, upper], 1).reshape(16 * rows, features)


def send_tokens(value, parts):
    core = lax.axis_index("shard") % 2
    width = parts * HEAD_DIM
    halves = value.reshape(16, 2, 32, width)
    keep = jnp.where(core == 0, halves[:, 0], halves[:, 1])
    take = swap_cores(jnp.where(core == 0, halves[:, 1], halves[:, 0]))
    lower = jnp.split(jnp.where(core == 0, keep, take), parts, 2)
    upper = jnp.split(jnp.where(core == 0, take, keep), parts, 2)
    pair = jnp.concatenate([piece for both in zip(lower, upper) for piece in both], 2)
    sends = jnp.broadcast_to(pair[None], (2, 16, 32, 2 * width)).reshape(32, 32, 2 * width)
    return exchange(sends, ALL).reshape(2, 2, 4, 2, 32, 2 * width)


def masked_scores(queries, keys, seg):
    scores = times_transposed(queries, keys) * SCALE
    return jnp.where(seg[:, None] == seg[None, :], scores, NEGATIVE)


def attend(packed, seg):
    queries, keys, values = jnp.split(packed, 3, 1)
    scores = masked_scores(queries, keys, seg)
    highest = jnp.max(scores, -1, keepdims=True)
    exponent = jnp.exp(scores - highest)
    totals = jnp.sum(exponent, -1, keepdims=True)
    context = matmul((exponent / totals).astype(LOW), values).astype(LOW)
    return context, highest + jnp.log(totals)


def normed(value):
    mean_value = jnp.mean(value, -1, keepdims=True)
    centred = value - mean_value
    spread = jnp.mean(centred * centred, -1, keepdims=True)
    scale = lax.rsqrt(spread + EPSILON)
    return centred * scale, scale


def normed_back(grad, value, gain):
    unit, scale = normed(value)
    weighted = grad * gain
    inner_mean = jnp.mean(weighted * unit, -1, keepdims=True)
    grad_value = scale * (weighted - jnp.mean(weighted, -1, keepdims=True) - unit * inner_mean)
    return (
        grad_value,
        jnp.sum(grad * unit, 0, keepdims=True),
        jnp.sum(grad, 0, keepdims=True),
    )


def gelu_share(value):
    return 0.5 * (1.0 + lax.erf(value * math.sqrt(0.5)))


def gelu_slope(value):
    return gelu_share(value) + value * jnp.exp(-0.5 * value * value) * (0.5 / math.pi) ** 0.5


PARTS = 4
WIDTH = 1024


def this_part(j):
    return jnp.minimum(j, PARTS - 1)


def part_before(j):
    return jnp.maximum(j - 1, 0)


def weight_specs(expand_at, contract_at):
    return [
        pl.BlockSpec((16, 64, 1024), lambda j: (0, 4, 0)),
        pl.BlockSpec((16, 64, WIDTH), lambda j: (0, 5 + expand_at(j), 0)),
        pl.BlockSpec((4, 256, 1024), lambda j: (contract_at(j), 0, 0)),
    ]


def full(*shape):
    return pl.BlockSpec(shape, lambda j: (0,) * len(shape))


ROWS_F32 = jax.ShapeDtypeStruct((128, 1024), jnp.float32)
ROWS_LOW = jax.ShapeDtypeStruct((128, 1024), LOW)
BLOCK_PARAMS = pltpu.CompilerParams(
    dimension_semantics=("arbitrary",), vmem_limit_bytes=48 * 1024 * 1024
)
BLOCK_COST = pl.CostEstimate(
    flops=2 * 128 * 1024 * 9216, bytes_accessed=24 * 1024 * 1024, transcendentals=128 * 4096
)


def forward_kernel(
    tokens,
    context,
    output_weight,
    expand_weight,
    contract_weight,
    params,
    hidden,
    output,
    residual,
    first_low,
    inner,
    second,
    context_rows,
    first,
    total,
    before,
):
    step = pl.program_id(0)

    @pl.when(step == 0)
    def start():
        pairs = [context[s, :, p].reshape(128, 128) for s in range(2) for p in range(4)]
        rows = jnp.concatenate(pairs, 1)
        context_rows[...] = rows
        attention = matmul(rows, output_weight[...].reshape(1024, 1024))
        summed = tokens[...].astype(jnp.float32) + (attention + params[0:1])
        residual[...] = summed
        after = normed(summed)[0] * params[4:5] + params[1:2]
        first[...] = after
        first_low[...] = after.astype(LOW)
        total[...] = jnp.zeros_like(total)
        before[...] = jnp.zeros_like(before)

    last_part = before[...]
    inner_part = matmul(first_low[...], expand_weight[...].reshape(1024, WIDTH)) + hidden[0]
    inner[...] = inner_part
    activation = (last_part * gelu_share(last_part)).astype(LOW)
    total[...] += matmul(activation, contract_weight[...].reshape(WIDTH, 1024))
    before[...] = inner_part

    @pl.when(step == PARTS)
    def finish():
        summed = first[...] + (total[...] + params[2:3])
        second[...] = summed
        output[...] = (normed(summed)[0] * params[5:6] + params[3:4]).astype(LOW)


def block_forward(tokens, context, gathered, params, hidden):
    output, *saved = pl.pallas_call(
        forward_kernel,
        grid=(PARTS + 1,),
        in_specs=[
            full(128, 1024),
            full(2, 2, 4, 2, 32, 128),
            *weight_specs(this_part, part_before),
            full(8, 1024),
            pl.BlockSpec((1, 1, WIDTH), lambda j: (this_part(j), 0, 0)),
        ],
        out_specs=[
            full(128, 1024),
            full(128, 1024),
            full(128, 1024),
            pl.BlockSpec((128, WIDTH), lambda j: (0, this_part(j))),
            full(128, 1024),
            full(128, 1024),
        ],
        out_shape=[
            ROWS_LOW,
            ROWS_F32,
            ROWS_LOW,
            jax.ShapeDtypeStruct((128, 4096), jnp.float32),
            ROWS_F32,
            ROWS_LOW,
        ],
        scratch_shapes=[
            pltpu.VMEM((128, 1024), jnp.float32),
            pltpu.VMEM((128, 1024), jnp.float32),
            pltpu.VMEM((128, WIDTH), jnp.float32),
        ],
        compiler_params=BLOCK_PARAMS,
        cost_estimate=BLOCK_COST,
    )(tokens, context, gathered, gathered, gathered, params, hidden)
    return output, saved


def backward_kernel(
    grad,
    output_weight,
    expand_weight,
    contract_weight,
    params,
    residual,
    inner,
    second,
    grad_residual,
    grad_attn,
    grad_context,
    sums,
    grad_mlp,
    grad_second,
    total,
    before,
):
    step = pl.program_id(0)

    @pl.when(step == 0)
    def start():
        by_value, by_gain, by_shift = normed_back(
            grad[...].astype(jnp.float32), second[...], params[5:6]
        )
        grad_second[...] = by_value
        grad_mlp[...] = by_value.astype(LOW)
        sums[1:2] = by_gain
        sums[4:5] = by_shift
        total[...] = jnp.zeros_like(total)
        before[...] = jnp.zeros_like(before)

    last_part = before[...]
    before[...] = times_transposed(grad_mlp[...], contract_weight[...].reshape(WIDTH, 1024))
    grad_inner = (last_part * gelu_slope(inner[...])).astype(LOW)
    total[...] += times_transposed(grad_inner, expand_weight[...].reshape(1024, WIDTH))

    @pl.when(step == PARTS)
    def finish():
        by_value, by_gain, by_shift = normed_back(
            grad_second[...] + total[...], residual[...], params[4:5]
        )
        grad_residual[...] = by_value
        rounded = by_value.astype(LOW)
        grad_attn[...] = rounded
        rows = times_transposed(rounded, output_weight[...].reshape(1024, 1024)).astype(LOW)
        for s, m, p in ((s, m, p) for s in range(2) for m in range(2) for p in range(4)):
            piece = rows[64 * m : 64 * m + 64, 128 * (4 * s + p) : 128 * (4 * s + p) + 128]
            grad_context[s, m, p, 0] = piece
            grad_context[s, m, p, 1] = piece
        sums[0:1] = by_gain
        sums[2:3] = jnp.sum(rounded.astype(jnp.float32), 0, keepdims=True)
        sums[3:4] = by_shift
        sums[5:8] = jnp.zeros((3, 1024), jnp.float32)


def block_back(grad, saved, gathered, params):
    residual, first_low, inner, second, context_rows = saved
    return pl.pallas_call(
        backward_kernel,
        grid=(PARTS + 1,),
        in_specs=[
            full(128, 1024),
            *weight_specs(part_before, this_part),
            full(8, 1024),
            full(128, 1024),
            pl.BlockSpec((128, WIDTH), lambda j: (0, part_before(j))),
            full(128, 1024),
        ],
        out_specs=[
            full(128, 1024),
            full(128, 1024),
            full(2, 2, 4, 2, 64, 128),
            full(8, 1024),
        ],
        out_shape=[
            ROWS_F32,
            ROWS_LOW,
            jax.ShapeDtypeStruct((2, 2, 4, 2, 64, 128), LOW),
            jax.ShapeDtypeStruct((8, 1024), jnp.float32),
        ],
        scratch_shapes=[
            pltpu.VMEM((128, 1024), LOW),
            pltpu.VMEM((128, 1024), jnp.float32),
            pltpu.VMEM((128, 1024), jnp.float32),
            pltpu.VMEM((128, WIDTH), jnp.float32),
        ],
        compiler_params=BLOCK_PARAMS,
        cost_estimate=BLOCK_COST,
    )(grad, gathered, gathered, gathered, params, residual, inner, second)


def grad_tokens_kernel(got, weight, grad_residual, result, rounded, total):
    step = pl.program_id(0)
    left = jnp.concatenate([got[0, :, p].reshape(128, 384) for p in range(2)], 1)
    product = times_transposed(left, weight[...])

    @pl.when(step == 0)
    def start():
        total[...] = grad_residual[...] + product

    @pl.when(step > 0)
    def proceed():
        total[...] += product

    @pl.when(step == 3)
    def finish():
        result[...] = total[...]
        rounded[...] = total[...].astype(LOW)


def grad_tokens(got, weight, grad_residual):
    return pl.pallas_call(
        grad_tokens_kernel,
        grid=(4,),
        in_specs=[
            pl.BlockSpec((1, 2, 2, 2, 32, 384), lambda i: (i // 2, 0, i % 2, 0, 0, 0)),
            pl.BlockSpec((1024, 768), lambda i: (0, i)),
            full(128, 1024),
        ],
        out_specs=[full(128, 1024), full(128, 1024)],
        out_shape=[ROWS_F32, ROWS_LOW],
        scratch_shapes=[pltpu.VMEM((128, 1024), jnp.float32)],
        compiler_params=BLOCK_PARAMS,
        cost_estimate=pl.CostEstimate(
            flops=2 * 128 * 3072 * 1024, bytes_accessed=8 * 1024 * 1024, transcendentals=0
        ),
    )(got, weight, grad_residual)


def attend_back_kernel(
    core,
    packed,
    log_totals,
    seg_rows,
    seg_columns,
    got,
    result,
    queries,
    keys,
    values,
    grads,
    grad_keys,
    grad_values,
):
    step = pl.program_id(0)

    @pl.when(step == 0)
    def start():
        queries[...] = packed[:, :HEAD_DIM]
        keys[...] = packed[:, HEAD_DIM : 2 * HEAD_DIM]
        values[...] = packed[:, 2 * HEAD_DIM :]
        pair = got[...].reshape(1024, 128)
        grads[...] = jnp.where(core[0] == 0, pair[:, :HEAD_DIM], pair[:, HEAD_DIM:])
        grad_keys[...] = jnp.zeros_like(grad_keys)
        grad_values[...] = jnp.zeros_like(grad_values)

    rows = pl.ds(pl.multiple_of(step * 256, 256), 256)
    block_queries = queries[rows]
    block_grads = grads[rows]
    scores = times_transposed(block_queries, keys[...]) * SCALE
    scores = jnp.where(seg_rows[rows] == seg_columns[...], scores, NEGATIVE)
    soft = jnp.exp(scores - log_totals[rows])
    grad_soft = times_transposed(block_grads, values[...])
    row_total = jnp.sum(soft * grad_soft, -1, keepdims=True)
    grad_scores = (soft * (grad_soft - row_total)).astype(LOW)
    result[rows, :HEAD_DIM] = (matmul(grad_scores, keys[...]) * SCALE).astype(LOW)
    grad_keys[...] += transposed_times(grad_scores, block_queries)
    grad_values[...] += transposed_times(soft.astype(LOW), block_grads)

    @pl.when(step == 3)
    def finish():
        result[:, HEAD_DIM : 2 * HEAD_DIM] = (grad_keys[...] * SCALE).astype(LOW)
        result[:, 2 * HEAD_DIM :] = grad_values[...].astype(LOW)


def attend_back(core, packed, log_totals, seg, got, layer):
    return pl.pallas_call(
        attend_back_kernel,
        grid=(4,),
        in_specs=[
            pl.BlockSpec(memory_space=pltpu.SMEM),
            full(1024, 192),
            full(1024, 1),
            full(1024, 1),
            full(1, 1024),
            pl.BlockSpec((16, 64, 128), lambda i: (layer, 0, 0)),
        ],
        out_specs=full(1024, 192),
        out_shape=jax.ShapeDtypeStruct((1024, 192), LOW),
        scratch_shapes=[pltpu.VMEM((1024, HEAD_DIM), LOW)] * 4
        + [pltpu.VMEM((1024, HEAD_DIM), jnp.float32)] * 2,
        compiler_params=BLOCK_PARAMS,
        cost_estimate=pl.CostEstimate(
            flops=10 * 1024 * 1024 * 64, bytes_accessed=2 * 1024 * 1024, transcendentals=1 << 20
        ),
    )(core, packed, log_totals, seg[:, None], seg[None, :], got)


def with_sums(grad, sums):
    rows = jnp.concatenate([sums[None], jnp.zeros((15, sums.shape[0]), jnp.float32)], 0)
    return jnp.concatenate([grad.astype(LOW), rows.astype(LOW)], 0)


def on_device(
    inputs,
    segments,
    cotangent,
    attend_weight,
    output_weight,
    expand_weight,
    contract_weight,
    biases,
    hidden_bias,
    gains,
):
    section = lax.axis_index("section")
    shard = lax.axis_index("shard")
    on_first = section == 0
    micro = shard // 8
    head = section * 8 + shard % 8
    inputs = inputs[:, 0]

    with jax.named_scope("gather_block_weights"):
        rows = jnp.concatenate(
            [contract_weight[0], output_weight[0]] + jnp.split(expand_weight[0], 4, 1), 0
        )
        quarter = lax.dynamic_slice_in_dim(rows, lax.axis_index("replica") * 144, 144, 0)
        gathered = lax.all_gather(quarter, REST, axis=0, tiled=False).reshape(16, 576, 1024)

    with jax.named_scope("head_weights"):
        by_head = attend_weight[0].reshape(64, 3, HEADS, HEAD_DIM).transpose(2, 0, 1, 3)
        small = jnp.concatenate(
            [
                biases.reshape(384),
                gains.reshape(128),
                hidden_bias.reshape(256),
                segments.reshape(128).astype(LOW),
                jnp.zeros((16 * 192 - 896,), LOW),
            ]
        ).reshape(1, 16, 192)
        block = jnp.concatenate(
            [by_head.reshape(HEADS, 64, 192), jnp.broadcast_to(small, (HEADS, 16, 192))], 1
        )
        block = jnp.broadcast_to(block.reshape(2, 1, 8, 80, 192), (2, 2, 8, 80, 192))
        got = exchange(block.reshape(32, 80, 192), ALL).reshape(2, 16, 80, 192)
        head_weight = got[:, :, :64].reshape(2, 1024, 192)
        small = got[:, :, 64:69].reshape(2, 16, 960)
        all_biases = small[:, :, :384].reshape(2, 16, 6, 64).transpose(0, 2, 1, 3)
        all_biases = all_biases.reshape(2, 6, 1024).astype(jnp.float32)
        all_gains = small[:, :, 384:512].reshape(2, 16, 2, 64).transpose(0, 2, 1, 3)
        all_gains = all_gains.reshape(2, 2, 1024).astype(jnp.float32)
        all_hidden = small[:, :, 512:768].reshape(2, 4096).astype(jnp.float32)
        seg = small[0, :, 768:896].reshape(16, 2, 64)
        seg = jnp.where(micro == 0, seg[:, 0], seg[:, 1]).reshape(1024)
        own_biases = jnp.where(on_first, all_biases[0], all_biases[1])
        own_gains = jnp.where(on_first, all_gains[0], all_gains[1])
        own_hidden = jnp.where(on_first, all_hidden[0], all_hidden[1]).reshape(PARTS, 1, WIDTH)
        params = jnp.concatenate([own_biases[2:], own_gains, jnp.zeros((2, 1024))], 0)
        head_bias = lax.dynamic_slice_in_dim(
            all_biases.reshape(2, 6, HEADS, HEAD_DIM), head, 1, 2
        )[:, :, 0]
        head_bias = jnp.concatenate(
            [head_bias[:, 0], jnp.zeros_like(head_bias[:, 0]), head_bias[:, 1]], 1
        )

    def attention(layer, tokens):
        with jax.named_scope("sequence_tokens"):
            whole = whole_sequence(tokens)
        with jax.named_scope("attention"):
            packed = (matmul(whole, head_weight[layer]) + head_bias[layer]).astype(LOW)
            context, log_totals = attend(packed, seg)
        with jax.named_scope("context_out"):
            context = send_tokens(context, 1)
        return context, (whole, packed, log_totals)

    def attention_back(layer, grad_context, kept, beside):
        unused, packed, log_totals = kept
        with jax.named_scope("grad_context_in"):
            got = exchange(grad_context.reshape(32, 64, 128), ALL)
            got, beside = lax.optimization_barrier((got, beside))
        with jax.named_scope("attention_back"):
            core = (shard % 2).astype(jnp.int32).reshape(1)
            grad_packed = attend_back(core, packed, log_totals, seg, got, layer)
        return grad_packed, beside

    def attend_part(tokens, grad_packed):
        grad_weight = transposed_times(tokens, grad_packed)
        return with_sums(grad_weight, jnp.sum(grad_packed.astype(jnp.float32), 0))

    context_0, kept_0 = attention(0, inputs)
    tokens_0 = inputs.reshape(128, 1024)
    with jax.named_scope("block_0"):
        output, unused = block_forward(tokens_0, context_0, gathered, params, own_hidden)
    with jax.named_scope("to_next_section"):
        tokens_1 = jnp.where(
            on_first, output, lax.ppermute(output, "section", [(0, 1)])
        )
    with jax.named_scope("gather_attend_weight"):
        own_pairs = attend_weight[0].reshape(64, 3, 8, 128).transpose(0, 2, 1, 3).reshape(64, 3072)
        other_pairs = lax.ppermute(own_pairs, "section", [(0, 1), (1, 0)])
        other_pairs, output = lax.optimization_barrier((other_pairs, output))
        other_attend = lax.all_gather(other_pairs, "shard", axis=0, tiled=True)
    context_1, kept_1 = attention(1, tokens_1.reshape(2, 64, 1024))
    own_tokens = jnp.where(on_first, tokens_0, tokens_1)
    own_context = jnp.where(on_first, context_0, context_1)
    with jax.named_scope("block_1"):
        output, saved = block_forward(own_tokens, own_context, gathered, params, own_hidden)
    layer_output = output.reshape(1, 2, 1, 64, 1024)
    with jax.named_scope("gather_first"):
        first_all = lax.all_gather(saved[1], "shard", axis=0, tiled=True)

    last_grad = cotangent.reshape(128, 1024)
    with jax.named_scope("block_back_1"):
        grad_residual, unused, grad_context, unused = block_back(
            last_grad, saved, gathered, params
        )
    with jax.named_scope("residual_to_other_section"):
        arrived_1 = lax.ppermute(grad_residual, "section", [(1, 0)])
    grad_packed_1, arrived_1 = attention_back(1, grad_context, kept_1, arrived_1)
    with jax.named_scope("grad_tokens_1"):
        result_1, rounded = grad_tokens(send_tokens(grad_packed_1, 3), other_attend, arrived_1)
        grad_tokens_1 = lax.ppermute(result_1, "section", [(0, 1)])
    own_grad = jnp.where(on_first, rounded, last_grad)
    with jax.named_scope("gather_grad_mlp"):
        grad_mlp = normed_back(own_grad.astype(jnp.float32), saved[3], params[5:6])[0].astype(LOW)
        grad_mlp, own_grad = lax.optimization_barrier((grad_mlp, own_grad))
        grad_mlp_all = lax.all_gather(grad_mlp, "shard", axis=0, tiled=True)
    with jax.named_scope("block_back_0"):
        grad_residual, grad_attn, grad_context, norm_sums = block_back(
            own_grad, saved, gathered, params
        )
    with jax.named_scope("residual_to_other_section"):
        arrived_0 = lax.ppermute(grad_residual, "section", [(0, 1)])
    late_tokens, late_packed, late_gathered, grad_context = lax.optimization_barrier(
        (kept_1[0], grad_packed_1, gathered, grad_context)
    )
    with jax.named_scope("swap_attend_grad"):
        part_1 = attend_part(late_tokens, late_packed)
        take_1 = lax.ppermute(part_1, "section", [(0, 1)])
    with jax.named_scope("sum_output_grad"):
        output_grad = transposed_times(saved[4], grad_attn)
        halves = [output_grad[:, :512], output_grad[:, 512:]]
        core = shard % 2
        keep = jnp.where(core == 0, halves[0], halves[1])
        give = jnp.where(core == 0, halves[1], halves[0]).astype(LOW)
        output_grad = (keep + swap_cores(give).astype(jnp.float32)).astype(LOW)
    grad_packed, output_grad = attention_back(0, grad_context, kept_0, output_grad)

    with jax.named_scope("sum_output_grad"):
        output_got = exchange(output_grad.reshape(64, 16, 512), REST)
    with jax.named_scope("swap_attend_grad"):
        part_0 = attend_part(kept_0[0], grad_packed)
        take_0 = lax.ppermute(part_0, "section", [(1, 0)])
        lower = jnp.where(on_first, part_0, take_1)
        upper = jnp.where(on_first, take_0, part_1)
        attend_grad = jnp.concatenate([lower[:1024], upper[:1024]], 1)
        sums = jnp.stack([lower[1024], upper[1024]]).reshape(2, 3, HEAD_DIM)
        norm_rows = norm_sums[:5].reshape(5, 16, 64).transpose(1, 0, 2)
        mine = jnp.arange(8) == shard % 8
        head_rows = jnp.where(
            mine[None, :, None, None], sums[:, None, ::2].astype(jnp.float32), 0.0
        ).reshape(16, 2, 64)
        vectors = jnp.pad(
            jnp.concatenate([norm_rows, head_rows], 1), ((0, 0), (0, 9), (0, 64))
        )
        vectors = jnp.broadcast_to(vectors[:, None], (16, 4, 16, 128)).reshape(1024, 128)
        vectors = vectors.astype(LOW)
    with jax.named_scope("sum_attend_grad"):
        parts = jnp.concatenate([attend_grad, vectors], 1)
        output_got, parts = lax.optimization_barrier((output_got, parts))
        got = exchange(parts.reshape(64, 16, 512), REST)
    with jax.named_scope("block_weight_grads"):
        expand_part = lax.dynamic_slice(
            late_gathered, (0, 320 + shard // 4 * 64, shard % 4 * 256), (16, 64, 256)
        ).reshape(1024, 256)
        hidden_part = lax.dynamic_slice_in_dim(own_hidden.reshape(4096), shard * 256, 256, 0)
        inner = matmul(first_all, expand_part) + hidden_part
        activation = inner * gelu_share(inner)
        grad_inner = times_transposed(grad_mlp_all, contract_weight[0]) * gelu_slope(inner)
        grad_inner = grad_inner.astype(LOW)
        expand_grad = transposed_times(first_all, grad_inner).astype(LOW)
        contract_grad = transposed_times(activation.astype(LOW), grad_mlp_all).astype(LOW)
        hidden_sum = jnp.sum(grad_inner.astype(jnp.float32), 0)
        mlp_sum = jnp.sum(grad_mlp_all.astype(jnp.float32), 0)
        extra = jnp.concatenate(
            [
                jnp.concatenate([hidden_sum, jnp.zeros((768,), jnp.float32)])[None],
                mlp_sum[None],
                jnp.zeros((14, 1024), jnp.float32),
            ],
            0,
        ).astype(LOW)
        rows = jnp.concatenate(
            [contract_grad.reshape(4, 64, 1024), jnp.broadcast_to(extra, (4, 16, 1024))], 1
        )
    with jax.named_scope("sum_expand_grad"):
        got, expand_grad, rows = lax.optimization_barrier((got, expand_grad, rows))
        expand_got = exchange(expand_grad.reshape(64, 16, 256), REST)
        expand_got, rows = lax.optimization_barrier((expand_got, rows))
    with jax.named_scope("sum_contract"):
        got_contract = exchange(rows, "replica").astype(jnp.float32).sum(0)
    with jax.named_scope("sum_attend_grad"):
        got_output = output_got.astype(jnp.float32).reshape(8, 2, 4, 16, 512).sum((0, 2))
        got_output = jnp.concatenate([got_output[0], got_output[1]], 1).astype(LOW)
        got_attend = got[:, :, :384].astype(jnp.float32).reshape(2, 8, 4, 16, 384).sum((0, 2))
        got_expand = expand_got.astype(jnp.float32).reshape(16, 4, 16, 256).sum(1)
        got_expand = got_expand.astype(LOW).transpose(1, 0, 2).reshape(16, 4096)
        got_vectors = got[:, :7, 384:448].astype(jnp.float32).sum(0)
        got_attend, got_output = lax.optimization_barrier((got_attend.astype(LOW), got_output))
        got_attend = got_attend.reshape(8, 16, 2, 3, 64).transpose(1, 3, 2, 0, 4)
        got_attend = got_attend.reshape(16, 3072)
    with jax.named_scope("gather_weight_grads"):
        contract_rows = got_contract[:64].astype(LOW).reshape(4, 16, 1024)
        owned = jnp.concatenate([got_attend, got_output, got_expand, *contract_rows], 1)
    with jax.named_scope("grad_tokens_0"):
        late_packed, owned = lax.optimization_barrier((grad_packed, owned))
        result_0, unused = grad_tokens(send_tokens(late_packed, 3), other_attend, arrived_0)
        grad_tokens_0 = lax.ppermute(result_0, "section", [(1, 0)])
    with jax.named_scope("gather_weight_grads"):
        totals = lax.all_gather(owned, "replica", axis=0, tiled=True)
        contract_total = totals[:, 8192:].reshape(4, 16, 4, 1024).transpose(0, 2, 1, 3)
        contract_total = contract_total.reshape(1, 256, 1024).astype(jnp.float32)
        totals = totals[None, :, :8192].astype(jnp.float32)
    input_grad = jnp.where(on_first, grad_tokens_0, grad_tokens_1).reshape(1, 2, 1, 64, 1024)
    mlp_own = lax.dynamic_slice_in_dim(got_contract[65], shard * 64, 64, 0)
    biases_grad = jnp.stack(
        [
            got_vectors[5],
            got_vectors[6],
            got_vectors[2],
            got_vectors[3],
            mlp_own,
            got_vectors[4],
        ]
    )
    return (
        layer_output,
        input_grad,
        totals[:, :, :3072],
        totals[:, :, 3072:4096],
        totals[:, :, 4096:],
        contract_total,
        biases_grad[None],
        got_contract[None, 64, :256],
        got_vectors[None, :2],
    )


def solution(mesh):
    placed = (
        P(None, "replica", "shard", None),
        P(None, "replica", "shard"),
        P(None, "replica", "shard", None),
        P("section", "shard", None),
        P("section", "shard", None),
        P("section", "shard", None),
        P("section", "shard", None),
        P("section", None, "shard"),
        P("section", "shard"),
        P("section", None, "shard"),
    )
    return jax.shard_map(
        on_device,
        mesh=mesh,
        in_specs=placed,
        out_specs=(
            P("section", None, "replica", "shard", None),
            P("section", None, "replica", "shard", None),
            P("section", "shard", None),
            P("section", "shard", None),
            P("section", "shard", None),
            P("section", "shard", None),
            P("section", None, "shard"),
            P("section", "shard"),
            P("section", None, "shard"),
        ),
        check_vma=False,
    )
```

```python
import math

import jax
import jax.numpy as jnp
from jax import lax
from jax.experimental import pallas as pl
from jax.experimental.pallas import tpu as pltpu
from jax.sharding import PartitionSpec as P

HEADS = 16
HEAD_DIM = 64
NEGATIVE = -1e30
EPSILON = 1e-05
SCALE = 1.0 / math.sqrt(HEAD_DIM)
LOW = jnp.bfloat16
ALL = ("section", "shard")
REST = ("shard", "replica")


def matmul(left, right):
    return jnp.dot(left, right, preferred_element_type=jnp.float32)


def times_transposed(left, right):
    return lax.dot_general(
        left, right, (((1,), (1,)), ((), ())), preferred_element_type=jnp.float32
    )


def transposed_times(left, right):
    return lax.dot_general(
        left, right, (((0,), (0,)), ((), ())), preferred_element_type=jnp.float32
    )


def exchange(value, axes):
    return lax.all_to_all(value, axes, 0, 0, tiled=True)


def swap_cores(value):
    return lax.ppermute(value, "shard", [(i, i ^ 1) for i in range(16)])


def whole_sequence(tokens):
    core = lax.axis_index("shard") % 2
    micros, rows, features = tokens.shape
    half = rows // 2
    sends = jnp.broadcast_to(
        tokens.reshape(micros, 1, 2, half, features), (micros, 4, 2, half, features)
    ).reshape(16, half, features)
    mine = exchange(sends, "shard")
    other = swap_cores(mine)
    lower = jnp.where(core == 0, mine, other)
    upper = jnp.where(core == 0, other, mine)
    return jnp.stack([lower, upper], 1).reshape(16 * rows, features)


def send_tokens(value, parts):
    core = lax.axis_index("shard") % 2
    width = parts * HEAD_DIM
    halves = value.reshape(16, 2, 32, width)
    keep = jnp.where(core == 0, halves[:, 0], halves[:, 1])
    take = swap_cores(jnp.where(core == 0, halves[:, 1], halves[:, 0]))
    lower = jnp.split(jnp.where(core == 0, keep, take), parts, 2)
    upper = jnp.split(jnp.where(core == 0, take, keep), parts, 2)
    pair = jnp.concatenate([piece for both in zip(lower, upper) for piece in both], 2)
    sends = jnp.broadcast_to(pair[None], (2, 16, 32, 2 * width)).reshape(32, 32, 2 * width)
    return exchange(sends, ALL).reshape(2, 2, 4, 2, 32, 2 * width)


def masked_scores(queries, keys, seg):
    scores = times_transposed(queries, keys) * SCALE
    return jnp.where(seg[:, None] == seg[None, :], scores, NEGATIVE)


def attend(packed, seg):
    queries, keys, values = jnp.split(packed, 3, 1)
    scores = masked_scores(queries, keys, seg)
    highest = jnp.max(scores, -1, keepdims=True)
    exponent = jnp.exp(scores - highest)
    totals = jnp.sum(exponent, -1, keepdims=True)
    context = matmul((exponent / totals).astype(LOW), values).astype(LOW)
    return context, highest + jnp.log(totals)


def normed(value):
    mean_value = jnp.mean(value, -1, keepdims=True)
    centred = value - mean_value
    spread = jnp.mean(centred * centred, -1, keepdims=True)
    scale = lax.rsqrt(spread + EPSILON)
    return centred * scale, scale


def normed_back(grad, value, gain):
    unit, scale = normed(value)
    weighted = grad * gain
    inner_mean = jnp.mean(weighted * unit, -1, keepdims=True)
    grad_value = scale * (weighted - jnp.mean(weighted, -1, keepdims=True) - unit * inner_mean)
    return (
        grad_value,
        jnp.sum(grad * unit, 0, keepdims=True),
        jnp.sum(grad, 0, keepdims=True),
    )


def gelu_share(value):
    return 0.5 * (1.0 + lax.erf(value * math.sqrt(0.5)))


def gelu_slope(value):
    return gelu_share(value) + value * jnp.exp(-0.5 * value * value) * (0.5 / math.pi) ** 0.5


PARTS = 4
WIDTH = 1024


def this_part(j):
    return jnp.minimum(j, PARTS - 1)


def part_before(j):
    return jnp.maximum(j - 1, 0)


def weight_specs(expand_at, contract_at):
    return [
        pl.BlockSpec((16, 64, 1024), lambda j: (0, 4, 0)),
        pl.BlockSpec((16, 64, WIDTH), lambda j: (0, 5 + expand_at(j), 0)),
        pl.BlockSpec((4, 256, 1024), lambda j: (contract_at(j), 0, 0)),
    ]


def full(*shape):
    return pl.BlockSpec(shape, lambda j: (0,) * len(shape))


ROWS_F32 = jax.ShapeDtypeStruct((128, 1024), jnp.float32)
ROWS_LOW = jax.ShapeDtypeStruct((128, 1024), LOW)
BLOCK_PARAMS = pltpu.CompilerParams(
    dimension_semantics=("arbitrary",), vmem_limit_bytes=48 * 1024 * 1024
)
BLOCK_COST = pl.CostEstimate(
    flops=2 * 128 * 1024 * 9216, bytes_accessed=24 * 1024 * 1024, transcendentals=128 * 4096
)


def forward_kernel(
    tokens,
    context,
    output_weight,
    expand_weight,
    contract_weight,
    params,
    hidden,
    output,
    residual,
    first_low,
    inner,
    second,
    context_rows,
    first,
    total,
    before,
):
    step = pl.program_id(0)

    @pl.when(step == 0)
    def start():
        pairs = [context[s, :, p].reshape(128, 128) for s in range(2) for p in range(4)]
        rows = jnp.concatenate(pairs, 1)
        context_rows[...] = rows
        attention = matmul(rows, output_weight[...].reshape(1024, 1024))
        summed = tokens[...].astype(jnp.float32) + (attention + params[0:1])
        residual[...] = summed
        after = normed(summed)[0] * params[4:5] + params[1:2]
        first[...] = after
        first_low[...] = after.astype(LOW)
        total[...] = jnp.zeros_like(total)
        before[...] = jnp.zeros_like(before)

    last_part = before[...]
    inner_part = matmul(first_low[...], expand_weight[...].reshape(1024, WIDTH)) + hidden[0]
    inner[...] = inner_part
    activation = (last_part * gelu_share(last_part)).astype(LOW)
    total[...] += matmul(activation, contract_weight[...].reshape(WIDTH, 1024))
    before[...] = inner_part

    @pl.when(step == PARTS)
    def finish():
        summed = first[...] + (total[...] + params[2:3])
        second[...] = summed
        output[...] = (normed(summed)[0] * params[5:6] + params[3:4]).astype(LOW)


def block_forward(tokens, context, gathered, params, hidden):
    output, *saved = pl.pallas_call(
        forward_kernel,
        grid=(PARTS + 1,),
        in_specs=[
            full(128, 1024),
            full(2, 2, 4, 2, 32, 128),
            *weight_specs(this_part, part_before),
            full(8, 1024),
            pl.BlockSpec((1, 1, WIDTH), lambda j: (this_part(j), 0, 0)),
        ],
        out_specs=[
            full(128, 1024),
            full(128, 1024),
            full(128, 1024),
            pl.BlockSpec((128, WIDTH), lambda j: (0, this_part(j))),
            full(128, 1024),
            full(128, 1024),
        ],
        out_shape=[
            ROWS_LOW,
            ROWS_F32,
            ROWS_LOW,
            jax.ShapeDtypeStruct((128, 4096), jnp.float32),
            ROWS_F32,
            ROWS_LOW,
        ],
        scratch_shapes=[
            pltpu.VMEM((128, 1024), jnp.float32),
            pltpu.VMEM((128, 1024), jnp.float32),
            pltpu.VMEM((128, WIDTH), jnp.float32),
        ],
        compiler_params=BLOCK_PARAMS,
        cost_estimate=BLOCK_COST,
    )(tokens, context, gathered, gathered, gathered, params, hidden)
    return output, saved


def backward_kernel(
    grad,
    output_weight,
    expand_weight,
    contract_weight,
    params,
    residual,
    inner,
    second,
    grad_residual,
    grad_attn,
    grad_context,
    sums,
    grad_mlp,
    grad_second,
    total,
    before,
):
    step = pl.program_id(0)

    @pl.when(step == 0)
    def start():
        by_value, by_gain, by_shift = normed_back(
            grad[...].astype(jnp.float32), second[...], params[5:6]
        )
        grad_second[...] = by_value
        grad_mlp[...] = by_value.astype(LOW)
        sums[1:2] = by_gain
        sums[4:5] = by_shift
        total[...] = jnp.zeros_like(total)
        before[...] = jnp.zeros_like(before)

    last_part = before[...]
    before[...] = times_transposed(grad_mlp[...], contract_weight[...].reshape(WIDTH, 1024))
    grad_inner = (last_part * gelu_slope(inner[...])).astype(LOW)
    total[...] += times_transposed(grad_inner, expand_weight[...].reshape(1024, WIDTH))

    @pl.when(step == PARTS)
    def finish():
        by_value, by_gain, by_shift = normed_back(
            grad_second[...] + total[...], residual[...], params[4:5]
        )
        grad_residual[...] = by_value
        rounded = by_value.astype(LOW)
        grad_attn[...] = rounded
        rows = times_transposed(rounded, output_weight[...].reshape(1024, 1024)).astype(LOW)
        for s, m, p in ((s, m, p) for s in range(2) for m in range(2) for p in range(4)):
            piece = rows[64 * m : 64 * m + 64, 128 * (4 * s + p) : 128 * (4 * s + p) + 128]
            grad_context[s, m, p, 0] = piece
            grad_context[s, m, p, 1] = piece
        sums[0:1] = by_gain
        sums[2:3] = jnp.sum(rounded.astype(jnp.float32), 0, keepdims=True)
        sums[3:4] = by_shift
        sums[5:8] = jnp.zeros((3, 1024), jnp.float32)


def block_back(grad, saved, gathered, params):
    residual, first_low, inner, second, context_rows = saved
    return pl.pallas_call(
        backward_kernel,
        grid=(PARTS + 1,),
        in_specs=[
            full(128, 1024),
            *weight_specs(part_before, this_part),
            full(8, 1024),
            full(128, 1024),
            pl.BlockSpec((128, WIDTH), lambda j: (0, part_before(j))),
            full(128, 1024),
        ],
        out_specs=[
            full(128, 1024),
            full(128, 1024),
            full(2, 2, 4, 2, 64, 128),
            full(8, 1024),
        ],
        out_shape=[
            ROWS_F32,
            ROWS_LOW,
            jax.ShapeDtypeStruct((2, 2, 4, 2, 64, 128), LOW),
            jax.ShapeDtypeStruct((8, 1024), jnp.float32),
        ],
        scratch_shapes=[
            pltpu.VMEM((128, 1024), LOW),
            pltpu.VMEM((128, 1024), jnp.float32),
            pltpu.VMEM((128, 1024), jnp.float32),
            pltpu.VMEM((128, WIDTH), jnp.float32),
        ],
        compiler_params=BLOCK_PARAMS,
        cost_estimate=BLOCK_COST,
    )(grad, gathered, gathered, gathered, params, residual, inner, second)


def grad_tokens_kernel(got, weight, grad_residual, result, rounded, total):
    step = pl.program_id(0)
    left = jnp.concatenate([got[0, :, p].reshape(128, 384) for p in range(2)], 1)
    product = times_transposed(left, weight[...])

    @pl.when(step == 0)
    def start():
        total[...] = grad_residual[...] + product

    @pl.when(step > 0)
    def proceed():
        total[...] += product

    @pl.when(step == 3)
    def finish():
        result[...] = total[...]
        rounded[...] = total[...].astype(LOW)


def grad_tokens(got, weight, grad_residual):
    return pl.pallas_call(
        grad_tokens_kernel,
        grid=(4,),
        in_specs=[
            pl.BlockSpec((1, 2, 2, 2, 32, 384), lambda i: (i // 2, 0, i % 2, 0, 0, 0)),
            pl.BlockSpec((1024, 768), lambda i: (0, i)),
            full(128, 1024),
        ],
        out_specs=[full(128, 1024), full(128, 1024)],
        out_shape=[ROWS_F32, ROWS_LOW],
        scratch_shapes=[pltpu.VMEM((128, 1024), jnp.float32)],
        compiler_params=BLOCK_PARAMS,
        cost_estimate=pl.CostEstimate(
            flops=2 * 128 * 3072 * 1024, bytes_accessed=8 * 1024 * 1024, transcendentals=0
        ),
    )(got, weight, grad_residual)


def attend_back_kernel(
    core,
    packed,
    log_totals,
    seg_rows,
    seg_columns,
    got,
    result,
    queries,
    keys,
    values,
    grads,
    grad_keys,
    grad_values,
):
    step = pl.program_id(0)

    @pl.when(step == 0)
    def start():
        queries[...] = packed[:, :HEAD_DIM]
        keys[...] = packed[:, HEAD_DIM : 2 * HEAD_DIM]
        values[...] = packed[:, 2 * HEAD_DIM :]
        pair = got[...].reshape(1024, 128)
        grads[...] = jnp.where(core[0] == 0, pair[:, :HEAD_DIM], pair[:, HEAD_DIM:])
        grad_keys[...] = jnp.zeros_like(grad_keys)
        grad_values[...] = jnp.zeros_like(grad_values)

    rows = pl.ds(pl.multiple_of(step * 256, 256), 256)
    block_queries = queries[rows]
    block_grads = grads[rows]
    scores = times_transposed(block_queries, keys[...]) * SCALE
    scores = jnp.where(seg_rows[rows] == seg_columns[...], scores, NEGATIVE)
    soft = jnp.exp(scores - log_totals[rows])
    grad_soft = times_transposed(block_grads, values[...])
    row_total = jnp.sum(soft * grad_soft, -1, keepdims=True)
    grad_scores = (soft * (grad_soft - row_total)).astype(LOW)
    result[rows, :HEAD_DIM] = (matmul(grad_scores, keys[...]) * SCALE).astype(LOW)
    grad_keys[...] += transposed_times(grad_scores, block_queries)
    grad_values[...] += transposed_times(soft.astype(LOW), block_grads)

    @pl.when(step == 3)
    def finish():
        result[:, HEAD_DIM : 2 * HEAD_DIM] = (grad_keys[...] * SCALE).astype(LOW)
        result[:, 2 * HEAD_DIM :] = grad_values[...].astype(LOW)


def attend_back(core, packed, log_totals, seg, got, layer):
    return pl.pallas_call(
        attend_back_kernel,
        grid=(4,),
        in_specs=[
            pl.BlockSpec(memory_space=pltpu.SMEM),
            full(1024, 192),
            full(1024, 1),
            full(1024, 1),
            full(1, 1024),
            pl.BlockSpec((16, 64, 128), lambda i: (layer, 0, 0)),
        ],
        out_specs=full(1024, 192),
        out_shape=jax.ShapeDtypeStruct((1024, 192), LOW),
        scratch_shapes=[pltpu.VMEM((1024, HEAD_DIM), LOW)] * 4
        + [pltpu.VMEM((1024, HEAD_DIM), jnp.float32)] * 2,
        compiler_params=BLOCK_PARAMS,
        cost_estimate=pl.CostEstimate(
            flops=10 * 1024 * 1024 * 64, bytes_accessed=2 * 1024 * 1024, transcendentals=1 << 20
        ),
    )(core, packed, log_totals, seg[:, None], seg[None, :], got)


def with_sums(grad, sums):
    rows = jnp.concatenate([sums[None], jnp.zeros((15, sums.shape[0]), jnp.float32)], 0)
    return jnp.concatenate([grad.astype(LOW), rows.astype(LOW)], 0)


def on_device(
    inputs,
    segments,
    cotangent,
    attend_weight,
    output_weight,
    expand_weight,
    contract_weight,
    biases,
    hidden_bias,
    gains,
):
    section = lax.axis_index("section")
    shard = lax.axis_index("shard")
    on_first = section == 0
    micro = shard // 8
    head = section * 8 + shard % 8
    inputs = inputs[:, 0]

    with jax.named_scope("gather_block_weights"):
        rows = jnp.concatenate(
            [contract_weight[0], output_weight[0]] + jnp.split(expand_weight[0], 4, 1), 0
        )
        quarter = lax.dynamic_slice_in_dim(rows, lax.axis_index("replica") * 144, 144, 0)
        gathered = lax.all_gather(quarter, REST, axis=0, tiled=False).reshape(16, 576, 1024)

    with jax.named_scope("head_weights"):
        by_head = attend_weight[0].reshape(64, 3, HEADS, HEAD_DIM).transpose(2, 0, 1, 3)
        small = jnp.concatenate(
            [
                biases.reshape(384),
                gains.reshape(128),
                hidden_bias.reshape(256),
                segments.reshape(128).astype(LOW),
                jnp.zeros((16 * 192 - 896,), LOW),
            ]
        ).reshape(1, 16, 192)
        block = jnp.concatenate(
            [by_head.reshape(HEADS, 64, 192), jnp.broadcast_to(small, (HEADS, 16, 192))], 1
        )
        block = jnp.broadcast_to(block.reshape(2, 1, 8, 80, 192), (2, 2, 8, 80, 192))
        got = exchange(block.reshape(32, 80, 192), ALL).reshape(2, 16, 80, 192)
        head_weight = got[:, :, :64].reshape(2, 1024, 192)
        small = got[:, :, 64:69].reshape(2, 16, 960)
        all_biases = small[:, :, :384].reshape(2, 16, 6, 64).transpose(0, 2, 1, 3)
        all_biases = all_biases.reshape(2, 6, 1024).astype(jnp.float32)
        all_gains = small[:, :, 384:512].reshape(2, 16, 2, 64).transpose(0, 2, 1, 3)
        all_gains = all_gains.reshape(2, 2, 1024).astype(jnp.float32)
        all_hidden = small[:, :, 512:768].reshape(2, 4096).astype(jnp.float32)
        seg = small[0, :, 768:896].reshape(16, 2, 64)
        seg = jnp.where(micro == 0, seg[:, 0], seg[:, 1]).reshape(1024)
        own_biases = jnp.where(on_first, all_biases[0], all_biases[1])
        own_gains = jnp.where(on_first, all_gains[0], all_gains[1])
        own_hidden = jnp.where(on_first, all_hidden[0], all_hidden[1]).reshape(PARTS, 1, WIDTH)
        params = jnp.concatenate([own_biases[2:], own_gains, jnp.zeros((2, 1024))], 0)
        head_bias = lax.dynamic_slice_in_dim(
            all_biases.reshape(2, 6, HEADS, HEAD_DIM), head, 1, 2
        )[:, :, 0]
        head_bias = jnp.concatenate(
            [head_bias[:, 0], jnp.zeros_like(head_bias[:, 0]), head_bias[:, 1]], 1
        )

    def attention(layer, tokens):
        with jax.named_scope("sequence_tokens"):
            whole = whole_sequence(tokens)
        with jax.named_scope("attention"):
            packed = (matmul(whole, head_weight[layer]) + head_bias[layer]).astype(LOW)
            context, log_totals = attend(packed, seg)
        with jax.named_scope("context_out"):
            context = send_tokens(context, 1)
        return context, (whole, packed, log_totals)

    def attention_back(layer, grad_context, kept, beside):
        unused, packed, log_totals = kept
        with jax.named_scope("grad_context_in"):
            got = exchange(grad_context.reshape(32, 64, 128), ALL)
            got, beside = lax.optimization_barrier((got, beside))
        with jax.named_scope("attention_back"):
            core = (shard % 2).astype(jnp.int32).reshape(1)
            grad_packed = attend_back(core, packed, log_totals, seg, got, layer)
        return grad_packed, beside

    def attend_part(tokens, grad_packed):
        grad_weight = transposed_times(tokens, grad_packed)
        return with_sums(grad_weight, jnp.sum(grad_packed.astype(jnp.float32), 0))

    context_0, kept_0 = attention(0, inputs)
    tokens_0 = inputs.reshape(128, 1024)
    with jax.named_scope("block_0"):
        output, unused = block_forward(tokens_0, context_0, gathered, params, own_hidden)
    with jax.named_scope("to_next_section"):
        tokens_1 = jnp.where(
            on_first, output, lax.ppermute(output, "section", [(0, 1)])
        )
    with jax.named_scope("gather_attend_weight"):
        own_pairs = attend_weight[0].reshape(64, 3, 8, 128).transpose(0, 2, 1, 3).reshape(64, 3072)
        other_pairs = lax.ppermute(own_pairs, "section", [(0, 1), (1, 0)])
        other_pairs, output = lax.optimization_barrier((other_pairs, output))
        other_attend = lax.all_gather(other_pairs, "shard", axis=0, tiled=True)
    context_1, kept_1 = attention(1, tokens_1.reshape(2, 64, 1024))
    own_tokens = jnp.where(on_first, tokens_0, tokens_1)
    own_context = jnp.where(on_first, context_0, context_1)
    with jax.named_scope("block_1"):
        output, saved = block_forward(own_tokens, own_context, gathered, params, own_hidden)
    layer_output = output.reshape(1, 2, 1, 64, 1024)
    with jax.named_scope("gather_first"):
        first_all = lax.all_gather(saved[1], "shard", axis=0, tiled=True)

    last_grad = cotangent.reshape(128, 1024)
    with jax.named_scope("block_back_1"):
        grad_residual, unused, grad_context, unused = block_back(
            last_grad, saved, gathered, params
        )
    with jax.named_scope("residual_to_other_section"):
        arrived_1 = lax.ppermute(grad_residual, "section", [(1, 0)])
    grad_packed_1, arrived_1 = attention_back(1, grad_context, kept_1, arrived_1)
    with jax.named_scope("grad_tokens_1"):
        result_1, rounded = grad_tokens(send_tokens(grad_packed_1, 3), other_attend, arrived_1)
        grad_tokens_1 = lax.ppermute(result_1, "section", [(0, 1)])
    own_grad = jnp.where(on_first, rounded, last_grad)
    with jax.named_scope("gather_grad_mlp"):
        grad_mlp = normed_back(own_grad.astype(jnp.float32), saved[3], params[5:6])[0].astype(LOW)
        grad_mlp, own_grad = lax.optimization_barrier((grad_mlp, own_grad))
        grad_mlp_all = lax.all_gather(grad_mlp, "shard", axis=0, tiled=True)
    with jax.named_scope("block_back_0"):
        grad_residual, grad_attn, grad_context, norm_sums = block_back(
            own_grad, saved, gathered, params
        )
    with jax.named_scope("residual_to_other_section"):
        arrived_0 = lax.ppermute(grad_residual, "section", [(0, 1)])
    late_tokens, late_packed, late_gathered, grad_context = lax.optimization_barrier(
        (kept_1[0], grad_packed_1, gathered, grad_context)
    )
    with jax.named_scope("swap_attend_grad"):
        part_1 = attend_part(late_tokens, late_packed)
        take_1 = lax.ppermute(part_1, "section", [(0, 1)])
    with jax.named_scope("sum_output_grad"):
        output_grad = transposed_times(saved[4], grad_attn)
        halves = [output_grad[:, :512], output_grad[:, 512:]]
        core = shard % 2
        keep = jnp.where(core == 0, halves[0], halves[1])
        give = jnp.where(core == 0, halves[1], halves[0]).astype(LOW)
        output_grad = (keep + swap_cores(give).astype(jnp.float32)).astype(LOW)
    grad_packed, (output_grad, arrived_0, grad_tokens_1) = attention_back(
        0, grad_context, kept_0, (output_grad, arrived_0, grad_tokens_1)
    )

    with jax.named_scope("sum_output_grad"):
        output_got = exchange(output_grad.reshape(64, 16, 512), REST)
        output_got, grad_packed = lax.optimization_barrier((output_got, grad_packed))
    with jax.named_scope("swap_attend_grad"):
        part_0 = attend_part(kept_0[0], grad_packed)
        take_0 = lax.ppermute(part_0, "section", [(1, 0)])
        lower = jnp.where(on_first, part_0, take_1)
        upper = jnp.where(on_first, take_0, part_1)
        attend_grad = jnp.concatenate([lower[:1024], upper[:1024]], 1)
        sums = jnp.stack([lower[1024], upper[1024]]).reshape(2, 3, HEAD_DIM)
        norm_rows = norm_sums[:5].reshape(5, 16, 64).transpose(1, 0, 2)
        mine = jnp.arange(8) == shard % 8
        head_rows = jnp.where(
            mine[None, :, None, None], sums[:, None, ::2].astype(jnp.float32), 0.0
        ).reshape(16, 2, 64)
        vectors = jnp.pad(
            jnp.concatenate([norm_rows, head_rows], 1), ((0, 0), (0, 9), (0, 64))
        )
        vectors = jnp.broadcast_to(vectors[:, None], (16, 4, 16, 128)).reshape(1024, 128)
        vectors = vectors.astype(LOW)
    with jax.named_scope("block_weight_grads"):
        expand_part = lax.dynamic_slice(
            late_gathered, (0, 320 + shard // 4 * 64, shard % 4 * 256), (16, 64, 256)
        ).reshape(1024, 256)
        hidden_part = lax.dynamic_slice_in_dim(own_hidden.reshape(4096), shard * 256, 256, 0)
        inner = matmul(first_all, expand_part) + hidden_part
        activation = inner * gelu_share(inner)
        grad_inner = times_transposed(grad_mlp_all, contract_weight[0]) * gelu_slope(inner)
        grad_inner = grad_inner.astype(LOW)
        expand_grad = transposed_times(first_all, grad_inner).astype(LOW)
        contract_grad = transposed_times(activation.astype(LOW), grad_mlp_all).astype(LOW)
        hidden_sum = jnp.sum(grad_inner.astype(jnp.float32), 0)
        mlp_sum = jnp.sum(grad_mlp_all.astype(jnp.float32), 0)
        extra = jnp.concatenate(
            [
                jnp.concatenate([hidden_sum, jnp.zeros((768,), jnp.float32)])[None],
                mlp_sum[None],
                jnp.zeros((14, 1024), jnp.float32),
            ],
            0,
        ).astype(LOW)
        rows = jnp.concatenate(
            [contract_grad.reshape(4, 64, 1024), jnp.broadcast_to(extra, (4, 16, 1024))], 1
        )
    with jax.named_scope("sum_attend_expand_grads"):
        attend_grad, expand_grad, vectors, rows = lax.optimization_barrier(
            (attend_grad, expand_grad, vectors, rows)
        )
        parts = jnp.concatenate([attend_grad, expand_grad, vectors], 1)
        got = exchange(parts.reshape(64, 16, 768), REST)
        got, rows = lax.optimization_barrier((got, rows))
    with jax.named_scope("sum_contract"):
        got_contract = exchange(rows, "replica").astype(jnp.float32).sum(0)
    with jax.named_scope("sum_attend_grad"):
        got_output = output_got.astype(jnp.float32).reshape(8, 2, 4, 16, 512).sum((0, 2))
        got_output = jnp.concatenate([got_output[0], got_output[1]], 1).astype(LOW)
        got_attend = got[:, :, :384].astype(jnp.float32).reshape(2, 8, 4, 16, 384).sum((0, 2))
        got_expand = got[:, :, 384:640].astype(jnp.float32).reshape(16, 4, 16, 256).sum(1)
        got_expand = got_expand.astype(LOW).transpose(1, 0, 2).reshape(16, 4096)
        got_vectors = got[:, :7, 640:704].astype(jnp.float32).sum(0)
        got_attend, got_output = lax.optimization_barrier((got_attend.astype(LOW), got_output))
        got_attend = got_attend.reshape(8, 16, 2, 3, 64).transpose(1, 3, 2, 0, 4)
        got_attend = got_attend.reshape(16, 3072)
    with jax.named_scope("gather_weight_grads"):
        contract_rows = got_contract[:64].astype(LOW).reshape(4, 16, 1024)
        owned = jnp.concatenate([got_attend, got_output, got_expand, *contract_rows], 1)
    with jax.named_scope("grad_tokens_0"):
        late_packed, owned = lax.optimization_barrier((grad_packed, owned))
        result_0, unused = grad_tokens(send_tokens(late_packed, 3), other_attend, arrived_0)
        grad_tokens_0 = lax.ppermute(result_0, "section", [(1, 0)])
    with jax.named_scope("gather_weight_grads"):
        totals = lax.all_gather(owned, "replica", axis=0, tiled=True)
        contract_total = totals[:, 8192:].reshape(4, 16, 4, 1024).transpose(0, 2, 1, 3)
        contract_total = contract_total.reshape(1, 256, 1024).astype(jnp.float32)
        totals = totals[None, :, :8192].astype(jnp.float32)
    attend_total = totals[:, :, :3072]
    output_total = totals[:, :, 3072:4096]
    expand_total = totals[:, :, 4096:]
    grad_tokens_0, attend_total, output_total, expand_total, contract_total = (
        lax.optimization_barrier(
            (grad_tokens_0, attend_total, output_total, expand_total, contract_total)
        )
    )
    input_grad = jnp.where(on_first, grad_tokens_0, grad_tokens_1).reshape(1, 2, 1, 64, 1024)
    mlp_own = lax.dynamic_slice_in_dim(got_contract[65], shard * 64, 64, 0)
    biases_grad = jnp.stack(
        [
            got_vectors[5],
            got_vectors[6],
            got_vectors[2],
            got_vectors[3],
            mlp_own,
            got_vectors[4],
        ]
    )
    return (
        layer_output,
        input_grad,
        attend_total,
        output_total,
        expand_total,
        contract_total,
        biases_grad[None],
        got_contract[None, 64, :256],
        got_vectors[None, :2],
    )


def solution(mesh):
    placed = (
        P(None, "replica", "shard", None),
        P(None, "replica", "shard"),
        P(None, "replica", "shard", None),
        P("section", "shard", None),
        P("section", "shard", None),
        P("section", "shard", None),
        P("section", "shard", None),
        P("section", None, "shard"),
        P("section", "shard"),
        P("section", None, "shard"),
    )
    return jax.shard_map(
        on_device,
        mesh=mesh,
        in_specs=placed,
        out_specs=(
            P("section", None, "replica", "shard", None),
            P("section", None, "replica", "shard", None),
            P("section", "shard", None),
            P("section", "shard", None),
            P("section", "shard", None),
            P("section", "shard", None),
            P("section", None, "shard"),
            P("section", "shard"),
            P("section", None, "shard"),
        ),
        check_vma=False,
    )
```

```python
import math

import jax
import jax.numpy as jnp
from jax import lax
from jax.experimental import pallas as pl
from jax.experimental.pallas import tpu as pltpu
from jax.sharding import PartitionSpec as P

HEADS = 16
HEAD_DIM = 64
NEGATIVE = -1e30
EPSILON = 1e-05
SCALE = 1.0 / math.sqrt(HEAD_DIM)
LOW = jnp.bfloat16
ALL = ("section", "shard")
REST = ("shard", "replica")


def matmul(left, right):
    return jnp.dot(left, right, preferred_element_type=jnp.float32)


def times_transposed(left, right):
    return lax.dot_general(
        left, right, (((1,), (1,)), ((), ())), preferred_element_type=jnp.float32
    )


def transposed_times(left, right):
    return lax.dot_general(
        left, right, (((0,), (0,)), ((), ())), preferred_element_type=jnp.float32
    )


def exchange(value, axes):
    return lax.all_to_all(value, axes, 0, 0, tiled=True)


def swap_cores(value):
    return lax.ppermute(value, "shard", [(i, i ^ 1) for i in range(16)])


def whole_sequence(tokens):
    core = lax.axis_index("shard") % 2
    micros, rows, features = tokens.shape
    half = rows // 2
    sends = jnp.broadcast_to(
        tokens.reshape(micros, 1, 2, half, features), (micros, 4, 2, half, features)
    ).reshape(16, half, features)
    mine = exchange(sends, "shard")
    other = swap_cores(mine)
    lower = jnp.where(core == 0, mine, other)
    upper = jnp.where(core == 0, other, mine)
    return jnp.stack([lower, upper], 1).reshape(16 * rows, features)


def send_tokens(value, parts):
    core = lax.axis_index("shard") % 2
    width = parts * HEAD_DIM
    halves = value.reshape(16, 2, 32, width)
    keep = jnp.where(core == 0, halves[:, 0], halves[:, 1])
    take = swap_cores(jnp.where(core == 0, halves[:, 1], halves[:, 0]))
    lower = jnp.split(jnp.where(core == 0, keep, take), parts, 2)
    upper = jnp.split(jnp.where(core == 0, take, keep), parts, 2)
    pair = jnp.concatenate([piece for both in zip(lower, upper) for piece in both], 2)
    sends = jnp.broadcast_to(pair[None], (2, 16, 32, 2 * width)).reshape(32, 32, 2 * width)
    return exchange(sends, ALL).reshape(2, 2, 4, 2, 32, 2 * width)


def masked_scores(queries, keys, seg):
    scores = times_transposed(queries, keys) * SCALE
    return jnp.where(seg[:, None] == seg[None, :], scores, NEGATIVE)


def attend(packed, seg):
    queries, keys, values = jnp.split(packed, 3, 1)
    scores = masked_scores(queries, keys, seg)
    highest = jnp.max(scores, -1, keepdims=True)
    exponent = jnp.exp(scores - highest)
    totals = jnp.sum(exponent, -1, keepdims=True)
    context = matmul((exponent / totals).astype(LOW), values).astype(LOW)
    return context, highest + jnp.log(totals)


def normed(value):
    mean_value = jnp.mean(value, -1, keepdims=True)
    centred = value - mean_value
    spread = jnp.mean(centred * centred, -1, keepdims=True)
    scale = lax.rsqrt(spread + EPSILON)
    return centred * scale, scale


def normed_back(grad, value, gain):
    unit, scale = normed(value)
    weighted = grad * gain
    inner_mean = jnp.mean(weighted * unit, -1, keepdims=True)
    grad_value = scale * (weighted - jnp.mean(weighted, -1, keepdims=True) - unit * inner_mean)
    return (
        grad_value,
        jnp.sum(grad * unit, 0, keepdims=True),
        jnp.sum(grad, 0, keepdims=True),
    )


def gelu_share(value):
    return 0.5 * (1.0 + lax.erf(value * math.sqrt(0.5)))


def gelu_slope(value):
    return gelu_share(value) + value * jnp.exp(-0.5 * value * value) * (0.5 / math.pi) ** 0.5


PARTS = 4
WIDTH = 1024


def this_part(j):
    return jnp.minimum(j, PARTS - 1)


def part_before(j):
    return jnp.maximum(j - 1, 0)


def weight_specs(expand_at, contract_at):
    return [
        pl.BlockSpec((16, 64, 1024), lambda j: (0, 4, 0)),
        pl.BlockSpec((16, 64, WIDTH), lambda j: (0, 5 + expand_at(j), 0)),
        pl.BlockSpec((4, 256, 1024), lambda j: (contract_at(j), 0, 0)),
    ]


def full(*shape):
    return pl.BlockSpec(shape, lambda j: (0,) * len(shape))


ROWS_F32 = jax.ShapeDtypeStruct((128, 1024), jnp.float32)
ROWS_LOW = jax.ShapeDtypeStruct((128, 1024), LOW)
BLOCK_PARAMS = pltpu.CompilerParams(
    dimension_semantics=("arbitrary",), vmem_limit_bytes=48 * 1024 * 1024
)
BLOCK_COST = pl.CostEstimate(
    flops=2 * 128 * 1024 * 9216, bytes_accessed=24 * 1024 * 1024, transcendentals=128 * 4096
)


def forward_kernel(
    tokens,
    context,
    output_weight,
    expand_weight,
    contract_weight,
    params,
    hidden,
    output,
    residual,
    first_low,
    inner,
    second,
    context_rows,
    first,
    total,
    before,
):
    step = pl.program_id(0)

    @pl.when(step == 0)
    def start():
        pairs = [context[s, :, p].reshape(128, 128) for s in range(2) for p in range(4)]
        rows = jnp.concatenate(pairs, 1)
        context_rows[...] = rows
        attention = matmul(rows, output_weight[...].reshape(1024, 1024))
        summed = tokens[...].astype(jnp.float32) + (attention + params[0:1])
        residual[...] = summed
        after = normed(summed)[0] * params[4:5] + params[1:2]
        first[...] = after
        first_low[...] = after.astype(LOW)
        total[...] = jnp.zeros_like(total)
        before[...] = jnp.zeros_like(before)

    last_part = before[...]
    inner_part = matmul(first_low[...], expand_weight[...].reshape(1024, WIDTH)) + hidden[0]
    inner[...] = inner_part
    activation = (last_part * gelu_share(last_part)).astype(LOW)
    total[...] += matmul(activation, contract_weight[...].reshape(WIDTH, 1024))
    before[...] = inner_part

    @pl.when(step == PARTS)
    def finish():
        summed = first[...] + (total[...] + params[2:3])
        second[...] = summed
        output[...] = (normed(summed)[0] * params[5:6] + params[3:4]).astype(LOW)


def block_forward(tokens, context, gathered, params, hidden):
    output, *saved = pl.pallas_call(
        forward_kernel,
        grid=(PARTS + 1,),
        in_specs=[
            full(128, 1024),
            full(2, 2, 4, 2, 32, 128),
            *weight_specs(this_part, part_before),
            full(8, 1024),
            pl.BlockSpec((1, 1, WIDTH), lambda j: (this_part(j), 0, 0)),
        ],
        out_specs=[
            full(128, 1024),
            full(128, 1024),
            full(128, 1024),
            pl.BlockSpec((128, WIDTH), lambda j: (0, this_part(j))),
            full(128, 1024),
            full(128, 1024),
        ],
        out_shape=[
            ROWS_LOW,
            ROWS_F32,
            ROWS_LOW,
            jax.ShapeDtypeStruct((128, 4096), jnp.float32),
            ROWS_F32,
            ROWS_LOW,
        ],
        scratch_shapes=[
            pltpu.VMEM((128, 1024), jnp.float32),
            pltpu.VMEM((128, 1024), jnp.float32),
            pltpu.VMEM((128, WIDTH), jnp.float32),
        ],
        compiler_params=BLOCK_PARAMS,
        cost_estimate=BLOCK_COST,
    )(tokens, context, gathered, gathered, gathered, params, hidden)
    return output, saved


def backward_kernel(
    grad,
    output_weight,
    expand_weight,
    contract_weight,
    params,
    residual,
    inner,
    second,
    grad_residual,
    grad_attn,
    grad_context,
    sums,
    grad_mlp,
    grad_second,
    total,
    before,
):
    step = pl.program_id(0)

    @pl.when(step == 0)
    def start():
        by_value, by_gain, by_shift = normed_back(
            grad[...].astype(jnp.float32), second[...], params[5:6]
        )
        grad_second[...] = by_value
        grad_mlp[...] = by_value.astype(LOW)
        sums[1:2] = by_gain
        sums[4:5] = by_shift
        total[...] = jnp.zeros_like(total)
        before[...] = jnp.zeros_like(before)

    last_part = before[...]
    before[...] = times_transposed(grad_mlp[...], contract_weight[...].reshape(WIDTH, 1024))
    grad_inner = (last_part * gelu_slope(inner[...])).astype(LOW)
    total[...] += times_transposed(grad_inner, expand_weight[...].reshape(1024, WIDTH))

    @pl.when(step == PARTS)
    def finish():
        by_value, by_gain, by_shift = normed_back(
            grad_second[...] + total[...], residual[...], params[4:5]
        )
        grad_residual[...] = by_value
        rounded = by_value.astype(LOW)
        grad_attn[...] = rounded
        rows = times_transposed(rounded, output_weight[...].reshape(1024, 1024)).astype(LOW)
        for s, m, p in ((s, m, p) for s in range(2) for m in range(2) for p in range(4)):
            piece = rows[64 * m : 64 * m + 64, 128 * (4 * s + p) : 128 * (4 * s + p) + 128]
            grad_context[s, m, p, 0] = piece
            grad_context[s, m, p, 1] = piece
        sums[0:1] = by_gain
        sums[2:3] = jnp.sum(rounded.astype(jnp.float32), 0, keepdims=True)
        sums[3:4] = by_shift
        sums[5:8] = jnp.zeros((3, 1024), jnp.float32)


def block_back(grad, saved, gathered, params):
    residual, first_low, inner, second, context_rows = saved
    return pl.pallas_call(
        backward_kernel,
        grid=(PARTS + 1,),
        in_specs=[
            full(128, 1024),
            *weight_specs(part_before, this_part),
            full(8, 1024),
            full(128, 1024),
            pl.BlockSpec((128, WIDTH), lambda j: (0, part_before(j))),
            full(128, 1024),
        ],
        out_specs=[
            full(128, 1024),
            full(128, 1024),
            full(2, 2, 4, 2, 64, 128),
            full(8, 1024),
        ],
        out_shape=[
            ROWS_F32,
            ROWS_LOW,
            jax.ShapeDtypeStruct((2, 2, 4, 2, 64, 128), LOW),
            jax.ShapeDtypeStruct((8, 1024), jnp.float32),
        ],
        scratch_shapes=[
            pltpu.VMEM((128, 1024), LOW),
            pltpu.VMEM((128, 1024), jnp.float32),
            pltpu.VMEM((128, 1024), jnp.float32),
            pltpu.VMEM((128, WIDTH), jnp.float32),
        ],
        compiler_params=BLOCK_PARAMS,
        cost_estimate=BLOCK_COST,
    )(grad, gathered, gathered, gathered, params, residual, inner, second)


def grad_tokens_kernel(got, weight, grad_residual, rounded, total):
    step = pl.program_id(0)
    left = jnp.concatenate([got[0, :, p].reshape(128, 384) for p in range(2)], 1)
    product = times_transposed(left, weight[...])

    @pl.when(step == 0)
    def start():
        total[...] = grad_residual[...] + product

    @pl.when(step > 0)
    def proceed():
        total[...] += product

    @pl.when(step == 3)
    def finish():
        rounded[...] = total[...].astype(LOW)


def grad_tokens(got, weight, grad_residual):
    return pl.pallas_call(
        grad_tokens_kernel,
        grid=(4,),
        in_specs=[
            pl.BlockSpec((1, 2, 2, 2, 32, 384), lambda i: (i // 2, 0, i % 2, 0, 0, 0)),
            pl.BlockSpec((1024, 768), lambda i: (0, i)),
            full(128, 1024),
        ],
        out_specs=full(128, 1024),
        out_shape=ROWS_LOW,
        scratch_shapes=[pltpu.VMEM((128, 1024), jnp.float32)],
        compiler_params=BLOCK_PARAMS,
        cost_estimate=pl.CostEstimate(
            flops=2 * 128 * 3072 * 1024, bytes_accessed=8 * 1024 * 1024, transcendentals=0
        ),
    )(got, weight, grad_residual)


def attend_back_kernel(
    core,
    packed,
    log_totals,
    seg_rows,
    seg_columns,
    got,
    result,
    queries,
    keys,
    values,
    grads,
    grad_keys,
    grad_values,
):
    step = pl.program_id(0)

    @pl.when(step == 0)
    def start():
        queries[...] = packed[:, :HEAD_DIM]
        keys[...] = packed[:, HEAD_DIM : 2 * HEAD_DIM]
        values[...] = packed[:, 2 * HEAD_DIM :]
        pair = got[...].reshape(1024, 128)
        grads[...] = jnp.where(core[0] == 0, pair[:, :HEAD_DIM], pair[:, HEAD_DIM:])
        grad_keys[...] = jnp.zeros_like(grad_keys)
        grad_values[...] = jnp.zeros_like(grad_values)

    rows = pl.ds(pl.multiple_of(step * 256, 256), 256)
    block_queries = queries[rows]
    block_grads = grads[rows]
    scores = times_transposed(block_queries, keys[...]) * SCALE
    scores = jnp.where(seg_rows[rows] == seg_columns[...], scores, NEGATIVE)
    soft = jnp.exp(scores - log_totals[rows])
    grad_soft = times_transposed(block_grads, values[...])
    row_total = jnp.sum(soft * grad_soft, -1, keepdims=True)
    grad_scores = (soft * (grad_soft - row_total)).astype(LOW)
    result[rows, :HEAD_DIM] = (matmul(grad_scores, keys[...]) * SCALE).astype(LOW)
    grad_keys[...] += transposed_times(grad_scores, block_queries)
    grad_values[...] += transposed_times(soft.astype(LOW), block_grads)

    @pl.when(step == 3)
    def finish():
        result[:, HEAD_DIM : 2 * HEAD_DIM] = (grad_keys[...] * SCALE).astype(LOW)
        result[:, 2 * HEAD_DIM :] = grad_values[...].astype(LOW)


def attend_back(core, packed, log_totals, seg, got, layer):
    return pl.pallas_call(
        attend_back_kernel,
        grid=(4,),
        in_specs=[
            pl.BlockSpec(memory_space=pltpu.SMEM),
            full(1024, 192),
            full(1024, 1),
            full(1024, 1),
            full(1, 1024),
            pl.BlockSpec((16, 64, 128), lambda i: (layer, 0, 0)),
        ],
        out_specs=full(1024, 192),
        out_shape=jax.ShapeDtypeStruct((1024, 192), LOW),
        scratch_shapes=[pltpu.VMEM((1024, HEAD_DIM), LOW)] * 4
        + [pltpu.VMEM((1024, HEAD_DIM), jnp.float32)] * 2,
        compiler_params=BLOCK_PARAMS,
        cost_estimate=pl.CostEstimate(
            flops=10 * 1024 * 1024 * 64, bytes_accessed=2 * 1024 * 1024, transcendentals=1 << 20
        ),
    )(core, packed, log_totals, seg[:, None], seg[None, :], got)


def with_sums(grad, sums):
    rows = jnp.concatenate([sums[None], jnp.zeros((15, sums.shape[0]), jnp.float32)], 0)
    return jnp.concatenate([grad.astype(LOW), rows.astype(LOW)], 0)


def on_device(
    inputs,
    segments,
    cotangent,
    attend_weight,
    output_weight,
    expand_weight,
    contract_weight,
    biases,
    hidden_bias,
    gains,
):
    section = lax.axis_index("section")
    shard = lax.axis_index("shard")
    on_first = section == 0
    micro = shard // 8
    head = section * 8 + shard % 8
    inputs = inputs[:, 0]

    with jax.named_scope("gather_block_weights"):
        rows = jnp.concatenate(
            [contract_weight[0], output_weight[0]] + jnp.split(expand_weight[0], 4, 1), 0
        )
        quarter = lax.dynamic_slice_in_dim(rows, lax.axis_index("replica") * 144, 144, 0)
        gathered = lax.all_gather(quarter, REST, axis=0, tiled=False).reshape(16, 576, 1024)

    with jax.named_scope("head_weights"):
        by_head = attend_weight[0].reshape(64, 3, HEADS, HEAD_DIM).transpose(2, 0, 1, 3)
        small = jnp.concatenate(
            [
                biases.reshape(384),
                gains.reshape(128),
                hidden_bias.reshape(256),
                segments.reshape(128).astype(LOW),
                jnp.zeros((16 * 192 - 896,), LOW),
            ]
        ).reshape(1, 16, 192)
        block = jnp.concatenate(
            [by_head.reshape(HEADS, 64, 192), jnp.broadcast_to(small, (HEADS, 16, 192))], 1
        )
        block = jnp.broadcast_to(block.reshape(2, 1, 8, 80, 192), (2, 2, 8, 80, 192))
        got = exchange(block.reshape(32, 80, 192), ALL).reshape(2, 16, 80, 192)
        head_weight = got[:, :, :64].reshape(2, 1024, 192)
        small = got[:, :, 64:69].reshape(2, 16, 960)
        all_biases = small[:, :, :384].reshape(2, 16, 6, 64).transpose(0, 2, 1, 3)
        all_biases = all_biases.reshape(2, 6, 1024).astype(jnp.float32)
        all_gains = small[:, :, 384:512].reshape(2, 16, 2, 64).transpose(0, 2, 1, 3)
        all_gains = all_gains.reshape(2, 2, 1024).astype(jnp.float32)
        all_hidden = small[:, :, 512:768].reshape(2, 4096).astype(jnp.float32)
        seg = small[0, :, 768:896].reshape(16, 2, 64)
        seg = jnp.where(micro == 0, seg[:, 0], seg[:, 1]).reshape(1024)
        own_biases = jnp.where(on_first, all_biases[0], all_biases[1])
        own_gains = jnp.where(on_first, all_gains[0], all_gains[1])
        own_hidden = jnp.where(on_first, all_hidden[0], all_hidden[1]).reshape(PARTS, 1, WIDTH)
        params = jnp.concatenate([own_biases[2:], own_gains, jnp.zeros((2, 1024))], 0)
        head_bias = lax.dynamic_slice_in_dim(
            all_biases.reshape(2, 6, HEADS, HEAD_DIM), head, 1, 2
        )[:, :, 0]
        head_bias = jnp.concatenate(
            [head_bias[:, 0], jnp.zeros_like(head_bias[:, 0]), head_bias[:, 1]], 1
        )

    def attention(layer, tokens):
        with jax.named_scope("sequence_tokens"):
            whole = whole_sequence(tokens)
        with jax.named_scope("attention"):
            packed = (matmul(whole, head_weight[layer]) + head_bias[layer]).astype(LOW)
            context, log_totals = attend(packed, seg)
        with jax.named_scope("context_out"):
            context = send_tokens(context, 1)
        return context, (whole, packed, log_totals)

    def attention_back(layer, grad_context, kept, beside):
        unused, packed, log_totals = kept
        with jax.named_scope("grad_context_in"):
            got = exchange(grad_context.reshape(32, 64, 128), ALL)
            got, beside = lax.optimization_barrier((got, beside))
        with jax.named_scope("attention_back"):
            core = (shard % 2).astype(jnp.int32).reshape(1)
            grad_packed = attend_back(core, packed, log_totals, seg, got, layer)
        return grad_packed, beside

    def attend_part(tokens, grad_packed):
        grad_weight = transposed_times(tokens, grad_packed)
        return with_sums(grad_weight, jnp.sum(grad_packed.astype(jnp.float32), 0))

    context_0, kept_0 = attention(0, inputs)
    tokens_0 = inputs.reshape(128, 1024)
    with jax.named_scope("block_0"):
        output, unused = block_forward(tokens_0, context_0, gathered, params, own_hidden)
    with jax.named_scope("to_next_section"):
        tokens_1 = jnp.where(
            on_first, output, lax.ppermute(output, "section", [(0, 1)])
        )
    with jax.named_scope("gather_attend_weight"):
        own_pairs = attend_weight[0].reshape(64, 3, 8, 128).transpose(0, 2, 1, 3).reshape(64, 3072)
        other_pairs = lax.ppermute(own_pairs, "section", [(0, 1), (1, 0)])
        other_pairs, output = lax.optimization_barrier((other_pairs, output))
        other_attend = lax.all_gather(other_pairs, "shard", axis=0, tiled=True)
    context_1, kept_1 = attention(1, tokens_1.reshape(2, 64, 1024))
    own_tokens = jnp.where(on_first, tokens_0, tokens_1)
    own_context = jnp.where(on_first, context_0, context_1)
    with jax.named_scope("block_1"):
        output, saved = block_forward(own_tokens, own_context, gathered, params, own_hidden)
    layer_output = output.reshape(1, 2, 1, 64, 1024)
    with jax.named_scope("gather_first"):
        first_all = lax.all_gather(saved[1], "shard", axis=0, tiled=True)

    last_grad = cotangent.reshape(128, 1024)
    with jax.named_scope("block_back_1"):
        grad_residual, unused, grad_context, unused = block_back(
            last_grad, saved, gathered, params
        )
    with jax.named_scope("residual_to_other_section"):
        arrived_1 = lax.ppermute(grad_residual, "section", [(1, 0)])
    grad_packed_1, arrived_1 = attention_back(1, grad_context, kept_1, arrived_1)
    with jax.named_scope("grad_tokens_1"):
        rounded = grad_tokens(send_tokens(grad_packed_1, 3), other_attend, arrived_1)
        grad_tokens_1 = lax.ppermute(rounded, "section", [(0, 1)])
    own_grad = jnp.where(on_first, rounded, last_grad)
    with jax.named_scope("gather_grad_mlp"):
        grad_mlp = normed_back(own_grad.astype(jnp.float32), saved[3], params[5:6])[0].astype(LOW)
        grad_mlp, own_grad = lax.optimization_barrier((grad_mlp, own_grad))
        grad_mlp_all = lax.all_gather(grad_mlp, "shard", axis=0, tiled=True)
    with jax.named_scope("block_back_0"):
        grad_residual, grad_attn, grad_context, norm_sums = block_back(
            own_grad, saved, gathered, params
        )
    with jax.named_scope("residual_to_other_section"):
        arrived_0 = lax.ppermute(grad_attn, "section", [(0, 1)])
    late_tokens, late_packed, late_gathered, grad_context = lax.optimization_barrier(
        (kept_1[0], grad_packed_1, gathered, grad_context)
    )
    with jax.named_scope("swap_attend_grad"):
        part_1 = attend_part(late_tokens, late_packed)
        take_1 = lax.ppermute(part_1, "section", [(0, 1)])
    with jax.named_scope("sum_output_grad"):
        output_grad = transposed_times(saved[4], grad_attn)
        halves = [output_grad[:, :512], output_grad[:, 512:]]
        core = shard % 2
        keep = jnp.where(core == 0, halves[0], halves[1])
        give = jnp.where(core == 0, halves[1], halves[0]).astype(LOW)
        output_grad = (keep + swap_cores(give).astype(jnp.float32)).astype(LOW)
    grad_packed, output_grad = attention_back(0, grad_context, kept_0, output_grad)

    with jax.named_scope("sum_output_grad"):
        output_got = exchange(output_grad.reshape(64, 16, 512), REST)
        output_got, grad_packed = lax.optimization_barrier((output_got, grad_packed))
    with jax.named_scope("swap_attend_grad"):
        part_0 = attend_part(kept_0[0], grad_packed)
        take_0 = lax.ppermute(part_0, "section", [(1, 0)])
        lower = jnp.where(on_first, part_0, take_1)
        upper = jnp.where(on_first, take_0, part_1)
        attend_grad = jnp.concatenate([lower[:1024], upper[:1024]], 1)
        sums = jnp.stack([lower[1024], upper[1024]]).reshape(2, 3, HEAD_DIM)
        norm_rows = norm_sums[:5].reshape(5, 16, 64).transpose(1, 0, 2)
        mine = jnp.arange(8) == shard % 8
        head_rows = jnp.where(
            mine[None, :, None, None], sums[:, None, ::2].astype(jnp.float32), 0.0
        ).reshape(16, 2, 64)
        vectors = jnp.pad(
            jnp.concatenate([norm_rows, head_rows], 1), ((0, 0), (0, 9), (0, 64))
        )
        vectors = jnp.broadcast_to(vectors[:, None], (16, 4, 16, 128)).reshape(1024, 128)
        vectors = vectors.astype(LOW)
    with jax.named_scope("sum_attend_grad"):
        parts = jnp.concatenate([attend_grad, vectors], 1)
        got = exchange(parts.reshape(64, 16, 512), REST)
    with jax.named_scope("block_weight_grads"):
        expand_part = lax.dynamic_slice(
            late_gathered, (0, 320 + shard // 4 * 64, shard % 4 * 256), (16, 64, 256)
        ).reshape(1024, 256)
        hidden_part = lax.dynamic_slice_in_dim(own_hidden.reshape(4096), shard * 256, 256, 0)
        inner = matmul(first_all, expand_part) + hidden_part
        activation = inner * gelu_share(inner)
        grad_inner = times_transposed(grad_mlp_all, contract_weight[0]) * gelu_slope(inner)
        grad_inner = grad_inner.astype(LOW)
        expand_grad = transposed_times(first_all, grad_inner).astype(LOW)
        contract_grad = transposed_times(activation.astype(LOW), grad_mlp_all).astype(LOW)
        hidden_sum = jnp.sum(grad_inner.astype(jnp.float32), 0)
        mlp_sum = jnp.sum(grad_mlp_all.astype(jnp.float32), 0)
        extra = jnp.concatenate(
            [
                jnp.concatenate([hidden_sum, jnp.zeros((768,), jnp.float32)])[None],
                mlp_sum[None],
                jnp.zeros((14, 1024), jnp.float32),
            ],
            0,
        ).astype(LOW)
        rows = jnp.concatenate(
            [contract_grad.reshape(4, 64, 1024), jnp.broadcast_to(extra, (4, 16, 1024))], 1
        )
    with jax.named_scope("sum_expand_grad"):
        got, expand_grad, rows, arrived_0, grad_tokens_1 = lax.optimization_barrier(
            (got, expand_grad, rows, arrived_0, grad_tokens_1)
        )
        expand_got = exchange(expand_grad.reshape(64, 16, 256), REST)
        expand_got, rows = lax.optimization_barrier((expand_got, rows))
    with jax.named_scope("sum_contract"):
        got_contract = exchange(rows, "replica").astype(jnp.float32).sum(0)
    with jax.named_scope("sum_attend_grad"):
        got_output = output_got.astype(jnp.float32).reshape(8, 2, 4, 16, 512).sum((0, 2))
        got_output = jnp.concatenate([got_output[0], got_output[1]], 1).astype(LOW)
        got_attend = got[:, :, :384].astype(jnp.float32).reshape(2, 8, 4, 16, 384).sum((0, 2))
        got_expand = expand_got.astype(jnp.float32).reshape(16, 4, 16, 256).sum(1)
        got_expand = got_expand.astype(LOW).transpose(1, 0, 2).reshape(16, 4096)
        got_vectors = got[:, :7, 384:448].astype(jnp.float32).sum(0)
        got_attend, got_output = lax.optimization_barrier((got_attend.astype(LOW), got_output))
        got_attend = got_attend.reshape(8, 16, 2, 3, 64).transpose(1, 3, 2, 0, 4)
        got_attend = got_attend.reshape(16, 3072)
    with jax.named_scope("gather_weight_grads"):
        contract_rows = got_contract[:64].astype(LOW).reshape(4, 16, 1024)
        owned = jnp.concatenate([got_attend, got_output, got_expand, *contract_rows], 1)
    with jax.named_scope("grad_tokens_0"):
        late_packed, owned = lax.optimization_barrier((grad_packed, owned))
        rounded = grad_tokens(
            send_tokens(late_packed, 3), other_attend, arrived_0.astype(jnp.float32)
        )
        grad_tokens_0 = lax.ppermute(rounded, "section", [(1, 0)])
    with jax.named_scope("gather_weight_grads"):
        totals = lax.all_gather(owned, "replica", axis=0, tiled=True)
        contract_total = totals[:, 8192:].reshape(4, 16, 4, 1024).transpose(0, 2, 1, 3)
        contract_total = contract_total.reshape(1, 256, 1024).astype(jnp.float32)
        totals = totals[None, :, :8192].astype(jnp.float32)
    attend_total = totals[:, :, :3072]
    output_total = totals[:, :, 3072:4096]
    expand_total = totals[:, :, 4096:]
    grad_tokens_0, attend_total, output_total, expand_total, contract_total = (
        lax.optimization_barrier(
            (grad_tokens_0, attend_total, output_total, expand_total, contract_total)
        )
    )
    input_grad = jnp.where(on_first, grad_tokens_0, grad_tokens_1).astype(jnp.float32)
    input_grad = input_grad.reshape(1, 2, 1, 64, 1024)
    mlp_own = lax.dynamic_slice_in_dim(got_contract[65], shard * 64, 64, 0)
    biases_grad = jnp.stack(
        [
            got_vectors[5],
            got_vectors[6],
            got_vectors[2],
            got_vectors[3],
            mlp_own,
            got_vectors[4],
        ]
    )
    return (
        layer_output,
        input_grad,
        attend_total,
        output_total,
        expand_total,
        contract_total,
        biases_grad[None],
        got_contract[None, 64, :256],
        got_vectors[None, :2],
    )


def solution(mesh):
    placed = (
        P(None, "replica", "shard", None),
        P(None, "replica", "shard"),
        P(None, "replica", "shard", None),
        P("section", "shard", None),
        P("section", "shard", None),
        P("section", "shard", None),
        P("section", "shard", None),
        P("section", None, "shard"),
        P("section", "shard"),
        P("section", None, "shard"),
    )
    return jax.shard_map(
        on_device,
        mesh=mesh,
        in_specs=placed,
        out_specs=(
            P("section", None, "replica", "shard", None),
            P("section", None, "replica", "shard", None),
            P("section", "shard", None),
            P("section", "shard", None),
            P("section", "shard", None),
            P("section", "shard", None),
            P("section", None, "shard"),
            P("section", "shard"),
            P("section", None, "shard"),
        ),
        check_vma=False,
    )
```

```python
import math

import jax
import jax.numpy as jnp
from jax import lax
from jax.experimental import pallas as pl
from jax.experimental.pallas import tpu as pltpu
from jax.sharding import PartitionSpec as P

HEADS = 16
HEAD_DIM = 64
NEGATIVE = -1e30
EPSILON = 1e-05
SCALE = 1.0 / math.sqrt(HEAD_DIM)
LOW = jnp.bfloat16
ALL = ("section", "shard")
REST = ("shard", "replica")


def matmul(left, right):
    return jnp.dot(left, right, preferred_element_type=jnp.float32)


def times_transposed(left, right):
    return lax.dot_general(
        left, right, (((1,), (1,)), ((), ())), preferred_element_type=jnp.float32
    )


def transposed_times(left, right):
    return lax.dot_general(
        left, right, (((0,), (0,)), ((), ())), preferred_element_type=jnp.float32
    )


def exchange(value, axes):
    return lax.all_to_all(value, axes, 0, 0, tiled=True)


def swap_cores(value):
    return lax.ppermute(value, "shard", [(i, i ^ 1) for i in range(16)])


def whole_sequence(tokens):
    core = lax.axis_index("shard") % 2
    micros, rows, features = tokens.shape
    half = rows // 2
    sends = jnp.broadcast_to(
        tokens.reshape(micros, 1, 2, half, features), (micros, 4, 2, half, features)
    ).reshape(16, half, features)
    mine = exchange(sends, "shard")
    other = swap_cores(mine)
    lower = jnp.where(core == 0, mine, other)
    upper = jnp.where(core == 0, other, mine)
    return jnp.stack([lower, upper], 1).reshape(16 * rows, features)


def send_tokens(value, parts):
    core = lax.axis_index("shard") % 2
    width = parts * HEAD_DIM
    halves = value.reshape(16, 2, 32, width)
    keep = jnp.where(core == 0, halves[:, 0], halves[:, 1])
    take = swap_cores(jnp.where(core == 0, halves[:, 1], halves[:, 0]))
    lower = jnp.split(jnp.where(core == 0, keep, take), parts, 2)
    upper = jnp.split(jnp.where(core == 0, take, keep), parts, 2)
    pair = jnp.concatenate([piece for both in zip(lower, upper) for piece in both], 2)
    sends = jnp.broadcast_to(pair[None], (2, 16, 32, 2 * width)).reshape(32, 32, 2 * width)
    return exchange(sends, ALL).reshape(2, 2, 4, 2, 32, 2 * width)


def masked_scores(queries, keys, seg):
    scores = times_transposed(queries, keys) * SCALE
    return jnp.where(seg[:, None] == seg[None, :], scores, NEGATIVE)


def attend(packed, seg):
    queries, keys, values = jnp.split(packed, 3, 1)
    scores = masked_scores(queries, keys, seg)
    highest = jnp.max(scores, -1, keepdims=True)
    exponent = jnp.exp(scores - highest)
    totals = jnp.sum(exponent, -1, keepdims=True)
    context = matmul((exponent / totals).astype(LOW), values).astype(LOW)
    return context, highest + jnp.log(totals)


def normed(value):
    mean_value = jnp.mean(value, -1, keepdims=True)
    centred = value - mean_value
    spread = jnp.mean(centred * centred, -1, keepdims=True)
    scale = lax.rsqrt(spread + EPSILON)
    return centred * scale, scale


def normed_back(grad, value, gain):
    unit, scale = normed(value)
    weighted = grad * gain
    inner_mean = jnp.mean(weighted * unit, -1, keepdims=True)
    grad_value = scale * (weighted - jnp.mean(weighted, -1, keepdims=True) - unit * inner_mean)
    return (
        grad_value,
        jnp.sum(grad * unit, 0, keepdims=True),
        jnp.sum(grad, 0, keepdims=True),
    )


def gelu_share(value):
    return 0.5 * (1.0 + lax.erf(value * math.sqrt(0.5)))


def gelu_slope(value):
    return gelu_share(value) + value * jnp.exp(-0.5 * value * value) * (0.5 / math.pi) ** 0.5


PARTS = 4
WIDTH = 1024


def this_part(j):
    return jnp.minimum(j, PARTS - 1)


def part_before(j):
    return jnp.maximum(j - 1, 0)


def weight_specs(expand_at, contract_at):
    return [
        pl.BlockSpec((16, 64, 1024), lambda j: (0, 4, 0)),
        pl.BlockSpec((16, 64, WIDTH), lambda j: (0, 5 + expand_at(j), 0)),
        pl.BlockSpec((4, 256, 1024), lambda j: (contract_at(j), 0, 0)),
    ]


def full(*shape):
    return pl.BlockSpec(shape, lambda j: (0,) * len(shape))


ROWS_F32 = jax.ShapeDtypeStruct((128, 1024), jnp.float32)
ROWS_LOW = jax.ShapeDtypeStruct((128, 1024), LOW)
BLOCK_PARAMS = pltpu.CompilerParams(
    dimension_semantics=("arbitrary",), vmem_limit_bytes=48 * 1024 * 1024
)
BLOCK_COST = pl.CostEstimate(
    flops=2 * 128 * 1024 * 9216, bytes_accessed=24 * 1024 * 1024, transcendentals=128 * 4096
)


def forward_kernel(
    tokens,
    context,
    output_weight,
    expand_weight,
    contract_weight,
    params,
    hidden,
    output,
    residual,
    first_low,
    inner,
    second,
    context_rows,
    first,
    total,
    before,
):
    step = pl.program_id(0)

    @pl.when(step == 0)
    def start():
        pairs = [context[s, :, p].reshape(128, 128) for s in range(2) for p in range(4)]
        rows = jnp.concatenate(pairs, 1)
        context_rows[...] = rows
        attention = matmul(rows, output_weight[...].reshape(1024, 1024))
        summed = tokens[...].astype(jnp.float32) + (attention + params[0:1])
        residual[...] = summed
        after = normed(summed)[0] * params[4:5] + params[1:2]
        first[...] = after
        first_low[...] = after.astype(LOW)
        total[...] = jnp.zeros_like(total)
        before[...] = jnp.zeros_like(before)

    last_part = before[...]
    inner_part = matmul(first_low[...], expand_weight[...].reshape(1024, WIDTH)) + hidden[0]
    inner[...] = inner_part
    activation = (last_part * gelu_share(last_part)).astype(LOW)
    total[...] += matmul(activation, contract_weight[...].reshape(WIDTH, 1024))
    before[...] = inner_part

    @pl.when(step == PARTS)
    def finish():
        summed = first[...] + (total[...] + params[2:3])
        second[...] = summed
        output[...] = (normed(summed)[0] * params[5:6] + params[3:4]).astype(LOW)


def block_forward(tokens, context, gathered, params, hidden):
    output, *saved = pl.pallas_call(
        forward_kernel,
        grid=(PARTS + 1,),
        in_specs=[
            full(128, 1024),
            full(2, 2, 4, 2, 32, 128),
            *weight_specs(this_part, part_before),
            full(8, 1024),
            pl.BlockSpec((1, 1, WIDTH), lambda j: (this_part(j), 0, 0)),
        ],
        out_specs=[
            full(128, 1024),
            full(128, 1024),
            full(128, 1024),
            pl.BlockSpec((128, WIDTH), lambda j: (0, this_part(j))),
            full(128, 1024),
            full(128, 1024),
        ],
        out_shape=[
            ROWS_LOW,
            ROWS_F32,
            ROWS_LOW,
            jax.ShapeDtypeStruct((128, 4096), jnp.float32),
            ROWS_F32,
            ROWS_LOW,
        ],
        scratch_shapes=[
            pltpu.VMEM((128, 1024), jnp.float32),
            pltpu.VMEM((128, 1024), jnp.float32),
            pltpu.VMEM((128, WIDTH), jnp.float32),
        ],
        compiler_params=BLOCK_PARAMS,
        cost_estimate=BLOCK_COST,
    )(tokens, context, gathered, gathered, gathered, params, hidden)
    return output, saved


def backward_kernel(
    grad,
    output_weight,
    expand_weight,
    contract_weight,
    params,
    residual,
    inner,
    second,
    grad_residual,
    grad_attn,
    grad_context,
    sums,
    grad_mlp,
    grad_second,
    total,
    before,
):
    step = pl.program_id(0)

    @pl.when(step == 0)
    def start():
        by_value, by_gain, by_shift = normed_back(
            grad[...].astype(jnp.float32), second[...], params[5:6]
        )
        grad_second[...] = by_value
        grad_mlp[...] = by_value.astype(LOW)
        sums[1:2] = by_gain
        sums[4:5] = by_shift
        total[...] = jnp.zeros_like(total)
        before[...] = jnp.zeros_like(before)

    last_part = before[...]
    before[...] = times_transposed(grad_mlp[...], contract_weight[...].reshape(WIDTH, 1024))
    grad_inner = (last_part * gelu_slope(inner[...])).astype(LOW)
    total[...] += times_transposed(grad_inner, expand_weight[...].reshape(1024, WIDTH))

    @pl.when(step == PARTS)
    def finish():
        by_value, by_gain, by_shift = normed_back(
            grad_second[...] + total[...], residual[...], params[4:5]
        )
        grad_residual[...] = by_value
        rounded = by_value.astype(LOW)
        grad_attn[...] = rounded
        rows = times_transposed(rounded, output_weight[...].reshape(1024, 1024)).astype(LOW)
        for s, m, p in ((s, m, p) for s in range(2) for m in range(2) for p in range(4)):
            piece = rows[64 * m : 64 * m + 64, 128 * (4 * s + p) : 128 * (4 * s + p) + 128]
            grad_context[s, m, p, 0] = piece
            grad_context[s, m, p, 1] = piece
        sums[0:1] = by_gain
        sums[2:3] = jnp.sum(rounded.astype(jnp.float32), 0, keepdims=True)
        sums[3:4] = by_shift
        sums[5:8] = jnp.zeros((3, 1024), jnp.float32)


def block_back(grad, saved, gathered, params):
    residual, first_low, inner, second, context_rows = saved
    return pl.pallas_call(
        backward_kernel,
        grid=(PARTS + 1,),
        in_specs=[
            full(128, 1024),
            *weight_specs(part_before, this_part),
            full(8, 1024),
            full(128, 1024),
            pl.BlockSpec((128, WIDTH), lambda j: (0, part_before(j))),
            full(128, 1024),
        ],
        out_specs=[
            full(128, 1024),
            full(128, 1024),
            full(2, 2, 4, 2, 64, 128),
            full(8, 1024),
        ],
        out_shape=[
            ROWS_F32,
            ROWS_LOW,
            jax.ShapeDtypeStruct((2, 2, 4, 2, 64, 128), LOW),
            jax.ShapeDtypeStruct((8, 1024), jnp.float32),
        ],
        scratch_shapes=[
            pltpu.VMEM((128, 1024), LOW),
            pltpu.VMEM((128, 1024), jnp.float32),
            pltpu.VMEM((128, 1024), jnp.float32),
            pltpu.VMEM((128, WIDTH), jnp.float32),
        ],
        compiler_params=BLOCK_PARAMS,
        cost_estimate=BLOCK_COST,
    )(grad, gathered, gathered, gathered, params, residual, inner, second)


def grad_tokens_kernel(got, weight, grad_residual, rounded, total):
    step = pl.program_id(0)
    left = jnp.concatenate([got[0, :, p].reshape(128, 384) for p in range(2)], 1)
    product = times_transposed(left, weight[...])

    @pl.when(step == 0)
    def start():
        total[...] = grad_residual[...] + product

    @pl.when(step > 0)
    def proceed():
        total[...] += product

    @pl.when(step == 3)
    def finish():
        rounded[...] = total[...].astype(LOW)


def grad_tokens(got, weight, grad_residual):
    return pl.pallas_call(
        grad_tokens_kernel,
        grid=(4,),
        in_specs=[
            pl.BlockSpec((1, 2, 2, 2, 32, 384), lambda i: (i // 2, 0, i % 2, 0, 0, 0)),
            pl.BlockSpec((1024, 768), lambda i: (0, i)),
            full(128, 1024),
        ],
        out_specs=full(128, 1024),
        out_shape=ROWS_LOW,
        scratch_shapes=[pltpu.VMEM((128, 1024), jnp.float32)],
        compiler_params=BLOCK_PARAMS,
        cost_estimate=pl.CostEstimate(
            flops=2 * 128 * 3072 * 1024, bytes_accessed=8 * 1024 * 1024, transcendentals=0
        ),
    )(got, weight, grad_residual)


def attend_back_kernel(
    core,
    packed,
    log_totals,
    seg_rows,
    seg_columns,
    got,
    result,
    queries,
    keys,
    values,
    grads,
    grad_keys,
    grad_values,
):
    step = pl.program_id(0)

    @pl.when(step == 0)
    def start():
        queries[...] = packed[:, :HEAD_DIM]
        keys[...] = packed[:, HEAD_DIM : 2 * HEAD_DIM]
        values[...] = packed[:, 2 * HEAD_DIM :]
        pair = got[...].reshape(1024, 128)
        grads[...] = jnp.where(core[0] == 0, pair[:, :HEAD_DIM], pair[:, HEAD_DIM:])
        grad_keys[...] = jnp.zeros_like(grad_keys)
        grad_values[...] = jnp.zeros_like(grad_values)

    rows = pl.ds(pl.multiple_of(step * 256, 256), 256)
    block_queries = queries[rows]
    block_grads = grads[rows]
    scores = times_transposed(block_queries, keys[...]) * SCALE
    scores = jnp.where(seg_rows[rows] == seg_columns[...], scores, NEGATIVE)
    soft = jnp.exp(scores - log_totals[rows])
    grad_soft = times_transposed(block_grads, values[...])
    row_total = jnp.sum(soft * grad_soft, -1, keepdims=True)
    grad_scores = (soft * (grad_soft - row_total)).astype(LOW)
    result[rows, :HEAD_DIM] = (matmul(grad_scores, keys[...]) * SCALE).astype(LOW)
    grad_keys[...] += transposed_times(grad_scores, block_queries)
    grad_values[...] += transposed_times(soft.astype(LOW), block_grads)

    @pl.when(step == 3)
    def finish():
        result[:, HEAD_DIM : 2 * HEAD_DIM] = (grad_keys[...] * SCALE).astype(LOW)
        result[:, 2 * HEAD_DIM :] = grad_values[...].astype(LOW)


def attend_back(core, packed, log_totals, seg, got, layer):
    return pl.pallas_call(
        attend_back_kernel,
        grid=(4,),
        in_specs=[
            pl.BlockSpec(memory_space=pltpu.SMEM),
            full(1024, 192),
            full(1024, 1),
            full(1024, 1),
            full(1, 1024),
            pl.BlockSpec((16, 64, 128), lambda i: (layer, 0, 0)),
        ],
        out_specs=full(1024, 192),
        out_shape=jax.ShapeDtypeStruct((1024, 192), LOW),
        scratch_shapes=[pltpu.VMEM((1024, HEAD_DIM), LOW)] * 4
        + [pltpu.VMEM((1024, HEAD_DIM), jnp.float32)] * 2,
        compiler_params=BLOCK_PARAMS,
        cost_estimate=pl.CostEstimate(
            flops=10 * 1024 * 1024 * 64, bytes_accessed=2 * 1024 * 1024, transcendentals=1 << 20
        ),
    )(core, packed, log_totals, seg[:, None], seg[None, :], got)


def with_sums(grad, sums):
    rows = jnp.concatenate([sums[None], jnp.zeros((15, sums.shape[0]), jnp.float32)], 0)
    return jnp.concatenate([grad.astype(LOW), rows.astype(LOW)], 0)


def on_device(
    inputs,
    segments,
    cotangent,
    attend_weight,
    output_weight,
    expand_weight,
    contract_weight,
    biases,
    hidden_bias,
    gains,
):
    section = lax.axis_index("section")
    shard = lax.axis_index("shard")
    on_first = section == 0
    micro = shard // 8
    head = section * 8 + shard % 8
    inputs = inputs[:, 0]

    with jax.named_scope("gather_block_weights"):
        rows = jnp.concatenate(
            [contract_weight[0], output_weight[0]] + jnp.split(expand_weight[0], 4, 1), 0
        )
        quarter = lax.dynamic_slice_in_dim(rows, lax.axis_index("replica") * 144, 144, 0)
        gathered = lax.all_gather(quarter, REST, axis=0, tiled=False).reshape(16, 576, 1024)

    with jax.named_scope("head_weights"):
        by_head = attend_weight[0].reshape(64, 3, HEADS, HEAD_DIM).transpose(2, 0, 1, 3)
        small = jnp.concatenate(
            [
                biases.reshape(384),
                gains.reshape(128),
                hidden_bias.reshape(256),
                segments.reshape(128).astype(LOW),
                jnp.zeros((16 * 192 - 896,), LOW),
            ]
        ).reshape(1, 16, 192)
        block = jnp.concatenate(
            [by_head.reshape(HEADS, 64, 192), jnp.broadcast_to(small, (HEADS, 16, 192))], 1
        )
        block = jnp.broadcast_to(block.reshape(2, 1, 8, 80, 192), (2, 2, 8, 80, 192))
        got = exchange(block.reshape(32, 80, 192), ALL).reshape(2, 16, 80, 192)
        head_weight = got[:, :, :64].reshape(2, 1024, 192)
        small = got[:, :, 64:69].reshape(2, 16, 960)
        all_biases = small[:, :, :384].reshape(2, 16, 6, 64).transpose(0, 2, 1, 3)
        all_biases = all_biases.reshape(2, 6, 1024).astype(jnp.float32)
        all_gains = small[:, :, 384:512].reshape(2, 16, 2, 64).transpose(0, 2, 1, 3)
        all_gains = all_gains.reshape(2, 2, 1024).astype(jnp.float32)
        all_hidden = small[:, :, 512:768].reshape(2, 4096).astype(jnp.float32)
        seg = small[0, :, 768:896].reshape(16, 2, 64)
        seg = jnp.where(micro == 0, seg[:, 0], seg[:, 1]).reshape(1024)
        own_biases = jnp.where(on_first, all_biases[0], all_biases[1])
        own_gains = jnp.where(on_first, all_gains[0], all_gains[1])
        own_hidden = jnp.where(on_first, all_hidden[0], all_hidden[1]).reshape(PARTS, 1, WIDTH)
        params = jnp.concatenate([own_biases[2:], own_gains, jnp.zeros((2, 1024))], 0)
        head_bias = lax.dynamic_slice_in_dim(
            all_biases.reshape(2, 6, HEADS, HEAD_DIM), head, 1, 2
        )[:, :, 0]
        head_bias = jnp.concatenate(
            [head_bias[:, 0], jnp.zeros_like(head_bias[:, 0]), head_bias[:, 1]], 1
        )

    def attention(layer, tokens):
        with jax.named_scope("sequence_tokens"):
            whole = whole_sequence(tokens)
        with jax.named_scope("attention"):
            packed = (matmul(whole, head_weight[layer]) + head_bias[layer]).astype(LOW)
            context, log_totals = attend(packed, seg)
        with jax.named_scope("context_out"):
            context = send_tokens(context, 1)
        return context, (whole, packed, log_totals)

    def attention_back(layer, grad_context, kept, beside):
        unused, packed, log_totals = kept
        with jax.named_scope("grad_context_in"):
            got = exchange(grad_context.reshape(32, 64, 128), ALL)
            got, beside = lax.optimization_barrier((got, beside))
        with jax.named_scope("attention_back"):
            core = (shard % 2).astype(jnp.int32).reshape(1)
            grad_packed = attend_back(core, packed, log_totals, seg, got, layer)
        return grad_packed, beside

    def attend_part(tokens, grad_packed):
        grad_weight = transposed_times(tokens, grad_packed)
        return with_sums(grad_weight, jnp.sum(grad_packed.astype(jnp.float32), 0))

    context_0, kept_0 = attention(0, inputs)
    tokens_0 = inputs.reshape(128, 1024)
    with jax.named_scope("block_0"):
        output, unused = block_forward(tokens_0, context_0, gathered, params, own_hidden)
    with jax.named_scope("to_next_section"):
        tokens_1 = jnp.where(
            on_first, output, lax.ppermute(output, "section", [(0, 1)])
        )
    with jax.named_scope("gather_attend_weight"):
        own_pairs = attend_weight[0].reshape(64, 3, 8, 128).transpose(0, 2, 1, 3).reshape(64, 3072)
        other_pairs = lax.ppermute(own_pairs, "section", [(0, 1), (1, 0)])
        other_pairs, output = lax.optimization_barrier((other_pairs, output))
        other_attend = lax.all_gather(other_pairs, "shard", axis=0, tiled=True)
    context_1, kept_1 = attention(1, tokens_1.reshape(2, 64, 1024))
    own_tokens = jnp.where(on_first, tokens_0, tokens_1)
    own_context = jnp.where(on_first, context_0, context_1)
    with jax.named_scope("block_1"):
        output, saved = block_forward(own_tokens, own_context, gathered, params, own_hidden)
    layer_output = output.reshape(1, 2, 1, 64, 1024)
    with jax.named_scope("gather_first"):
        first_all = lax.all_gather(saved[1], "shard", axis=0, tiled=True)

    last_grad = cotangent.reshape(128, 1024)
    with jax.named_scope("block_back_1"):
        grad_residual, unused, grad_context, unused = block_back(
            last_grad, saved, gathered, params
        )
    with jax.named_scope("residual_to_other_section"):
        arrived_1 = lax.ppermute(grad_residual, "section", [(1, 0)])
    grad_packed_1, arrived_1 = attention_back(1, grad_context, kept_1, arrived_1)
    with jax.named_scope("grad_tokens_1"):
        rounded = grad_tokens(send_tokens(grad_packed_1, 3), other_attend, arrived_1)
        rounded_1 = rounded
    own_grad = jnp.where(on_first, rounded, last_grad)
    with jax.named_scope("gather_grad_mlp"):
        grad_mlp = normed_back(own_grad.astype(jnp.float32), saved[3], params[5:6])[0].astype(LOW)
        grad_mlp, own_grad = lax.optimization_barrier((grad_mlp, own_grad))
        grad_mlp_all = lax.all_gather(grad_mlp, "shard", axis=0, tiled=True)
    with jax.named_scope("block_back_0"):
        grad_residual, grad_attn, grad_context, norm_sums = block_back(
            own_grad, saved, gathered, params
        )
    late_tokens, late_packed, late_gathered, grad_context = lax.optimization_barrier(
        (kept_1[0], grad_packed_1, gathered, grad_context)
    )
    with jax.named_scope("swap_attend_grad"):
        part_1 = attend_part(late_tokens, late_packed)
        take_1 = lax.ppermute(part_1, "section", [(0, 1)])
    with jax.named_scope("sum_output_grad"):
        output_grad = transposed_times(saved[4], grad_attn)
        halves = [output_grad[:, :512], output_grad[:, 512:]]
        core = shard % 2
        keep = jnp.where(core == 0, halves[0], halves[1])
        give = jnp.where(core == 0, halves[1], halves[0]).astype(LOW)
        output_grad = (keep + swap_cores(give).astype(jnp.float32)).astype(LOW)
    grad_packed, output_grad = attention_back(0, grad_context, kept_0, output_grad)

    with jax.named_scope("sum_output_grad"):
        output_got = exchange(output_grad.reshape(64, 16, 512), REST)
        output_got, grad_packed = lax.optimization_barrier((output_got, grad_packed))
    with jax.named_scope("swap_attend_grad"):
        part_0 = attend_part(kept_0[0], grad_packed)
        take_0 = lax.ppermute(part_0, "section", [(1, 0)])
        lower = jnp.where(on_first, part_0, take_1)
        upper = jnp.where(on_first, take_0, part_1)
        attend_grad = jnp.concatenate([lower[:1024], upper[:1024]], 1)
        sums = jnp.stack([lower[1024], upper[1024]]).reshape(2, 3, HEAD_DIM)
        norm_rows = norm_sums[:5].reshape(5, 16, 64).transpose(1, 0, 2)
        mine = jnp.arange(8) == shard % 8
        head_rows = jnp.where(
            mine[None, :, None, None], sums[:, None, ::2].astype(jnp.float32), 0.0
        ).reshape(16, 2, 64)
        vectors = jnp.pad(
            jnp.concatenate([norm_rows, head_rows], 1), ((0, 0), (0, 9), (0, 64))
        )
        vectors = jnp.broadcast_to(vectors[:, None], (16, 4, 16, 128)).reshape(1024, 128)
        vectors = vectors.astype(LOW)
    with jax.named_scope("sum_attend_grad"):
        parts = jnp.concatenate([attend_grad, vectors], 1)
        parts, late_attn, late_rounded = lax.optimization_barrier((parts, grad_attn, rounded_1))
        got = exchange(parts.reshape(64, 16, 512), REST)
        arrived_0 = lax.ppermute(late_attn, "section", [(0, 1)])
        grad_tokens_1 = lax.ppermute(late_rounded, "section", [(0, 1)])
    with jax.named_scope("block_weight_grads"):
        expand_part = lax.dynamic_slice(
            late_gathered, (0, 320 + shard // 4 * 64, shard % 4 * 256), (16, 64, 256)
        ).reshape(1024, 256)
        hidden_part = lax.dynamic_slice_in_dim(own_hidden.reshape(4096), shard * 256, 256, 0)
        inner = matmul(first_all, expand_part) + hidden_part
        activation = inner * gelu_share(inner)
        grad_inner = times_transposed(grad_mlp_all, contract_weight[0]) * gelu_slope(inner)
        grad_inner = grad_inner.astype(LOW)
        expand_grad = transposed_times(first_all, grad_inner).astype(LOW)
        contract_grad = transposed_times(activation.astype(LOW), grad_mlp_all).astype(LOW)
        hidden_sum = jnp.sum(grad_inner.astype(jnp.float32), 0)
        mlp_sum = jnp.sum(grad_mlp_all.astype(jnp.float32), 0)
        extra = jnp.concatenate(
            [
                jnp.concatenate([hidden_sum, jnp.zeros((768,), jnp.float32)])[None],
                mlp_sum[None],
                jnp.zeros((14, 1024), jnp.float32),
            ],
            0,
        ).astype(LOW)
        rows = jnp.concatenate(
            [contract_grad.reshape(4, 64, 1024), jnp.broadcast_to(extra, (4, 16, 1024))], 1
        )
    with jax.named_scope("sum_expand_grad"):
        got, expand_grad, rows, arrived_0, grad_tokens_1 = lax.optimization_barrier(
            (got, expand_grad, rows, arrived_0, grad_tokens_1)
        )
        expand_got = exchange(expand_grad.reshape(64, 16, 256), REST)
        expand_got, rows = lax.optimization_barrier((expand_got, rows))
    with jax.named_scope("sum_contract"):
        got_contract = exchange(rows, "replica").astype(jnp.float32).sum(0)
    with jax.named_scope("sum_attend_grad"):
        got_output = output_got.astype(jnp.float32).reshape(8, 2, 4, 16, 512).sum((0, 2))
        got_output = jnp.concatenate([got_output[0], got_output[1]], 1).astype(LOW)
        got_attend = got[:, :, :384].astype(jnp.float32).reshape(2, 8, 4, 16, 384).sum((0, 2))
        got_expand = expand_got.astype(jnp.float32).reshape(16, 4, 16, 256).sum(1)
        got_expand = got_expand.astype(LOW).transpose(1, 0, 2).reshape(16, 4096)
        got_vectors = got[:, :7, 384:448].astype(jnp.float32).sum(0)
        got_attend, got_output = lax.optimization_barrier((got_attend.astype(LOW), got_output))
        got_attend = got_attend.reshape(8, 16, 2, 3, 64).transpose(1, 3, 2, 0, 4)
        got_attend = got_attend.reshape(16, 3072)
    with jax.named_scope("gather_weight_grads"):
        contract_rows = got_contract[:64].astype(LOW).reshape(4, 16, 1024)
        owned = jnp.concatenate([got_attend, got_output, got_expand, *contract_rows], 1)
    with jax.named_scope("grad_tokens_0"):
        late_packed, owned = lax.optimization_barrier((grad_packed, owned))
        rounded = grad_tokens(
            send_tokens(late_packed, 3), other_attend, arrived_0.astype(jnp.float32)
        )
        grad_tokens_0 = lax.ppermute(rounded, "section", [(1, 0)])
    with jax.named_scope("gather_weight_grads"):
        totals = lax.all_gather(owned, "replica", axis=0, tiled=True)
        contract_total = totals[:, 8192:].reshape(4, 16, 4, 1024).transpose(0, 2, 1, 3)
        contract_total = contract_total.reshape(1, 256, 1024).astype(jnp.float32)
        totals = totals[None, :, :8192].astype(jnp.float32)
    attend_total = totals[:, :, :3072]
    output_total = totals[:, :, 3072:4096]
    expand_total = totals[:, :, 4096:]
    grad_tokens_0, attend_total, output_total, expand_total, contract_total = (
        lax.optimization_barrier(
            (grad_tokens_0, attend_total, output_total, expand_total, contract_total)
        )
    )
    input_grad = jnp.where(on_first, grad_tokens_0, grad_tokens_1).astype(jnp.float32)
    input_grad = input_grad.reshape(1, 2, 1, 64, 1024)
    mlp_own = lax.dynamic_slice_in_dim(got_contract[65], shard * 64, 64, 0)
    biases_grad = jnp.stack(
        [
            got_vectors[5],
            got_vectors[6],
            got_vectors[2],
            got_vectors[3],
            mlp_own,
            got_vectors[4],
        ]
    )
    return (
        layer_output,
        input_grad,
        attend_total,
        output_total,
        expand_total,
        contract_total,
        biases_grad[None],
        got_contract[None, 64, :256],
        got_vectors[None, :2],
    )


def solution(mesh):
    placed = (
        P(None, "replica", "shard", None),
        P(None, "replica", "shard"),
        P(None, "replica", "shard", None),
        P("section", "shard", None),
        P("section", "shard", None),
        P("section", "shard", None),
        P("section", "shard", None),
        P("section", None, "shard"),
        P("section", "shard"),
        P("section", None, "shard"),
    )
    return jax.shard_map(
        on_device,
        mesh=mesh,
        in_specs=placed,
        out_specs=(
            P("section", None, "replica", "shard", None),
            P("section", None, "replica", "shard", None),
            P("section", "shard", None),
            P("section", "shard", None),
            P("section", "shard", None),
            P("section", "shard", None),
            P("section", None, "shard"),
            P("section", "shard"),
            P("section", None, "shard"),
        ),
        check_vma=False,
    )
```

```python
import math

import jax
import jax.numpy as jnp
from jax import lax
from jax.experimental import pallas as pl
from jax.experimental.pallas import tpu as pltpu
from jax.sharding import PartitionSpec as P

HEADS = 16
HEAD_DIM = 64
NEGATIVE = -1e30
EPSILON = 1e-05
SCALE = 1.0 / math.sqrt(HEAD_DIM)
LOW = jnp.bfloat16
ALL = ("section", "shard")
REST = ("shard", "replica")


def matmul(left, right):
    return jnp.dot(left, right, preferred_element_type=jnp.float32)


def times_transposed(left, right):
    return lax.dot_general(
        left, right, (((1,), (1,)), ((), ())), preferred_element_type=jnp.float32
    )


def transposed_times(left, right):
    return lax.dot_general(
        left, right, (((0,), (0,)), ((), ())), preferred_element_type=jnp.float32
    )


def exchange(value, axes):
    return lax.all_to_all(value, axes, 0, 0, tiled=True)


def swap_cores(value):
    return lax.ppermute(value, "shard", [(i, i ^ 1) for i in range(16)])


def whole_sequence(tokens):
    core = lax.axis_index("shard") % 2
    micros, rows, features = tokens.shape
    half = rows // 2
    sends = jnp.broadcast_to(
        tokens.reshape(micros, 1, 2, half, features), (micros, 4, 2, half, features)
    ).reshape(16, half, features)
    mine = exchange(sends, "shard")
    other = swap_cores(mine)
    lower = jnp.where(core == 0, mine, other)
    upper = jnp.where(core == 0, other, mine)
    return jnp.stack([lower, upper], 1).reshape(16 * rows, features)


def send_tokens(value, parts):
    core = lax.axis_index("shard") % 2
    width = parts * HEAD_DIM
    halves = value.reshape(16, 2, 32, width)
    keep = jnp.where(core == 0, halves[:, 0], halves[:, 1])
    take = swap_cores(jnp.where(core == 0, halves[:, 1], halves[:, 0]))
    lower = jnp.split(jnp.where(core == 0, keep, take), parts, 2)
    upper = jnp.split(jnp.where(core == 0, take, keep), parts, 2)
    pair = jnp.concatenate([piece for both in zip(lower, upper) for piece in both], 2)
    sends = jnp.broadcast_to(pair[None], (2, 16, 32, 2 * width)).reshape(32, 32, 2 * width)
    return exchange(sends, ALL).reshape(2, 2, 4, 2, 32, 2 * width)


def masked_scores(queries, keys, seg):
    scores = times_transposed(queries, keys) * SCALE
    return jnp.where(seg[:, None] == seg[None, :], scores, NEGATIVE)


def attend(packed, seg):
    queries, keys, values = jnp.split(packed, 3, 1)
    scores = masked_scores(queries, keys, seg)
    highest = jnp.max(scores, -1, keepdims=True)
    exponent = jnp.exp(scores - highest)
    totals = jnp.sum(exponent, -1, keepdims=True)
    context = matmul((exponent / totals).astype(LOW), values).astype(LOW)
    return context, highest + jnp.log(totals)


def normed(value):
    mean_value = jnp.mean(value, -1, keepdims=True)
    centred = value - mean_value
    spread = jnp.mean(centred * centred, -1, keepdims=True)
    scale = lax.rsqrt(spread + EPSILON)
    return centred * scale, scale


def normed_back(grad, value, gain):
    unit, scale = normed(value)
    weighted = grad * gain
    inner_mean = jnp.mean(weighted * unit, -1, keepdims=True)
    grad_value = scale * (weighted - jnp.mean(weighted, -1, keepdims=True) - unit * inner_mean)
    return (
        grad_value,
        jnp.sum(grad * unit, 0, keepdims=True),
        jnp.sum(grad, 0, keepdims=True),
    )


def gelu_share(value):
    return 0.5 * (1.0 + lax.erf(value * math.sqrt(0.5)))


def gelu_slope(value):
    return gelu_share(value) + value * jnp.exp(-0.5 * value * value) * (0.5 / math.pi) ** 0.5


PARTS = 4
WIDTH = 1024


def this_part(j):
    return jnp.minimum(j, PARTS - 1)


def part_before(j):
    return jnp.maximum(j - 1, 0)


def weight_specs(expand_at, contract_at):
    return [
        pl.BlockSpec((16, 64, 1024), lambda j: (0, 4, 0)),
        pl.BlockSpec((16, 64, WIDTH), lambda j: (0, 5 + expand_at(j), 0)),
        pl.BlockSpec((4, 256, 1024), lambda j: (contract_at(j), 0, 0)),
    ]


def full(*shape):
    return pl.BlockSpec(shape, lambda j: (0,) * len(shape))


ROWS_F32 = jax.ShapeDtypeStruct((128, 1024), jnp.float32)
ROWS_LOW = jax.ShapeDtypeStruct((128, 1024), LOW)
BLOCK_PARAMS = pltpu.CompilerParams(
    dimension_semantics=("arbitrary",), vmem_limit_bytes=48 * 1024 * 1024
)
BLOCK_COST = pl.CostEstimate(
    flops=2 * 128 * 1024 * 9216, bytes_accessed=24 * 1024 * 1024, transcendentals=128 * 4096
)


def forward_kernel(
    tokens,
    context,
    output_weight,
    expand_weight,
    contract_weight,
    params,
    hidden,
    output,
    residual,
    first_low,
    inner,
    second,
    context_rows,
    first,
    total,
    before,
):
    step = pl.program_id(0)

    @pl.when(step == 0)
    def start():
        pairs = [context[s, :, p].reshape(128, 128) for s in range(2) for p in range(4)]
        rows = jnp.concatenate(pairs, 1)
        context_rows[...] = rows
        attention = matmul(rows, output_weight[...].reshape(1024, 1024))
        summed = tokens[...].astype(jnp.float32) + (attention + params[0:1])
        residual[...] = summed
        after = normed(summed)[0] * params[4:5] + params[1:2]
        first[...] = after
        first_low[...] = after.astype(LOW)
        total[...] = jnp.zeros_like(total)
        before[...] = jnp.zeros_like(before)

    last_part = before[...]
    inner_part = matmul(first_low[...], expand_weight[...].reshape(1024, WIDTH)) + hidden[0]
    inner[...] = inner_part
    activation = (last_part * gelu_share(last_part)).astype(LOW)
    total[...] += matmul(activation, contract_weight[...].reshape(WIDTH, 1024))
    before[...] = inner_part

    @pl.when(step == PARTS)
    def finish():
        summed = first[...] + (total[...] + params[2:3])
        second[...] = summed
        output[...] = (normed(summed)[0] * params[5:6] + params[3:4]).astype(LOW)


def block_forward(tokens, context, gathered, params, hidden):
    output, *saved = pl.pallas_call(
        forward_kernel,
        grid=(PARTS + 1,),
        in_specs=[
            full(128, 1024),
            full(2, 2, 4, 2, 32, 128),
            *weight_specs(this_part, part_before),
            full(8, 1024),
            pl.BlockSpec((1, 1, WIDTH), lambda j: (this_part(j), 0, 0)),
        ],
        out_specs=[
            full(128, 1024),
            full(128, 1024),
            full(128, 1024),
            pl.BlockSpec((128, WIDTH), lambda j: (0, this_part(j))),
            full(128, 1024),
            full(128, 1024),
        ],
        out_shape=[
            ROWS_LOW,
            ROWS_F32,
            ROWS_LOW,
            jax.ShapeDtypeStruct((128, 4096), jnp.float32),
            ROWS_F32,
            ROWS_LOW,
        ],
        scratch_shapes=[
            pltpu.VMEM((128, 1024), jnp.float32),
            pltpu.VMEM((128, 1024), jnp.float32),
            pltpu.VMEM((128, WIDTH), jnp.float32),
        ],
        compiler_params=BLOCK_PARAMS,
        cost_estimate=BLOCK_COST,
    )(tokens, context, gathered, gathered, gathered, params, hidden)
    return output, saved


def backward_kernel(
    grad,
    output_weight,
    expand_weight,
    contract_weight,
    params,
    residual,
    inner,
    second,
    grad_residual,
    grad_attn,
    grad_context,
    sums,
    grad_mlp,
    grad_second,
    total,
    before,
):
    step = pl.program_id(0)

    @pl.when(step == 0)
    def start():
        by_value, by_gain, by_shift = normed_back(
            grad[...].astype(jnp.float32), second[...], params[5:6]
        )
        grad_second[...] = by_value
        grad_mlp[...] = by_value.astype(LOW)
        sums[1:2] = by_gain
        sums[4:5] = by_shift
        total[...] = jnp.zeros_like(total)
        before[...] = jnp.zeros_like(before)

    last_part = before[...]
    before[...] = times_transposed(grad_mlp[...], contract_weight[...].reshape(WIDTH, 1024))
    grad_inner = (last_part * gelu_slope(inner[...])).astype(LOW)
    total[...] += times_transposed(grad_inner, expand_weight[...].reshape(1024, WIDTH))

    @pl.when(step == PARTS)
    def finish():
        by_value, by_gain, by_shift = normed_back(
            grad_second[...] + total[...], residual[...], params[4:5]
        )
        grad_residual[...] = by_value
        rounded = by_value.astype(LOW)
        grad_attn[...] = rounded
        rows = times_transposed(rounded, output_weight[...].reshape(1024, 1024)).astype(LOW)
        for s, m, p in ((s, m, p) for s in range(2) for m in range(2) for p in range(4)):
            piece = rows[64 * m : 64 * m + 64, 128 * (4 * s + p) : 128 * (4 * s + p) + 128]
            grad_context[s, m, p, 0] = piece
            grad_context[s, m, p, 1] = piece
        sums[0:1] = by_gain
        sums[2:3] = jnp.sum(rounded.astype(jnp.float32), 0, keepdims=True)
        sums[3:4] = by_shift
        sums[5:8] = jnp.zeros((3, 1024), jnp.float32)


def block_back(grad, saved, gathered, params):
    residual, first_low, inner, second, context_rows = saved
    return pl.pallas_call(
        backward_kernel,
        grid=(PARTS + 1,),
        in_specs=[
            full(128, 1024),
            *weight_specs(part_before, this_part),
            full(8, 1024),
            full(128, 1024),
            pl.BlockSpec((128, WIDTH), lambda j: (0, part_before(j))),
            full(128, 1024),
        ],
        out_specs=[
            full(128, 1024),
            full(128, 1024),
            full(2, 2, 4, 2, 64, 128),
            full(8, 1024),
        ],
        out_shape=[
            ROWS_F32,
            ROWS_LOW,
            jax.ShapeDtypeStruct((2, 2, 4, 2, 64, 128), LOW),
            jax.ShapeDtypeStruct((8, 1024), jnp.float32),
        ],
        scratch_shapes=[
            pltpu.VMEM((128, 1024), LOW),
            pltpu.VMEM((128, 1024), jnp.float32),
            pltpu.VMEM((128, 1024), jnp.float32),
            pltpu.VMEM((128, WIDTH), jnp.float32),
        ],
        compiler_params=BLOCK_PARAMS,
        cost_estimate=BLOCK_COST,
    )(grad, gathered, gathered, gathered, params, residual, inner, second)


def grad_tokens_kernel(got, weight, grad_residual, rounded, total):
    step = pl.program_id(0)
    left = jnp.concatenate([got[0, :, p].reshape(128, 384) for p in range(2)], 1)
    product = times_transposed(left, weight[...])

    @pl.when(step == 0)
    def start():
        total[...] = grad_residual[...].astype(jnp.float32) + product

    @pl.when(step > 0)
    def proceed():
        total[...] += product

    @pl.when(step == 3)
    def finish():
        rounded[...] = total[...].astype(LOW)


def grad_tokens(got, weight, grad_residual):
    return pl.pallas_call(
        grad_tokens_kernel,
        grid=(4,),
        in_specs=[
            pl.BlockSpec((1, 2, 2, 2, 32, 384), lambda i: (i // 2, 0, i % 2, 0, 0, 0)),
            pl.BlockSpec((1024, 768), lambda i: (0, i)),
            full(128, 1024),
        ],
        out_specs=full(128, 1024),
        out_shape=ROWS_LOW,
        scratch_shapes=[pltpu.VMEM((128, 1024), jnp.float32)],
        compiler_params=BLOCK_PARAMS,
        cost_estimate=pl.CostEstimate(
            flops=2 * 128 * 3072 * 1024, bytes_accessed=8 * 1024 * 1024, transcendentals=0
        ),
    )(got, weight, grad_residual)


def attend_back_kernel(
    core,
    packed,
    log_totals,
    seg_rows,
    seg_columns,
    got,
    result,
    queries,
    keys,
    values,
    grads,
    grad_keys,
    grad_values,
):
    step = pl.program_id(0)

    @pl.when(step == 0)
    def start():
        queries[...] = packed[:, :HEAD_DIM]
        keys[...] = packed[:, HEAD_DIM : 2 * HEAD_DIM]
        values[...] = packed[:, 2 * HEAD_DIM :]
        pair = got[...].reshape(1024, 128)
        grads[...] = jnp.where(core[0] == 0, pair[:, :HEAD_DIM], pair[:, HEAD_DIM:])
        grad_keys[...] = jnp.zeros_like(grad_keys)
        grad_values[...] = jnp.zeros_like(grad_values)

    rows = pl.ds(pl.multiple_of(step * 256, 256), 256)
    block_queries = queries[rows]
    block_grads = grads[rows]
    scores = times_transposed(block_queries, keys[...]) * SCALE
    scores = jnp.where(seg_rows[rows] == seg_columns[...], scores, NEGATIVE)
    soft = jnp.exp(scores - log_totals[rows])
    grad_soft = times_transposed(block_grads, values[...])
    row_total = jnp.sum(soft * grad_soft, -1, keepdims=True)
    grad_scores = (soft * (grad_soft - row_total)).astype(LOW)
    result[rows, :HEAD_DIM] = (matmul(grad_scores, keys[...]) * SCALE).astype(LOW)
    grad_keys[...] += transposed_times(grad_scores, block_queries)
    grad_values[...] += transposed_times(soft.astype(LOW), block_grads)

    @pl.when(step == 3)
    def finish():
        result[:, HEAD_DIM : 2 * HEAD_DIM] = (grad_keys[...] * SCALE).astype(LOW)
        result[:, 2 * HEAD_DIM :] = grad_values[...].astype(LOW)


def attend_back(core, packed, log_totals, seg, got, layer):
    return pl.pallas_call(
        attend_back_kernel,
        grid=(4,),
        in_specs=[
            pl.BlockSpec(memory_space=pltpu.SMEM),
            full(1024, 192),
            full(1024, 1),
            full(1024, 1),
            full(1, 1024),
            pl.BlockSpec((16, 64, 128), lambda i: (layer, 0, 0)),
        ],
        out_specs=full(1024, 192),
        out_shape=jax.ShapeDtypeStruct((1024, 192), LOW),
        scratch_shapes=[pltpu.VMEM((1024, HEAD_DIM), LOW)] * 4
        + [pltpu.VMEM((1024, HEAD_DIM), jnp.float32)] * 2,
        compiler_params=BLOCK_PARAMS,
        cost_estimate=pl.CostEstimate(
            flops=10 * 1024 * 1024 * 64, bytes_accessed=2 * 1024 * 1024, transcendentals=1 << 20
        ),
    )(core, packed, log_totals, seg[:, None], seg[None, :], got)


def with_sums(grad, sums):
    rows = jnp.concatenate([sums[None], jnp.zeros((15, sums.shape[0]), jnp.float32)], 0)
    return jnp.concatenate([grad.astype(LOW), rows.astype(LOW)], 0)


def on_device(
    inputs,
    segments,
    cotangent,
    attend_weight,
    output_weight,
    expand_weight,
    contract_weight,
    biases,
    hidden_bias,
    gains,
):
    section = lax.axis_index("section")
    shard = lax.axis_index("shard")
    on_first = section == 0
    micro = shard // 8
    head = section * 8 + shard % 8
    inputs = inputs[:, 0]

    with jax.named_scope("gather_block_weights"):
        rows = jnp.concatenate(
            [contract_weight[0], output_weight[0]] + jnp.split(expand_weight[0], 4, 1), 0
        )
        quarter = lax.dynamic_slice_in_dim(rows, lax.axis_index("replica") * 144, 144, 0)
        gathered = lax.all_gather(quarter, REST, axis=0, tiled=False).reshape(16, 576, 1024)

    with jax.named_scope("head_weights"):
        by_head = attend_weight[0].reshape(64, 3, HEADS, HEAD_DIM).transpose(2, 0, 1, 3)
        small = jnp.concatenate(
            [
                biases.reshape(384),
                gains.reshape(128),
                hidden_bias.reshape(256),
                segments.reshape(128).astype(LOW),
                jnp.zeros((16 * 192 - 896,), LOW),
            ]
        ).reshape(1, 16, 192)
        block = jnp.concatenate(
            [by_head.reshape(HEADS, 64, 192), jnp.broadcast_to(small, (HEADS, 16, 192))], 1
        )
        block = jnp.broadcast_to(block.reshape(2, 1, 8, 80, 192), (2, 2, 8, 80, 192))
        got = exchange(block.reshape(32, 80, 192), ALL).reshape(2, 16, 80, 192)
        head_weight = got[:, :, :64].reshape(2, 1024, 192)
        small = got[:, :, 64:69].reshape(2, 16, 960)
        all_biases = small[:, :, :384].reshape(2, 16, 6, 64).transpose(0, 2, 1, 3)
        all_biases = all_biases.reshape(2, 6, 1024).astype(jnp.float32)
        all_gains = small[:, :, 384:512].reshape(2, 16, 2, 64).transpose(0, 2, 1, 3)
        all_gains = all_gains.reshape(2, 2, 1024).astype(jnp.float32)
        all_hidden = small[:, :, 512:768].reshape(2, 4096).astype(jnp.float32)
        seg = small[0, :, 768:896].reshape(16, 2, 64)
        seg = jnp.where(micro == 0, seg[:, 0], seg[:, 1]).reshape(1024)
        own_biases = jnp.where(on_first, all_biases[0], all_biases[1])
        own_gains = jnp.where(on_first, all_gains[0], all_gains[1])
        own_hidden = jnp.where(on_first, all_hidden[0], all_hidden[1]).reshape(PARTS, 1, WIDTH)
        params = jnp.concatenate([own_biases[2:], own_gains, jnp.zeros((2, 1024))], 0)
        head_bias = lax.dynamic_slice_in_dim(
            all_biases.reshape(2, 6, HEADS, HEAD_DIM), head, 1, 2
        )[:, :, 0]
        head_bias = jnp.concatenate(
            [head_bias[:, 0], jnp.zeros_like(head_bias[:, 0]), head_bias[:, 1]], 1
        )

    def attention(layer, tokens):
        with jax.named_scope("sequence_tokens"):
            whole = whole_sequence(tokens)
        with jax.named_scope("attention"):
            packed = (matmul(whole, head_weight[layer]) + head_bias[layer]).astype(LOW)
            context, log_totals = attend(packed, seg)
        with jax.named_scope("context_out"):
            context = send_tokens(context, 1)
        return context, (whole, packed, log_totals)

    def attention_back(layer, grad_context, kept, beside):
        unused, packed, log_totals = kept
        with jax.named_scope("grad_context_in"):
            got = exchange(grad_context.reshape(32, 64, 128), ALL)
            got, beside = lax.optimization_barrier((got, beside))
        with jax.named_scope("attention_back"):
            core = (shard % 2).astype(jnp.int32).reshape(1)
            grad_packed = attend_back(core, packed, log_totals, seg, got, layer)
        return grad_packed, beside

    def attend_part(tokens, grad_packed):
        grad_weight = transposed_times(tokens, grad_packed)
        return with_sums(grad_weight, jnp.sum(grad_packed.astype(jnp.float32), 0))

    context_0, kept_0 = attention(0, inputs)
    tokens_0 = inputs.reshape(128, 1024)
    with jax.named_scope("block_0"):
        output, unused = block_forward(tokens_0, context_0, gathered, params, own_hidden)
    with jax.named_scope("to_next_section"):
        tokens_1 = jnp.where(
            on_first, output, lax.ppermute(output, "section", [(0, 1)])
        )
    with jax.named_scope("gather_attend_weight"):
        own_pairs = attend_weight[0].reshape(64, 3, 8, 128).transpose(0, 2, 1, 3).reshape(64, 3072)
        other_pairs = lax.ppermute(own_pairs, "section", [(0, 1), (1, 0)])
        other_pairs, output = lax.optimization_barrier((other_pairs, output))
        other_attend = lax.all_gather(other_pairs, "shard", axis=0, tiled=True)
    context_1, kept_1 = attention(1, tokens_1.reshape(2, 64, 1024))
    own_tokens = jnp.where(on_first, tokens_0, tokens_1)
    own_context = jnp.where(on_first, context_0, context_1)
    with jax.named_scope("block_1"):
        output, saved = block_forward(own_tokens, own_context, gathered, params, own_hidden)
    layer_output = output.reshape(1, 2, 1, 64, 1024)
    with jax.named_scope("gather_first"):
        first_all = lax.all_gather(saved[1], "shard", axis=0, tiled=True)

    last_grad = cotangent.reshape(128, 1024)
    with jax.named_scope("block_back_1"):
        unused, grad_attn_1, grad_context, unused = block_back(
            last_grad, saved, gathered, params
        )
    with jax.named_scope("residual_to_other_section"):
        arrived_1 = lax.ppermute(grad_attn_1, "section", [(1, 0)])
    grad_packed_1, arrived_1 = attention_back(1, grad_context, kept_1, arrived_1)
    with jax.named_scope("grad_tokens_1"):
        rounded = grad_tokens(send_tokens(grad_packed_1, 3), other_attend, arrived_1)
        rounded_1 = rounded
    own_grad = jnp.where(on_first, rounded, last_grad)
    with jax.named_scope("gather_grad_mlp"):
        grad_mlp = normed_back(own_grad.astype(jnp.float32), saved[3], params[5:6])[0].astype(LOW)
        grad_mlp, own_grad = lax.optimization_barrier((grad_mlp, own_grad))
        grad_mlp_all = lax.all_gather(grad_mlp, "shard", axis=0, tiled=True)
    with jax.named_scope("block_back_0"):
        grad_residual, grad_attn, grad_context, norm_sums = block_back(
            own_grad, saved, gathered, params
        )
    late_tokens, late_packed, late_gathered, grad_context = lax.optimization_barrier(
        (kept_1[0], grad_packed_1, gathered, grad_context)
    )
    with jax.named_scope("swap_attend_grad"):
        part_1 = attend_part(late_tokens, late_packed)
        take_1 = lax.ppermute(part_1, "section", [(0, 1)])
    with jax.named_scope("sum_output_grad"):
        output_grad = transposed_times(saved[4], grad_attn)
        halves = [output_grad[:, :512], output_grad[:, 512:]]
        core = shard % 2
        keep = jnp.where(core == 0, halves[0], halves[1])
        give = jnp.where(core == 0, halves[1], halves[0]).astype(LOW)
        output_grad = (keep + swap_cores(give).astype(jnp.float32)).astype(LOW)
    grad_packed, output_grad = attention_back(0, grad_context, kept_0, output_grad)

    with jax.named_scope("sum_output_grad"):
        output_got = exchange(output_grad.reshape(64, 16, 512), REST)
        output_got, grad_packed = lax.optimization_barrier((output_got, grad_packed))
    with jax.named_scope("swap_attend_grad"):
        part_0 = attend_part(kept_0[0], grad_packed)
        take_0 = lax.ppermute(part_0, "section", [(1, 0)])
        lower = jnp.where(on_first, part_0, take_1)
        upper = jnp.where(on_first, take_0, part_1)
        attend_grad = jnp.concatenate([lower[:1024], upper[:1024]], 1)
        sums = jnp.stack([lower[1024], upper[1024]]).reshape(2, 3, HEAD_DIM)
        norm_rows = norm_sums[:5].reshape(5, 16, 64).transpose(1, 0, 2)
        mine = jnp.arange(8) == shard % 8
        head_rows = jnp.where(
            mine[None, :, None, None], sums[:, None, ::2].astype(jnp.float32), 0.0
        ).reshape(16, 2, 64)
        vectors = jnp.pad(
            jnp.concatenate([norm_rows, head_rows], 1), ((0, 0), (0, 9), (0, 64))
        )
        vectors = jnp.broadcast_to(vectors[:, None], (16, 4, 16, 128)).reshape(1024, 128)
        vectors = vectors.astype(LOW)
    with jax.named_scope("sum_attend_grad"):
        parts = jnp.concatenate([attend_grad, vectors], 1)
        parts, late_attn, late_rounded = lax.optimization_barrier((parts, grad_attn, rounded_1))
        got = exchange(parts.reshape(64, 16, 512), REST)
        arrived_0 = lax.ppermute(late_attn, "section", [(0, 1)])
        grad_tokens_1 = lax.ppermute(late_rounded, "section", [(0, 1)])
    with jax.named_scope("block_weight_grads"):
        expand_part = lax.dynamic_slice(
            late_gathered, (0, 320 + shard // 4 * 64, shard % 4 * 256), (16, 64, 256)
        ).reshape(1024, 256)
        hidden_part = lax.dynamic_slice_in_dim(own_hidden.reshape(4096), shard * 256, 256, 0)
        inner = matmul(first_all, expand_part) + hidden_part
        activation = inner * gelu_share(inner)
        grad_inner = times_transposed(grad_mlp_all, contract_weight[0]) * gelu_slope(inner)
        grad_inner = grad_inner.astype(LOW)
        expand_grad = transposed_times(first_all, grad_inner).astype(LOW)
        contract_grad = transposed_times(activation.astype(LOW), grad_mlp_all).astype(LOW)
        hidden_sum = jnp.sum(grad_inner.astype(jnp.float32), 0)
        mlp_sum = jnp.sum(grad_mlp_all.astype(jnp.float32), 0)
        extra = jnp.concatenate(
            [
                jnp.concatenate([hidden_sum, jnp.zeros((768,), jnp.float32)])[None],
                mlp_sum[None],
                jnp.zeros((14, 1024), jnp.float32),
            ],
            0,
        ).astype(LOW)
        rows = jnp.concatenate(
            [contract_grad.reshape(4, 64, 1024), jnp.broadcast_to(extra, (4, 16, 1024))], 1
        )
    with jax.named_scope("sum_expand_grad"):
        got, expand_grad, rows = lax.optimization_barrier((got, expand_grad, rows))
        expand_got = exchange(expand_grad.reshape(64, 16, 256), REST)
        expand_got, rows, arrived_0, grad_tokens_1 = lax.optimization_barrier(
            (expand_got, rows, arrived_0, grad_tokens_1)
        )
    with jax.named_scope("sum_contract"):
        got_contract = exchange(rows, "replica").astype(jnp.float32).sum(0)
    with jax.named_scope("sum_attend_grad"):
        got_output = output_got.astype(jnp.float32).reshape(8, 2, 4, 16, 512).sum((0, 2))
        got_output = jnp.concatenate([got_output[0], got_output[1]], 1).astype(LOW)
        got_attend = got[:, :, :384].astype(jnp.float32).reshape(2, 8, 4, 16, 384).sum((0, 2))
        got_expand = expand_got.astype(jnp.float32).reshape(16, 4, 16, 256).sum(1)
        got_expand = got_expand.astype(LOW).transpose(1, 0, 2).reshape(16, 4096)
        got_vectors = got[:, :7, 384:448].astype(jnp.float32).sum(0)
        got_attend, got_output = lax.optimization_barrier((got_attend.astype(LOW), got_output))
        got_attend = got_attend.reshape(8, 16, 2, 3, 64).transpose(1, 3, 2, 0, 4)
        got_attend = got_attend.reshape(16, 3072)
    with jax.named_scope("gather_weight_grads"):
        contract_rows = got_contract[:64].astype(LOW).reshape(4, 16, 1024)
        owned = jnp.concatenate([got_attend, got_output, got_expand, *contract_rows], 1)
    with jax.named_scope("grad_tokens_0"):
        late_packed, owned = lax.optimization_barrier((grad_packed, owned))
        rounded = grad_tokens(send_tokens(late_packed, 3), other_attend, arrived_0)
        grad_tokens_0 = lax.ppermute(rounded, "section", [(1, 0)])
    with jax.named_scope("gather_weight_grads"):
        totals = lax.all_gather(owned, "replica", axis=0, tiled=True)
        contract_total = totals[:, 8192:].reshape(4, 16, 4, 1024).transpose(0, 2, 1, 3)
        contract_total = contract_total.reshape(1, 256, 1024).astype(jnp.float32)
        totals = totals[None, :, :8192].astype(jnp.float32)
    attend_total = totals[:, :, :3072]
    output_total = totals[:, :, 3072:4096]
    expand_total = totals[:, :, 4096:]
    grad_tokens_0, attend_total, output_total, expand_total, contract_total = (
        lax.optimization_barrier(
            (grad_tokens_0, attend_total, output_total, expand_total, contract_total)
        )
    )
    input_grad = jnp.where(on_first, grad_tokens_0, grad_tokens_1).astype(jnp.float32)
    input_grad = input_grad.reshape(1, 2, 1, 64, 1024)
    mlp_own = lax.dynamic_slice_in_dim(got_contract[65], shard * 64, 64, 0)
    biases_grad = jnp.stack(
        [
            got_vectors[5],
            got_vectors[6],
            got_vectors[2],
            got_vectors[3],
            mlp_own,
            got_vectors[4],
        ]
    )
    return (
        layer_output,
        input_grad,
        attend_total,
        output_total,
        expand_total,
        contract_total,
        biases_grad[None],
        got_contract[None, 64, :256],
        got_vectors[None, :2],
    )


def solution(mesh):
    placed = (
        P(None, "replica", "shard", None),
        P(None, "replica", "shard"),
        P(None, "replica", "shard", None),
        P("section", "shard", None),
        P("section", "shard", None),
        P("section", "shard", None),
        P("section", "shard", None),
        P("section", None, "shard"),
        P("section", "shard"),
        P("section", None, "shard"),
    )
    return jax.shard_map(
        on_device,
        mesh=mesh,
        in_specs=placed,
        out_specs=(
            P("section", None, "replica", "shard", None),
            P("section", None, "replica", "shard", None),
            P("section", "shard", None),
            P("section", "shard", None),
            P("section", "shard", None),
            P("section", "shard", None),
            P("section", None, "shard"),
            P("section", "shard"),
            P("section", None, "shard"),
        ),
        check_vma=False,
    )
```
